32 devices in a mesh: fsdp: 8 (over z, y), rep: 4 (over x, core).
Axes of the slice: x: 2, y: 2, z: 4, core: 2. Of those that a mesh axis runs over, the one named last changes fastest.
Arguments:
- tokens: bfloat16 [8192, 2048], P(('fsdp', 'rep')), may hold values from -6 to 6
- lengths: int32 [32], P(('fsdp', 'rep')), may hold values from 1 to 256, 5120 in all
- mixer_gain: bfloat16 [2048], P('fsdp'), may hold values from 0.5 to 1.5
- in_proj: bfloat16 [2048, 6704], P('fsdp'), may hold values from -0.125 to 0.125
- conv_weight: bfloat16 [4, 3584], P(None, 'fsdp'), may hold values from -3 to 3
- conv_bias: bfloat16 [3584], P('fsdp'), may hold values from -3 to 3
- decay_log: float32 [48], replicated, may hold values from 0 to 2.8
- step_bias: float32 [48], replicated, may hold values from -5 to -1
- skip_gain: float32 [48], replicated, may hold values from 0.5 to 1.5
- query_weight: bfloat16 [2048, 1024], P('fsdp'), may hold values from -0.125 to 0.125
- key_weight: bfloat16 [2048, 256], P('fsdp'), may hold values from -0.125 to 0.125
- value_weight: bfloat16 [2048, 256], P('fsdp'), may hold values from -0.125 to 0.125
- mamba_out: bfloat16 [3072, 2048], P('fsdp'), may hold values from -0.109375 to 0.109375
- attn_out: bfloat16 [1024, 2048], P('fsdp'), may hold values from -1 to 1
- mlp_gain: bfloat16 [2048], P('fsdp'), may hold values from 0.5 to 1.5
- gate_weight: bfloat16 [2048, 4096], P('fsdp'), may hold values from -0.125 to 0.125
- up_weight: bfloat16 [2048, 4096], P('fsdp'), may hold values from -0.125 to 0.125
- down_weight: bfloat16 [4096, 2048], P('fsdp'), may hold values from -0.09375 to 0.09375
- cotangent: bfloat16 [8192, 2048], P(('fsdp', 'rep')), may hold values from -6 to 6
Outputs:
- output: bfloat16 [8192, 2048], P(('fsdp', 'rep'))
- grad_tokens: bfloat16 [8192, 2048], P(('fsdp', 'rep'))
- grad_mixer_gain: float32 [2048], P('fsdp')
- grad_in_proj: float32 [2048, 6704], P('fsdp')
- grad_conv_weight: float32 [4, 3584], P(None, 'fsdp')
- grad_conv_bias: float32 [3584], P('fsdp')
- grad_decay_log: float32 [48], replicated
- grad_step_bias: float32 [48], replicated
- grad_skip_gain: float32 [48], replicated
- grad_query: float32 [2048, 1024], P('fsdp')
- grad_key: float32 [2048, 256], P('fsdp')
- grad_value: float32 [2048, 256], P('fsdp')
- grad_mamba_out: float32 [3072, 2048], P('fsdp')
- grad_attn_out: float32 [1024, 2048], P('fsdp')
- grad_mlp_gain: float32 [2048], P('fsdp')
- grad_gate: float32 [2048, 4096], P('fsdp')
- grad_up: float32 [2048, 4096], P('fsdp')
- grad_down: float32 [4096, 2048], P('fsdp')
The draws below stay inside these ranges and needn't reach their ends.
Inputs may be any that keep to these rules, and one draw needn't show every extreme that they name: `lengths`: live length of each sequence; positions at or past it are padding. Some sequence is full in every draw.
All inputs are finite; a program needn't handle non-finite values. No bound on the sum of `lengths` on one device may be relied on, other than what follows from the above.
Results may differ from the reference program's by a relative error of at most 0.018.
Values may be sent and summed in bfloat16 or wider, within the bound.
A program may use at most 448 MiB of HBM per device.

```python
import math
import jax
import jax.numpy as jnp
import numpy as np
from jax import lax

D = 2048
HEADS = 48
HDIM = 64
STATE = 256
CONV = 4
QH = 8
KVH = 2
HEAD_WIDTH = 128
FF = 4096
LEN = 256
BLK = 128
INNER = 3072
CHANNELS = 3584
PROJ = 6704
SEQS = 32
TOKENS = 8192


def block_scale(rng, extent, split, low, largest):
    def one(dim, blocks):
        heights = jax.random.uniform(jax.random.fold_in(jax.random.fold_in(rng, 6), dim), (blocks,), jnp.float32, low / len(split), largest / len(split))
        return jnp.repeat(jnp.exp(heights), extent[dim] // blocks).reshape((-1,) + (1,) * (len(extent) - dim - 1))

    factor_of = one(*split[0])
    for cut in split[1:]:
        factor_of = factor_of * one(*cut)
    return factor_of


def profile(count, total, limit, skew):
    loads = [(1 << 20) // math.isqrt(standing ** skew) + 1 for standing in range(2, count + 1)]
    rest, holding = total - limit - (count - 1), [1] * (count - 1)
    while rest > 0:
        movable = [i for i in range(count - 1) if holding[i] < limit]
        pool, left = sum([loads[i] for i in movable]), rest
        for i in movable:
            more = min(limit - holding[i], max(1, left * loads[i] // pool), rest)
            holding[i] = holding[i] + more
            rest = rest - more
    return np.array([limit] + holding)


def uneven_parts(key, amount, total, reach, skew):
    if amount == 2:
        one = jax.random.randint(key, (), max(1, total - reach), min(reach, total - 1) + 1)
        return jnp.stack([one, total - one])
    tallies = jnp.asarray(profile(amount, total, reach, skew), jnp.int32)
    couples = (amount - 1) // 2
    giver, taker = tallies[1:1 + 2 * couples:2], tallies[2:2 + 2 * couples:2]
    room = jnp.minimum(giver - 1, reach - taker)
    shifted = jax.random.randint(jax.random.fold_in(key, 1), (couples,), 0, 1 << 20) % (room + 1)
    tallies = tallies.at[1:1 + 2 * couples:2].set(giver - shifted).at[2:2 + 2 * couples:2].set(taker + shifted)
    return tallies[jax.random.permutation(jax.random.fold_in(key, 2), amount)]


def normal_values(stream_key, shape, width, reach, split=(), dtype=jnp.bfloat16):
    drawn = width * jax.random.normal(stream_key, shape, jnp.float32)
    if split:
        drawn = drawn * block_scale(stream_key, shape, split, -0.22, 0.18)
    return jnp.clip(drawn, -reach, reach).astype(dtype)


def setup_inputs(seed: int = 0) -> dict:
    splits = jax.random.split(jax.random.key(seed), 20)
    tokens = normal_values(splits[0], (TOKENS, D), 1.0, 6.0, ((0, 32),))
    lengths = uneven_parts(splits[1], SEQS, SEQS * LEN * 5 // 8, LEN, 1).astype(jnp.int32)
    mixer_gain = jnp.clip(1.0 + 0.1 * jax.random.normal(splits[2], (D,), jnp.float32), 0.5, 1.5).astype(jnp.bfloat16)
    in_proj = normal_values(splits[3], (D, PROJ), D ** -0.5, 0.125, ((0, 8),))
    conv_weight = normal_values(splits[4], (CONV, CHANNELS), CONV ** -0.5, 3.0, ((1, 8),))
    conv_bias = normal_values(splits[5], (CHANNELS,), 0.5, 3.0, ((0, 8),))
    decay_log = jnp.clip(jax.random.uniform(splits[6], (HEADS,), jnp.float32, 0.0, 2.8), 0.0, 2.8)
    step_bias = jnp.clip(jax.random.uniform(splits[7], (HEADS,), jnp.float32, -5.0, -1.0), -5.0, -1.0)
    skip_gain = jnp.clip(jax.random.uniform(splits[8], (HEADS,), jnp.float32, 0.5, 1.5), 0.5, 1.5)
    query_weight = normal_values(splits[9], (D, QH * HEAD_WIDTH), D ** -0.5, 0.125, ((0, 8),))
    key_weight = normal_values(splits[10], (D, KVH * HEAD_WIDTH), D ** -0.5, 0.125, ((0, 8),))
    value_weight = normal_values(splits[11], (D, KVH * HEAD_WIDTH), D ** -0.5, 0.125, ((0, 8),))
    mamba_out = normal_values(splits[12], (INNER, D), INNER ** -0.5, 0.109375, ((0, 8),))
    attn_out = normal_values(splits[13], (QH * HEAD_WIDTH, D), (max(QH * HEAD_WIDTH * 8 // LEN, 1)) ** -0.5, 1.0, ((0, 8),))
    mlp_gain = jnp.clip(1.0 + 0.1 * jax.random.normal(splits[14], (D,), jnp.float32), 0.5, 1.5).astype(jnp.bfloat16)
    gate_weight = normal_values(splits[15], (D, FF), D ** -0.5, 0.125, ((0, 8),))
    up_weight = normal_values(splits[16], (D, FF), D ** -0.5, 0.125, ((0, 8),))
    down_weight = normal_values(splits[17], (FF, D), FF ** -0.5, 0.09375, ((0, 8),))
    cotangent = normal_values(splits[18], (TOKENS, D), 1.0, 6.0, ((0, 32),))
    return {"tokens": tokens, "lengths": lengths, "mixer_gain": mixer_gain, "in_proj": in_proj, "conv_weight": conv_weight, "conv_bias": conv_bias, "decay_log": decay_log, "step_bias": step_bias, "skip_gain": skip_gain, "query_weight": query_weight, "key_weight": key_weight, "value_weight": value_weight, "mamba_out": mamba_out, "attn_out": attn_out, "mlp_gain": mlp_gain, "gate_weight": gate_weight, "up_weight": up_weight, "down_weight": down_weight, "cotangent": cotangent}


epsilon = 1e-05

@jax.custom_vjp
def low(v):
    return lax.optimization_barrier(v.astype(jnp.bfloat16)).astype(jnp.float32)

@jax.custom_vjp
def low_back(v):
    return v

def low_keep(v):
    return (low(v), None)

def low_pass(kept, grad):
    return (grad,)

def back_keep(v):
    return (v, None)

def back_low(kept, grad):
    return (low(grad),)
low.defvjp(low_keep, low_pass)
low_back.defvjp(back_keep, back_low)

def highest(left, right):
    return jnp.dot(left, right, precision=lax.Precision.HIGHEST)

def rms_norm(values, gain):
    return values * lax.rsqrt(lax.optimization_barrier(jnp.mean(values * values, axis=-1, keepdims=True)) + epsilon) * gain

def rotate(values):
    length = values.shape[0]
    half_width = values.shape[-1] // 2
    position = jnp.arange(length).astype(jnp.float32)
    freqs = 10000.0 ** (-jnp.arange(half_width).astype(jnp.float32) * 2.0 / values.shape[-1])
    angles = position[:, None] * freqs[None, :]
    cosine = jnp.cos(angles)[:, None, :]
    sine_part = jnp.sin(angles)[:, None, :]
    first_half = values[..., :half_width]
    second_half = values[..., half_width:]
    return jnp.concatenate([first_half * cosine - second_half * sine_part, first_half * sine_part + second_half * cosine], axis=-1)

def attention_core(query_proj, key_proj, value_proj):
    length = query_proj.shape[0]
    group_size = QH // KVH
    query_rot = low(rotate(query_proj.reshape(length, QH, HEAD_WIDTH)))
    rotated_key = low(rotate(key_proj.reshape(length, KVH, HEAD_WIDTH)))
    value_reduced = low(value_proj.reshape(length, KVH, HEAD_WIDTH))
    block_rows = min(length, 512)
    block_count = length // block_rows
    query_split = query_rot.reshape(block_count, block_rows, KVH, group_size, HEAD_WIDTH)
    starts = (jnp.arange(block_count) * block_rows).astype(jnp.int32)

    def one_block(inputs):
        query_block_rows, start = inputs
        unscaled_value = jnp.einsum('aklh,pkh->klap', query_block_rows, rotated_key, precision=lax.Precision.HIGHEST) * HEAD_WIDTH ** (-0.5)
        scores = low_back(unscaled_value)
        index_of_row = start + jnp.arange(block_rows).astype(jnp.int32)
        col_index = jnp.arange(length).astype(jnp.int32)
        allowed = index_of_row[:, None] >= col_index[None, :]
        masked = jnp.where(allowed, scores, -1e+30)
        probability_reduced = low(jax.nn.softmax(masked, axis=-1))
        return jnp.einsum('kmou,ukf->okmf', probability_reduced, value_reduced, precision=lax.Precision.HIGHEST)
    result = lax.map(jax.checkpoint(one_block), (query_split, starts))
    return result.reshape(length, QH * HEAD_WIDTH)

def ssd_scan(ssm_input, step_size, decay, input_map, output_map):
    length = ssm_input.shape[0]
    block_count = length // BLK
    blocks = (ssm_input.reshape(block_count, BLK, HEADS, HDIM), step_size.reshape(block_count, BLK, HEADS), decay.reshape(block_count, BLK, HEADS), input_map.reshape(block_count, BLK, STATE), output_map.reshape(block_count, BLK, STATE))

    def one_block(ssm_state, inputs):
        block_input, block_step, block_decay, block_in_map, block_out_map = inputs
        running = jnp.cumsum(block_decay, axis=0)
        index_of_row = jnp.arange(BLK)
        lower_mask = (index_of_row[:, None] >= index_of_row[None, :])[:, :, None]
        decay_gap = running[:, None, :] - running[None, :, :]
        weight = jnp.where(lower_mask, jnp.exp(jnp.where(lower_mask, decay_gap, 0.0)), 0.0)
        pairing = jnp.dot(block_out_map, block_in_map.T, precision=lax.Precision.HIGHEST)
        mixing = pairing[:, :, None] * weight * block_step[None, :, :]
        local_part = jnp.einsum('tsh,shp->thp', mixing, block_input, precision=lax.Precision.HIGHEST)
        carried = jnp.einsum('tn,hpn->thp', block_out_map, ssm_state, precision=lax.Precision.HIGHEST) * jnp.exp(running)[:, :, None]
        total_decay = running[-1]
        tail_weight = jnp.exp(total_decay[None, :] - running) * block_step
        new_state = ssm_state * jnp.exp(total_decay)[:, None, None] + jnp.einsum('sh,shp,sn->hpn', tail_weight, block_input, block_in_map, precision=lax.Precision.HIGHEST)
        return (new_state, local_part + carried)
    initial = jnp.zeros((HEADS, HDIM, STATE), jnp.float32)
    final_state, result = lax.scan(jax.checkpoint(one_block), initial, blocks)
    return result.reshape(length, HEADS, HDIM)

def mixer_core(projected, query_proj, key_proj, value_proj, conv_weight, conv_bias, decay_log, step_bias, skip_gain):
    length = projected.shape[0]
    inner_width = HEADS * HDIM
    channel_count = inner_width + 2 * STATE
    gate_z = projected[:, :inner_width]
    conv_in = projected[:, inner_width:inner_width + channel_count]
    step_raw = projected[:, inner_width + channel_count:]
    padded = jnp.pad(conv_in, ((CONV - 1, 0), (0, 0)))
    conv_out = conv_bias[None, :] + jnp.zeros_like(conv_in)
    for offset in range(CONV):
        conv_out = conv_out + conv_weight[offset][None, :] * padded[offset:offset + length]
    conv_act = jax.nn.silu(conv_out)
    ssm_input = conv_act[:, :inner_width].reshape(length, HEADS, HDIM)
    input_map = conv_act[:, inner_width:inner_width + STATE]
    output_map = conv_act[:, inner_width + STATE:]
    step_size = jax.nn.softplus(step_raw + step_bias[None, :])
    decay = -step_size * jnp.exp(decay_log)[None, :]
    ssm_out = ssd_scan(ssm_input, step_size, decay, input_map, output_map) + skip_gain[None, :, None] * ssm_input
    mamba_mixed = low(ssm_out.reshape(length, inner_width) * jax.nn.silu(gate_z))
    attended = low(low_back(attention_core(query_proj, key_proj, value_proj)))
    return (mamba_mixed, attended)

def layer_one(params, seq_tokens, live_mask):
    mixer_gain, in_proj, conv_weight, conv_bias, decay_log, step_bias, skip_gain, query_weight, key_weight, value_weight, mamba_out, attn_out, mlp_gain, gate_weight, up_weight, down_weight = params
    normed = low(rms_norm(seq_tokens, mixer_gain))
    projected = low_back(highest(normed, in_proj))
    query_proj = low_back(highest(normed, query_weight))
    key_proj = low_back(highest(normed, key_weight))
    value_proj = low_back(highest(normed, value_weight))
    mamba_mixed, attended = mixer_core(projected, query_proj, key_proj, value_proj, conv_weight, conv_bias, decay_log, step_bias, skip_gain)
    mamba_branch = low_back(highest(mamba_mixed, mamba_out))
    attn_branch = low_back(highest(attended, attn_out))
    mixed_stream = seq_tokens + live_mask * (mamba_branch + attn_branch)
    normed_two = low(rms_norm(mixed_stream, mlp_gain))
    gate_value = low_back(highest(normed_two, gate_weight))
    up_value = low_back(highest(normed_two, up_weight))
    activated = low(jax.nn.silu(gate_value) * up_value)
    ffn_branch = low_back(highest(activated, down_weight))
    return mixed_stream + live_mask * ffn_branch

def reference(tokens, lengths, mixer_gain, in_proj, conv_weight, conv_bias, decay_log, step_bias, skip_gain, query_weight, key_weight, value_weight, mamba_out, attn_out, mlp_gain, gate_weight, up_weight, down_weight, cotangent):
    weights = tuple((member.astype(jnp.float32) for member in (mixer_gain, in_proj, conv_weight, conv_bias, decay_log, step_bias, skip_gain, query_weight, key_weight, value_weight, mamba_out, attn_out, mlp_gain, gate_weight, up_weight, down_weight)))
    seq_tokens = tokens.astype(jnp.float32).reshape(SEQS, LEN, D)
    live_mask = (jnp.arange(LEN).astype(jnp.int32)[None, :] < lengths.astype(jnp.int32)[:, None]).astype(jnp.float32)[:, :, None]

    def forward(inputs, params):

        def one_seq(carry, pair):
            return (carry, layer_one(params, pair[0], pair[1]))
        final_carry, result = lax.scan(jax.checkpoint(one_seq), jnp.zeros((), jnp.float32), (inputs, live_mask))
        return result
    result, pullback = jax.vjp(forward, seq_tokens, weights)
    grad_inputs, grad_weights = pullback(cotangent.astype(jnp.float32).reshape(SEQS, LEN, D))
    grad_mixer_gain, grad_in_proj, grad_conv_weight, grad_conv_bias, grad_decay_log, grad_step_bias, grad_skip_gain, grad_query, grad_key, grad_value, grad_mamba_out, grad_attn_out, grad_mlp_gain, grad_gate, grad_up, grad_down = grad_weights
    return (result.reshape(TOKENS, D).astype(jnp.bfloat16), grad_inputs.reshape(TOKENS, D).astype(jnp.bfloat16), grad_mixer_gain, grad_in_proj, grad_conv_weight, grad_conv_bias, grad_decay_log, grad_step_bias, grad_skip_gain, grad_query, grad_key, grad_value, grad_mamba_out, grad_attn_out, grad_mlp_gain, grad_gate, grad_up, grad_down)
```

```python
import functools

import jax
import jax.numpy as jnp
from jax import lax
from jax.experimental import pallas as pl
from jax.experimental.pallas import tpu as pltpu
from jax.sharding import PartitionSpec as P

HEADS = 48
HDIM = 64
STATE = 256
CONV = 4
QH = 8
KVH = 2
HEAD_WIDTH = 128
INNER = HEADS * HDIM
LANES = 128
ROWS = 128
MIB = 1 << 20
MESH = pl.DeviceIdType.MESH

epsilon = 1e-05
BF16 = jnp.bfloat16
F32 = jnp.float32
HIGHEST = lax.Precision.HIGHEST


def dot(left, right, contract=((1,), (0,)), precision=None):
    return lax.dot_general(
        left, right, (contract, ((), ())), preferred_element_type=F32, precision=precision
    )


def dot_tn(left, right, precision=None):
    return dot(left, right, ((0,), (0,)), precision)


def dot_nt(left, right, precision=None):
    return dot(left, right, ((1,), (1,)), precision)


def sigmoid(v):
    return 1.0 / (1.0 + jnp.exp(-v))


def silu_slope(v, sig):
    return sig * (1.0 + v * (1.0 - sig))


def softplus(v):
    return jnp.maximum(v, 0.0) + jnp.log1p(jnp.exp(-jnp.abs(v)))


def shift_down(v, by):
    if by == 0:
        return v
    return jnp.concatenate([jnp.zeros((by, v.shape[1]), v.dtype), v[:-by]], axis=0)


def shift_up(v, by):
    if by == 0:
        return v
    return jnp.concatenate([v[by:], jnp.zeros((by, v.shape[1]), v.dtype)], axis=0)


class Cut:
    def __init__(self, reps):
        self.heads = HEADS // reps
        self.inner = INNER // reps
        self.qheads = QH // reps
        self.qwidth = self.qheads * HEAD_WIDTH
        self.q = 0
        self.step = self.qwidth
        self.z = self.step + LANES
        self.x = self.z + self.inner
        self.maps = self.x + self.inner
        self.k = self.maps + 2 * STATE
        self.v = self.k + HEAD_WIDTH
        self.width = self.v + HEAD_WIDTH
        self.conv = self.inner + 2 * STATE
        self.shared = (self.width - self.maps) // 2
        self.way = (self.maps + self.shared) // 2

    def ring_row(self, column):
        half = self.maps // 2
        return column if column < half else column - half + self.way


def conv_out_of(ref, lanes, start, conv_ref):
    width = lanes.stop - lanes.start
    given = ref[:, start : start + width].astype(F32)
    total = conv_ref[CONV : CONV + 1, lanes]
    for tap in range(CONV):
        total = total + conv_ref[tap : tap + 1, lanes] * shift_down(given, CONV - 1 - tap)
    return total, given


def conv_back(d_out, given, conv_ref, lanes, sums_ref):
    d_given = jnp.zeros_like(d_out)
    for tap in range(CONV):
        back = CONV - 1 - tap
        d_given = d_given + conv_ref[tap : tap + 1, lanes] * shift_up(d_out, back)
        sums_ref[tap : tap + 1, lanes] += jnp.sum(
            d_out * shift_down(given, back), axis=0, keepdims=True
        )
    sums_ref[CONV : CONV + 1, lanes] += jnp.sum(d_out, axis=0, keepdims=True)
    return d_given


def ones_triangle(length, upper):
    row = lax.broadcasted_iota(jnp.int32, (length, length), 0)
    col = lax.broadcasted_iota(jnp.int32, (length, length), 1)
    return jnp.where(col >= row if upper else col <= row, 1.0, 0.0).astype(F32)


def steps_of(step_ref, head_ref):
    raw = step_ref[...] + head_ref[1:2, :]
    step = softplus(raw)
    decay = -step * jnp.exp(head_ref[0:1, :])
    running = dot(ones_triangle(raw.shape[0], False), decay, precision=HIGHEST)
    return raw, step, decay, running


def decay_block(running, running_t, head, block):
    top, width = block * ROWS, (block + 1) * ROWS
    gap = running[top:width, head : head + 1] - running_t[head : head + 1, :width]
    row = lax.broadcasted_iota(jnp.int32, (ROWS, width), 0) + top
    col = lax.broadcasted_iota(jnp.int32, (ROWS, width), 1)
    return jnp.where(row >= col, jnp.exp(gap), 0.0)


def turn(v, cos_ref, sin_ref):
    half = HEAD_WIDTH // 2
    return v * cos_ref[...] + pltpu.roll(v, half, 1) * sin_ref[...]


def turn_back(v, cos_ref, sin_ref):
    half = HEAD_WIDTH // 2
    return v * cos_ref[...] - pltpu.roll(v, half, 1) * sin_ref[...]


def softmax_rows(q, k):
    scores = dot_nt(q, k) * HEAD_WIDTH ** (-0.5)
    row = lax.broadcasted_iota(jnp.int32, scores.shape, 0)
    col = lax.broadcasted_iota(jnp.int32, scores.shape, 1)
    scores = jnp.where(row >= col, scores, -1e30)
    top = jnp.max(scores, axis=1, keepdims=True)
    weight = jnp.exp(scores - top)
    return weight / jnp.sum(weight, axis=1, keepdims=True)


def mixer_forward(
    cut, proj_ref, step_ref, conv_ref, head_ref, chan_ref, cos_ref, sin_ref, out_ref, act_ref
):
    length = proj_ref.shape[0]
    for lane in range(0, cut.conv, 2 * LANES):
        lanes = slice(lane, min(lane + 2 * LANES, cut.conv))
        total, _ = conv_out_of(proj_ref, lanes, cut.x + lane, conv_ref)
        act_ref[:, lanes] = total * sigmoid(total)
    _, step, _, running = steps_of(step_ref, head_ref)
    step_t, running_t = step.T, running.T
    in_map = act_ref[:, cut.inner : cut.inner + STATE].astype(BF16)
    out_map = act_ref[:, cut.inner + STATE : cut.inner + 2 * STATE].astype(BF16)
    pairing = dot_nt(out_map, in_map)
    first = lax.broadcasted_iota(jnp.int32, (ROWS, LANES), 1) < HDIM
    for pair in range(cut.heads // 2):
        lanes = slice(pair * LANES, (pair + 1) * LANES)
        given = act_ref[:, lanes].astype(BF16)
        for block in range(length // ROWS):
            rows = slice(block * ROWS, (block + 1) * ROWS)
            parts = []
            for head in (2 * pair, 2 * pair + 1):
                mixing = (
                    pairing[rows, : rows.stop]
                    * decay_block(running, running_t, head, block)
                    * step_t[head : head + 1, : rows.stop]
                )
                parts.append(dot(mixing.astype(BF16), given[: rows.stop]))
            ssm = jnp.where(first, parts[0], parts[1])
            ssm = ssm + chan_ref[0:1, lanes] * act_ref[rows, lanes]
            gate = proj_ref[rows, cut.z + lanes.start : cut.z + lanes.stop].astype(F32)
            out_ref[rows, lanes] = (ssm * gate * sigmoid(gate)).astype(BF16)
    key = turn(proj_ref[:, cut.k : cut.k + HEAD_WIDTH].astype(F32), cos_ref, sin_ref).astype(BF16)
    value = proj_ref[:, cut.v : cut.v + HEAD_WIDTH].astype(BF16)
    for head in range(cut.qheads):
        at = cut.q + head * HEAD_WIDTH
        query = turn(proj_ref[:, at : at + HEAD_WIDTH].astype(F32), cos_ref, sin_ref).astype(BF16)
        probs = softmax_rows(query, key).astype(BF16)
        to = cut.inner + head * HEAD_WIDTH
        out_ref[:, to : to + HEAD_WIDTH] = dot(probs, value).astype(BF16)


def mixer_backward(
    cut,
    proj_ref,
    step_ref,
    grad_ref,
    conv_ref,
    head_ref,
    chan_ref,
    cos_ref,
    sin_ref,
    d_ref,
    conv_sum_ref,
    head_sum_ref,
    chan_sum_ref,
    act_ref,
    d_act_ref,
    d_pair_ref,
    col_ref,
):
    length = proj_ref.shape[0]

    for lane in range(0, cut.conv, 2 * LANES):
        lanes = slice(lane, min(lane + 2 * LANES, cut.conv))
        total, _ = conv_out_of(proj_ref, lanes, cut.x + lane, conv_ref)
        act_ref[:, lanes] = total * sigmoid(total)
    raw, step, decay, running = steps_of(step_ref, head_ref)
    step_t, running_t = step.T, running.T
    in_map = act_ref[:, cut.inner : cut.inner + STATE].astype(BF16)
    out_map = act_ref[:, cut.inner + STATE : cut.inner + 2 * STATE].astype(BF16)
    pairing = dot_nt(out_map, in_map)
    d_pair_ref[...] = jnp.zeros_like(d_pair_ref)
    col_ref[...] = jnp.zeros_like(col_ref)
    first = lax.broadcasted_iota(jnp.int32, (ROWS, LANES), 1) < HDIM
    lane_of = lax.broadcasted_iota(jnp.int32, (ROWS, LANES), 1)
    row_sums = [jnp.zeros((ROWS, LANES), F32) for _ in range(length // ROWS)]
    for pair in range(cut.heads // 2):
        lanes = slice(pair * LANES, (pair + 1) * LANES)
        given_f = act_ref[:, lanes]
        given = given_f.astype(BF16)
        skip = chan_ref[0:1, lanes]
        skip_sum = jnp.zeros((1, LANES), F32)
        for block in range(length // ROWS):
            rows = slice(block * ROWS, (block + 1) * ROWS)
            width = rows.stop
            z_lanes = slice(cut.z + lanes.start, cut.z + lanes.stop)
            gate = proj_ref[rows, z_lanes].astype(F32)
            sig = sigmoid(gate)
            d_mixed = grad_ref[rows, lanes].astype(F32)
            d_ssm = d_mixed * gate * sig
            skip_sum = skip_sum + jnp.sum(d_ssm * given_f[rows], axis=0, keepdims=True)
            parts = []
            d_given = jnp.zeros((width, LANES), F32)
            for which in range(2):
                head = 2 * pair + which
                d_head = jnp.where(first if which == 0 else ~first, d_ssm, 0.0).astype(BF16)
                fall = decay_block(running, running_t, head, block)
                step_row = step_t[head : head + 1, :width]
                d_mixing = dot_nt(d_head, given[:width])
                stepped = fall * step_row
                mixing = pairing[rows, :width] * stepped
                mixing_low = mixing.astype(BF16)
                parts.append(dot(mixing_low, given[:width]))
                d_given = d_given + dot_tn(mixing_low, d_head)
                d_pair_ref[rows, :width] += d_mixing * stepped
                flow = d_mixing * mixing
                row_sums[block] = jnp.where(
                    lane_of == head,
                    jnp.sum(flow, axis=1, keepdims=True),
                    row_sums[block],
                )
                col_ref[head : head + 1, :width] += jnp.sum(
                    d_mixing * pairing[rows, :width] * fall, axis=0, keepdims=True
                )
            if block == 0:
                d_act_ref[:, lanes] = jnp.zeros((length, LANES), F32)
            d_act_ref[:width, lanes] += d_given
            d_act_ref[rows, lanes] += d_ssm * skip
            ssm = jnp.where(first, parts[0], parts[1]) + skip * given_f[rows]
            d_ref[rows, z_lanes] = (d_mixed * ssm * silu_slope(gate, sig)).astype(BF16)
        chan_sum_ref[0:1, lanes] += skip_sum
    d_pair = d_pair_ref[...].astype(BF16)
    d_act_ref[:, cut.inner : cut.inner + STATE] = dot_tn(d_pair, out_map)
    d_act_ref[:, cut.inner + STATE : cut.inner + 2 * STATE] = dot(d_pair, in_map)
    col_sum = col_ref[...].T
    d_running = jnp.concatenate(row_sums, axis=0) - step * col_sum
    d_decay = dot(ones_triangle(length, True), d_running, precision=HIGHEST)
    d_step = col_sum - d_decay * jnp.exp(head_ref[0:1, :])
    d_raw = d_step * sigmoid(raw)
    valid = lax.broadcasted_iota(jnp.int32, d_raw.shape, 1) < cut.heads
    d_raw = jnp.where(valid, d_raw, 0.0)
    d_ref[:, cut.step : cut.step + LANES] = d_raw.astype(BF16)
    head_sum_ref[0:1, :] += jnp.sum(d_decay * decay, axis=0, keepdims=True)
    head_sum_ref[1:2, :] += jnp.sum(d_raw, axis=0, keepdims=True)
    for lane in range(0, cut.conv, 2 * LANES):
        lanes = slice(lane, min(lane + 2 * LANES, cut.conv))
        total, given = conv_out_of(proj_ref, lanes, cut.x + lane, conv_ref)
        d_out = d_act_ref[:, lanes] * silu_slope(total, sigmoid(total))
        d_given = conv_back(d_out, given, conv_ref, lanes, conv_sum_ref)
        d_ref[:, cut.x + lane : cut.x + lanes.stop] = d_given.astype(BF16)
    key = turn(proj_ref[:, cut.k : cut.k + HEAD_WIDTH].astype(F32), cos_ref, sin_ref).astype(BF16)
    value = proj_ref[:, cut.v : cut.v + HEAD_WIDTH].astype(BF16)
    d_key = jnp.zeros((length, HEAD_WIDTH), F32)
    d_value = jnp.zeros((length, HEAD_WIDTH), F32)
    for head in range(cut.qheads):
        at = cut.q + head * HEAD_WIDTH
        query = turn(proj_ref[:, at : at + HEAD_WIDTH].astype(F32), cos_ref, sin_ref).astype(BF16)
        probs = softmax_rows(query, key)
        to = cut.inner + head * HEAD_WIDTH
        d_attended = grad_ref[:, to : to + HEAD_WIDTH].astype(BF16)
        d_probs = dot_nt(d_attended, value)
        inner = jnp.sum(probs * d_probs, axis=1, keepdims=True)
        d_scores = (probs * (d_probs - inner)).astype(BF16)
        d_query = dot(d_scores, key) * HEAD_WIDTH ** (-0.5)
        d_key = d_key + dot_tn(d_scores, query) * HEAD_WIDTH ** (-0.5)
        d_value = d_value + dot_tn(probs.astype(BF16), d_attended)
        d_ref[:, at : at + HEAD_WIDTH] = turn_back(d_query, cos_ref, sin_ref).astype(BF16)
    d_ref[:, cut.k : cut.k + HEAD_WIDTH] = turn_back(d_key, cos_ref, sin_ref).astype(BF16)
    d_ref[:, cut.v : cut.v + HEAD_WIDTH] = d_value.astype(BF16)


def spread(moves, places_ref, blocks_ref, *refs):
    for which in range(4):
        at = places_ref[which]
        for out, rows, lanes, row_by, lane_by, lane_from in moves:
            height, width = rows.stop - rows.start, lanes.stop - lanes.start
            row, lane = at * row_by, lane_from + at * lane_by
            if row_by:
                row = pl.multiple_of(row, row_by)
            if lane_by and lane_by % LANES == 0:
                lane = pl.multiple_of(lane, LANES)
            refs[out][pl.ds(row, height), pl.ds(lane, width)] = blocks_ref[
                which, rows, lanes
            ].astype(F32)


def spread_call(places, blocks, outs, moves):
    if any(move[4] % LANES for move in moves):
        return spread_plain(places, blocks, outs, moves)
    return pl.pallas_call(
        functools.partial(spread, moves),
        out_shape=[jax.ShapeDtypeStruct(shape, F32) for shape in outs],
        in_specs=[pl.BlockSpec(memory_space=pltpu.SMEM)]
        + [pl.BlockSpec(memory_space=pltpu.VMEM)],
        out_specs=[pl.BlockSpec(memory_space=pltpu.VMEM)] * len(outs),
        compiler_params=pltpu.CompilerParams(vmem_limit_bytes=40 * MIB),
        name="spread",
    )(places, blocks)


def spread_plain(places, blocks, outs, moves):
    result = [jnp.zeros(shape, F32) for shape in outs]
    for which in range(4):
        block, at = blocks[which], places[which]
        for out, rows, lanes, row_by, lane_by, lane_from in moves:
            result[out] = lax.dynamic_update_slice(
                result[out],
                block[rows, lanes].astype(F32),
                (at * row_by, lane_from + at * lane_by),
            )
    return result


def spread_in(cut, places_ref, *refs):
    blocks_ref, wide_ref, query_ref, key_ref, value_ref = refs
    key_ref[...] = jnp.zeros_like(key_ref)
    value_ref[...] = jnp.zeros_like(value_ref)
    split = cut.maps // 2
    first = split - cut.z
    maps = 2 * INNER
    for which in range(4):
        block = blocks_ref.at[which]
        at = places_ref[which]
        lanes = pl.ds(pl.multiple_of(at * cut.qwidth, LANES), cut.qwidth)
        query_ref[:, lanes] = block[: cut.qwidth].astype(F32).T
        to = pl.multiple_of(at * cut.inner, ROWS)
        wide_ref[pl.ds(to, first)] = block[cut.z : split].astype(F32)
        wide_ref[pl.ds(pl.multiple_of(to + first, 64), cut.inner - first)] = block[
            cut.way : cut.way + cut.inner - first
        ].astype(F32)
        wide_ref[pl.ds(INNER + to, cut.inner)] = block[
            cut.way + cut.inner - first : cut.way + split
        ].astype(F32)
    halves = [
        jnp.concatenate(
            [
                blocks_ref[which, split : cut.way].astype(F32),
                blocks_ref[which, cut.way + split :].astype(F32),
            ],
            axis=0,
        )
        for which in range(4)
    ]
    ones = [places_ref[which] % 2 for which in range(4)]
    low_half = sum(jnp.where(one == 0, half, 0.0) for one, half in zip(ones, halves))
    wide_ref[maps : maps + cut.shared] = low_half
    rest = 2 * STATE - cut.shared
    high = [jnp.where(one == 1, half, 0.0) for one, half in zip(ones, halves)]
    wide_ref[maps + cut.shared : maps + 2 * STATE] = sum(half[:rest] for half in high)
    for which, half in enumerate(high):
        lanes = pl.ds(
            pl.multiple_of(places_ref[which] * KVH // 4 * HEAD_WIDTH, LANES), HEAD_WIDTH
        )
        key_ref[:, lanes] += half[rest : rest + HEAD_WIDTH].T
        value_ref[:, lanes] += half[rest + HEAD_WIDTH :].T
    for rep in range(4):
        steps = sum(
            jnp.where(places_ref[which] == rep, 1.0, 0.0)
            * blocks_ref[which, cut.step : cut.step + LANES].astype(F32)
            for which in range(4)
        )
        to = maps + 2 * STATE + rep * cut.heads
        wide_ref[to : to + cut.heads] = steps[: cut.heads]


def spread_in_call(cut, places, blocks):
    depth = blocks.shape[2]
    vmem = pl.BlockSpec(memory_space=pltpu.VMEM)
    columns_in = 2 * INNER + 2 * STATE + HEADS
    return pl.pallas_call(
        functools.partial(spread_in, cut),
        out_shape=[
            jax.ShapeDtypeStruct((columns_in, depth), F32),
            jax.ShapeDtypeStruct((depth, QH * HEAD_WIDTH), F32),
            jax.ShapeDtypeStruct((depth, KVH * HEAD_WIDTH), F32),
            jax.ShapeDtypeStruct((depth, KVH * HEAD_WIDTH), F32),
        ],
        in_specs=[pl.BlockSpec(memory_space=pltpu.SMEM), vmem],
        out_specs=[vmem] * 4,
        compiler_params=pltpu.CompilerParams(vmem_limit_bytes=40 * MIB),
        name="spread_in",
    )(places, blocks)


def turn_tables(length):
    half = HEAD_WIDTH // 2
    position = jnp.arange(length).astype(F32)
    freqs = 10000.0 ** (-jnp.arange(half).astype(F32) * 2.0 / HEAD_WIDTH)
    angles = position[:, None] * freqs[None, :]
    cosine, sine = jnp.cos(angles), jnp.sin(angles)
    return (
        jnp.concatenate([cosine, cosine], axis=1),
        jnp.concatenate([-sine, sine], axis=1),
    )


class Ring:
    def __init__(self, shards):
        self.shards = shards
        self.index = lax.axis_index("fsdp")
        self.place = ring_place(self.index, shards)

    def at(self, offset):
        return ring_at(self.place + offset, self.shards)

    def peer(self, way):
        return {"fsdp": self.at(1 - 2 * way)}


class Pair:
    def __init__(self):
        self.rep = lax.axis_index("rep")
        across, core = self.rep // 2, self.rep % 2
        self.peers = ({"rep": (1 - across) * 2 + core}, {"rep": across * 2 + 1 - core})
        self.corner = {"rep": (1 - across) * 2 + 1 - core}


def greet(ring, pair, *more, maybe=(), are=None):
    barrier = pltpu.get_barrier_semaphore()

    def signal(peers):
        for peer in peers:
            pl.semaphore_signal(barrier, inc=1, device_id=peer, device_id_type=MESH)

    peers = (ring.peer(0), ring.peer(1)) + pair.peers + more
    signal(peers)
    if not maybe:
        pl.semaphore_wait(barrier, len(peers))
        return
    pl.when(are == 1)(lambda: signal(maybe))
    pl.semaphore_wait(barrier, len(peers) + len(maybe) * are)


class Gather:
    def __init__(self, ring, ways, send, recv, hook=None):
        self.ring, self.ways, self.send, self.recv = ring, ways, send, recv
        self.hook = hook or (lambda step, way, piece: None)

    def pieces(self):
        for piece in range(max(len(way) for way in self.ways)):
            for way in range(2):
                if piece < len(self.ways[way]):
                    yield way, piece

    def copy(self, step, way, piece, first=False):
        own, place = self.ways[way][piece]
        there = place(self.ring.at((2 * way - 1) * (step - 1)))
        return pltpu.make_async_remote_copy(
            src_ref=own if first else there,
            dst_ref=there,
            send_sem=self.send.at[step - 1, way, piece],
            recv_sem=self.recv.at[step - 1, way, piece],
            device_id=self.ring.peer(way),
            device_id_type=MESH,
        )

    def landed(self, step, way, piece):
        here = self.ways[way][piece][1](self.ring.at((2 * way - 1) * step))
        return pltpu.make_async_remote_copy(
            src_ref=here,
            dst_ref=here,
            send_sem=self.send.at[step - 1, way, piece],
            recv_sem=self.recv.at[step - 1, way, piece],
            device_id=self.ring.peer(way),
            device_id_type=MESH,
        )

    def start(self):
        for way, piece in self.pieces():
            self.copy(1, way, piece, True).start()

    def advance(self, step):
        for way, piece in self.pieces():
            self.landed(step - 1, way, piece).wait_recv()
            self.copy(step, way, piece).start()
            self.hook(step - 1, way, piece)

    def run(self, first, stop):
        def body(step, carry):
            self.advance(step)
            return carry

        lax.fori_loop(first, stop, body, 0)

    def finish(self):
        for way, piece in self.pieces():
            self.landed(self.ring.shards - 1, way, piece).wait_recv()
            self.hook(self.ring.shards - 1, way, piece)
            self.copy(1, way, piece, True).wait_send()

        def body(step, carry):
            for way, piece in self.pieces():
                self.copy(step, way, piece).wait_send()
            return carry

        lax.fori_loop(2, self.ring.shards, body, 0)


def ring_sems(shards, pieces):
    return [pltpu.SemaphoreType.DMA((shards - 1, 2, pieces))] * 2


def remote(src, dst, send, recv, peer):
    return pltpu.make_async_remote_copy(
        src_ref=src, dst_ref=dst, send_sem=send, recv_sem=recv, device_id=peer, device_id_type=MESH
    )


def block_at(ref, index, rows, lanes):
    if len(ref.shape) == 2:
        return ref.at[rows, pl.ds(pl.multiple_of(index * lanes, LANES), lanes)]
    return ref.at[index, rows]


def gather_in(shards, cut, inside, *refs):
    refs = list(refs)
    take = lambda number: [refs.pop(0) for _ in range(number)]
    in_ref, query_ref, key_ref, value_ref, aux_ref, tokens_ref, cot_ref, live_ref = take(8)
    w_ref, aux_all_ref, branch_all_ref = take(3)
    if inside:
        normed_ref, proj_ref, steps_ref = take(3)
    else:
        (tokens_all_ref,) = take(1)
    share_ref, turn_ref, rows_ref, branch_ref = take(4)
    pack_sem, send, recv, core_send, core_recv = take(5)
    token_sems, branch_sems = take(3), take(3)
    if inside:
        sum_ref, scale_ref, w_sem, w_out_ref = take(4)
        w_ref, w_out_ref = w_out_ref, w_ref
        tokens_all_ref = take(1)[0]

    ring, pair = Ring(shards), Pair()
    rep, core = pair.rep, pair.rep % 2
    depth = in_ref.shape[1]
    copies = (
        (
            in_ref.at[pl.ds(pl.multiple_of(cut.inner * rep, ROWS), cut.inner)],
            share_ref.at[pl.ds(cut.z, cut.inner)],
        ),
        (
            in_ref.at[pl.ds(pl.multiple_of(INNER + cut.inner * rep, ROWS), cut.inner)],
            share_ref.at[pl.ds(cut.x, cut.inner)],
        ),
        (
            in_ref.at[pl.ds(2 * INNER, 2 * STATE)],
            share_ref.at[pl.ds(cut.maps, 2 * STATE)],
        ),
        (in_ref.at[pl.ds(2 * INNER + 2 * STATE, HEADS)], rows_ref),
        (
            query_ref.at[:, pl.ds(pl.multiple_of(cut.qwidth * rep, LANES), cut.qwidth)],
            turn_ref.at[:, pl.ds(0, cut.qwidth)],
        ),
    ) + tuple(
        (
            ref.at[:, pl.ds(pl.multiple_of(rep * KVH // 4 * HEAD_WIDTH, LANES), HEAD_WIDTH)],
            turn_ref.at[:, pl.ds(cut.qwidth + number * HEAD_WIDTH, HEAD_WIDTH)],
        )
        for number, ref in enumerate((key_ref, value_ref))
    )
    packs = [
        pltpu.make_async_copy(src, dst, pack_sem.at[number])
        for number, (src, dst) in enumerate(copies)
    ]
    for pack in packs:
        pack.start()
    greet(ring, pair)
    branch_ref[...] = (cot_ref[...].astype(F32) * live_ref[:, 0:1]).astype(BF16)
    for pack in packs:
        pack.wait()
    share_ref[: cut.qwidth] = turn_ref[:, : cut.qwidth].T
    share_ref[cut.k :] = turn_ref[:, cut.qwidth :].T
    row = lax.broadcasted_iota(jnp.int32, (LANES, HEADS), 0)
    column = lax.broadcasted_iota(jnp.int32, (LANES, HEADS), 1)
    chosen = jnp.logical_and(column == row + cut.heads * rep, row < cut.heads)
    chosen = jnp.where(chosen, 1.0, 0.0).astype(BF16)
    share_ref[cut.step : cut.z] = dot(chosen, rows_ref[...]).astype(BF16)
    every = pl.ds(0, cut.width)
    keeps = [
        pltpu.make_async_copy(src, dst, pack_sem.at[len(packs) + number])
        for number, (src, dst) in enumerate(
            (
                (share_ref, block_at(w_ref, ring.index, every, depth)),
                (aux_ref, aux_all_ref.at[ring.index]),
            )
        )
    ]
    quarter = cut.maps // 4
    half = cut.shared // 2
    rows = lambda number: pl.ds(number * quarter, quarter)

    def shared(which, way):
        return pl.ds(pl.multiple_of(cut.maps + which * cut.shared + way * half, 16), half)

    def piece(rows):
        return share_ref.at[rows], lambda index: block_at(w_ref, index, rows, depth)

    ways = (
        [
            piece(rows(0)),
            piece(rows(1)),
            piece(shared(core, 0)),
            (aux_ref, lambda index: aux_all_ref.at[index]),
        ],
        [piece(rows(2)), piece(rows(3)), piece(shared(core, 1))],
    )

    def over_core(step, way, which):
        here = block_at(w_ref, ring.at((2 * way - 1) * step), shared(which, way), depth)
        return remote(
            here, here, core_send.at[step - 1, way], core_recv.at[step - 1, way], pair.peers[1]
        )

    def hook(step, way, piece):
        if piece == 2:
            over_core(step, way, core).start()

    gather = Gather(ring, ways, send, recv, hook)
    gather.start()
    tokens = Share(pair, 1, tokens_ref, tokens_all_ref, token_sems)
    branch = Share(pair, 1, branch_ref, branch_all_ref, branch_sems)
    tokens.start(0)
    branch.start(0)
    for keep in keeps:
        keep.start()
    gather.run(2, 4)
    tokens.pass_on(0)
    gather.advance(4)
    branch.pass_on(0)
    gather.advance(5)
    tokens.finish()
    for keep in keeps:
        keep.wait()
    if inside:
        length = tokens_ref.shape[0]
        chunk = cut.width // 7

        def scale(number, carry):
            values = tokens_all_ref[number].astype(F32)
            rows = pl.ds(pl.multiple_of(number * length, length), length)
            scale_ref[rows] = jnp.broadcast_to(norm_scale(values), (length, LANES))
            return carry

        lax.fori_loop(0, 4, scale, 0)

    def add(offset, fresh=False, last=False):
        index = ring.at(offset)
        if not fresh:
            over_core(offset, 1, 1 - core).wait_recv()
            over_core(shards - offset, 0, 1 - core).wait_recv()
        lanes = pl.ds(pl.multiple_of(index * depth, LANES), depth)
        gain = aux_all_ref[index, 0:1, :].astype(F32)

        def body(number, carry):
            rows = pl.ds(pl.multiple_of(number * length, length), length)
            left = tokens_all_ref[number, :, lanes].astype(F32) * scale_ref[rows, 0:1] * gain
            left = left.astype(BF16)
            normed_ref[rows, lanes] = left
            for at in range(0, cut.width, chunk):
                out = slice(at, at + chunk)
                total = dot_nt(left, w_ref[out, lanes])
                if not fresh:
                    total = sum_ref[rows, out] + total
                if not last:
                    sum_ref[rows, out] = total
                    continue
                proj_ref[rows, out] = total.astype(BF16)
                if at <= cut.step < at + chunk:
                    steps_ref[rows] = total[:, cut.step - at : cut.step - at + LANES]
            return carry

        lax.fori_loop(0, 4, body, 0)
        store(offset).start()

    def store(offset):
        lanes = pl.ds(pl.multiple_of(ring.at(offset) * depth, LANES), depth)
        return pltpu.make_async_copy(w_ref.at[:, lanes], w_out_ref.at[:, lanes], w_sem.at[offset])

    done = {0}
    if inside:
        add(0, True)

    def add_landed(step):
        for offset in range(1, shards):
            if inside and offset not in done and max(offset, shards - offset) <= step:
                done.add(offset)
                add(offset, False, len(done) == shards)

    add_landed(4)
    gather.advance(6)
    add_landed(5)
    gather.run(7, shards)
    add_landed(shards - 2)
    gather.finish()
    add_landed(shards - 1)

    def rest(step, carry):
        for way in range(2):
            if not inside:
                over_core(step, way, 1 - core).wait_recv()
            over_core(step, way, core).wait_send()
        return carry

    lax.fori_loop(1, shards, rest, 0)
    branch.finish()
    if inside:
        for offset in range(shards):
            store(offset).wait()


def share_sems(chunks):
    return [
        pltpu.SemaphoreType.DMA((3, chunks)),
        pltpu.SemaphoreType.DMA((3, chunks)),
        pltpu.SemaphoreType.DMA((chunks,)),
    ]


def gather_in_call(shards, cut, in_t, query, key, value, aux, tokens, cot, live):
    depth = in_t.shape[1]
    length, width = tokens.shape
    inside = depth % LANES == 0
    hbm = pl.BlockSpec(memory_space=pl.ANY)
    vmem = pl.BlockSpec(memory_space=pltpu.VMEM)
    out_shape = [
        jax.ShapeDtypeStruct((shards,) + aux.shape, BF16),
        jax.ShapeDtypeStruct((4, length, width), BF16),
    ]
    scratch = [
        pltpu.VMEM((cut.width, depth), BF16),
        pltpu.VMEM((depth, cut.qwidth + 2 * HEAD_WIDTH), BF16),
        pltpu.VMEM((HEADS, depth), BF16),
        pltpu.VMEM((length, width), BF16),
        pltpu.SemaphoreType.DMA((9,)),
        *ring_sems(shards, 4),
        pltpu.SemaphoreType.DMA((shards - 1, 2)),
        pltpu.SemaphoreType.DMA((shards - 1, 2)),
        *share_sems(1),
        *share_sems(1),
    ]
    if inside:
        rows = 4 * length
        out_shape = [jax.ShapeDtypeStruct((cut.width, width), BF16)] + out_shape
        out_shape += [
            jax.ShapeDtypeStruct((rows, width), BF16),
            jax.ShapeDtypeStruct((rows, cut.width), BF16),
            jax.ShapeDtypeStruct((rows, LANES), F32),
        ]
        out_specs = [hbm, vmem, hbm] + [vmem] * 3
        scratch += [
            pltpu.VMEM((rows, cut.width), F32),
            pltpu.VMEM((rows, LANES), F32),
            pltpu.SemaphoreType.DMA((shards,)),
            pltpu.VMEM((cut.width, width), BF16),
            pltpu.VMEM((4, length, width), BF16),
        ]
    else:
        out_shape = [jax.ShapeDtypeStruct((shards, cut.width, depth), BF16)] + out_shape
        out_shape += [jax.ShapeDtypeStruct((4, length, width), BF16)]
        out_specs = [hbm] * 4
    return pl.pallas_call(
        functools.partial(gather_in, shards, cut, inside),
        out_shape=out_shape,
        in_specs=[hbm] * 6 + [vmem] * 2,
        out_specs=out_specs,
        scratch_shapes=scratch,
        compiler_params=pltpu.CompilerParams(
            collective_id=0, has_side_effects=True, vmem_limit_bytes=56 * MIB
        ),
        name="gather_in",
    )(in_t, query, key, value, aux, tokens, cot, live)


def gather_rows(
    shards,
    cut,
    length,
    heads_ref,
    down_ref,
    proj_ref,
    step_ref,
    conv_ref,
    head_ref,
    chan_ref,
    cos_ref,
    sin_ref,
    heads_all_ref,
    down_all_ref,
    out_ref,
    act_ref,
    pack_sem,
    send,
    recv,
):
    ring, pair = Ring(shards), Pair()
    half = down_ref.shape[0] // 2
    rows = lambda number: pl.ds(number * half, half)
    down_way = [
        (
            down_ref.at[rows(number)],
            lambda index, number=number: down_all_ref.at[index, rows(number)],
        )
        for number in range(2)
    ]
    if len(heads_all_ref.shape) == 2:
        mamba = cut.inner // shards
        attn = heads_ref.shape[0] - mamba

        def mamba_place(index):
            return heads_all_ref.at[pl.ds(pl.multiple_of(index * mamba, 16), mamba)]

        def attn_place(index):
            start = pl.multiple_of(cut.inner + index * attn, 16)
            return heads_all_ref.at[pl.ds(start, attn)]

        heads_way = [
            (heads_ref.at[pl.ds(0, mamba)], mamba_place),
            (heads_ref.at[pl.ds(mamba, attn)], attn_place),
        ]
    else:
        heads_way = [
            (
                heads_ref.at[rows(number)],
                lambda index, number=number: heads_all_ref.at[index, rows(number)],
            )
            for number in range(2)
        ]
    ways = (heads_way, down_way)
    packs = [
        pltpu.make_async_copy(own, place(ring.index), pack_sem.at[2 * way + number])
        for way in range(2)
        for number, (own, place) in enumerate(ways[way])
    ]
    for pack in packs:
        pack.start()
    greet(ring, pair)
    gather = Gather(ring, ways, send, recv)
    gather.start()
    count = proj_ref.shape[0] // length

    def body(number, carry):
        rows = pl.ds(pl.multiple_of(number * length, length), length)
        mixer_forward(
            cut,
            proj_ref.at[rows],
            step_ref.at[rows],
            conv_ref,
            head_ref,
            chan_ref,
            cos_ref,
            sin_ref,
            out_ref.at[rows],
            act_ref,
        )
        gather.advance(number + 2)
        return carry

    lax.fori_loop(0, count, body, 0)
    gather.run(count + 2, shards)
    gather.finish()
    for pack in packs:
        pack.wait()


def gather_rows_call(
    shards, cut, length, ordered, heads, down, proj, steps, conv, head, chan, cosine, sine
):
    rows = proj.shape[0]
    tall, width = heads.shape
    hbm = pl.BlockSpec(memory_space=pl.ANY)
    vmem = pl.BlockSpec(memory_space=pltpu.VMEM)
    return pl.pallas_call(
        functools.partial(gather_rows, shards, cut, length),
        out_shape=[
            jax.ShapeDtypeStruct(
                (shards * tall, width) if ordered else (shards, tall, width), BF16
            ),
            jax.ShapeDtypeStruct((shards,) + down.shape, BF16),
            jax.ShapeDtypeStruct((rows, cut.inner + cut.qwidth), BF16),
        ],
        in_specs=[vmem] * 9,
        out_specs=[hbm] * 2 + [vmem],
        scratch_shapes=[
            pltpu.VMEM((length, cut.conv), F32),
            pltpu.SemaphoreType.DMA((4,)),
        ]
        + ring_sems(shards, 2),
        compiler_params=pltpu.CompilerParams(
            collective_id=1, has_side_effects=True, vmem_limit_bytes=48 * MIB
        ),
        name="gather_rows",
    )(heads, down, proj, steps, conv, head, chan, cosine, sine)


class Exchange:
    def __init__(self, pair, chunks, part_ref, core_ref, cross_ref, came_ref, sems):
        self.pair, self.chunks = pair, chunks
        self.part, self.core, self.cross, self.came = part_ref, core_ref, cross_ref, came_ref
        self.send, self.recv = sems
        self.tall = part_ref.shape[1] // chunks

    def rows(self, chunk):
        return pl.ds(chunk * self.tall, self.tall)

    def over_core(self, chunk, which):
        return remote(
            self.part.at[2 + which, self.rows(chunk)],
            self.core.at[which, self.rows(chunk)],
            self.send.at[0, which, chunk],
            self.recv.at[0, which, chunk],
            self.pair.peers[1],
        )

    def over_x(self, chunk):
        return remote(
            self.cross.at[self.rows(chunk)],
            self.came.at[self.rows(chunk)],
            self.send.at[1, 0, chunk],
            self.recv.at[1, 0, chunk],
            self.pair.peers[0],
        )

    def start_one(self, which):
        for chunk in range(self.chunks):
            self.over_core(chunk, which).start()

    def start(self):
        self.start_one(1)
        self.start_one(0)

    def middle(self, chunk):
        self.over_core(chunk, 1).wait_recv()
        rows = self.rows(chunk)
        total = self.part[1, rows].astype(F32) + self.core[1, rows].astype(F32)
        self.cross[rows] = total.astype(BF16)
        self.over_x(chunk).start()

    def sum(self, chunk):
        self.over_core(chunk, 0).wait_recv()
        self.over_x(chunk).wait_recv()
        rows = self.rows(chunk)
        return (
            self.part[0, rows].astype(F32)
            + self.core[0, rows].astype(F32)
            + self.came[rows].astype(F32)
        )

    def finish(self):
        for chunk in range(self.chunks):
            for which in range(2):
                self.over_core(chunk, which).wait_send()
            self.over_x(chunk).wait_send()


class Share:
    def __init__(self, pair, chunks, own_ref, all_ref, sems):
        self.pair, self.chunks, self.own, self.all = pair, chunks, own_ref, all_ref
        self.send, self.recv, self.local = sems
        self.tall = own_ref.shape[0] // chunks

    def rows(self, chunk):
        return pl.ds(chunk * self.tall, self.tall)

    def direct(self, chunk, which):
        return remote(
            self.own.at[self.rows(chunk)],
            self.all.at[1 + which, self.rows(chunk)],
            self.send.at[which, chunk],
            self.recv.at[which, chunk],
            self.pair.peers[which],
        )

    def onward(self, chunk):
        return remote(
            self.all.at[1, self.rows(chunk)],
            self.all.at[3, self.rows(chunk)],
            self.send.at[2, chunk],
            self.recv.at[2, chunk],
            self.pair.peers[1],
        )

    def keep(self, chunk):
        return pltpu.make_async_copy(
            self.own.at[self.rows(chunk)], self.all.at[0, self.rows(chunk)], self.local.at[chunk]
        )

    def start(self, chunk):
        self.direct(chunk, 0).start()
        self.direct(chunk, 1).start()
        self.keep(chunk).start()

    def pass_on(self, chunk):
        self.direct(chunk, 0).wait_recv()
        self.onward(chunk).start()

    def finish(self):
        for chunk in range(self.chunks):
            self.direct(chunk, 0).wait_send()
            self.direct(chunk, 1).wait()
            self.onward(chunk).wait()
            self.keep(chunk).wait()


CHUNKS = 2


def exchange_scratch(length, width):
    return [
        pltpu.VMEM((2, length, width), BF16),
        pltpu.VMEM((length, width), BF16),
        pltpu.VMEM((length, width), BF16),
        pltpu.SemaphoreType.DMA((2, 2, CHUNKS)),
        pltpu.SemaphoreType.DMA((2, 2, CHUNKS)),
    ]


class Scatter:
    def __init__(self, ring, pieces, term, first_ref, slots_ref, send, recv, groups=1):
        self.ring, self.pieces, self.groups, self.term = ring, pieces, groups, term
        self.first, self.slots, self.send, self.recv = first_ref, slots_ref, send, recv
        self.half = slots_ref.shape[2]
        self.tall = self.half // pieces

    def each(self, group):
        size = self.pieces // self.groups
        for piece in range(group * size, (group + 1) * size):
            for way in range(2):
                yield way, piece

    def rows(self, way, piece):
        return pl.ds(way * self.half + piece * self.tall, self.tall)

    def local(self, piece):
        return pl.ds(piece * self.tall, self.tall)

    def due(self, step, way, piece):
        return self.term(self.ring.at((2 * way - 1) * step), self.rows(way, piece))

    def copy(self, step, way, piece, first=False):
        src = self.first.at[way] if first else self.slots.at[step - 2, way]
        return remote(
            src.at[self.local(piece)],
            self.slots.at[step - 1, way, self.local(piece)],
            self.send.at[step - 1, way, piece],
            self.recv.at[step - 1, way, piece],
            self.ring.peer(way),
        )

    def landed(self, step, way, piece):
        here = self.slots.at[step - 1, way, self.local(piece)]
        return remote(
            here,
            here,
            self.send.at[step - 1, way, piece],
            self.recv.at[step - 1, way, piece],
            self.ring.peer(way),
        )

    def start(self, group=0):
        for way, piece in self.each(group):
            self.first[way, self.local(piece)] = self.due(1, way, piece).astype(BF16)
            self.copy(1, way, piece, True).start()

    def total(self, step, way, piece):
        term = self.due(step, way, piece)
        self.landed(step - 1, way, piece).wait_recv()
        return self.slots[step - 2, way, self.local(piece)].astype(F32) + term

    def advance(self, step, group=0):
        for way, piece in self.each(group):
            total = self.total(step, way, piece)
            self.slots[step - 2, way, self.local(piece)] = total.astype(BF16)
            self.copy(step, way, piece).start()

    def run(self, first, stop, group=0):
        def body(step, carry):
            self.advance(step, group)
            return carry

        lax.fori_loop(first, stop, body, 0)

    def result(self, own_ref, share=None, group=0):
        for way, piece in self.each(group):
            total = self.total(self.ring.shards, way, piece)
            own_ref[self.rows(way, piece)] = total.astype(BF16)
            if share is not None:
                share.start(way * self.pieces + piece)

    def chunks(self, group):
        return [way * self.pieces + piece for way, piece in self.each(group)]

    def finish(self):
        for group in range(self.groups):
            for way, piece in self.each(group):
                self.copy(1, way, piece, True).wait_send()

        def body(step, carry):
            for group in range(self.groups):
                for way, piece in self.each(group):
                    self.copy(step, way, piece).wait_send()
            return carry

        lax.fori_loop(2, self.ring.shards, body, 0)


def stored(ref):
    return lambda index, rows: ref[index, rows].astype(F32)


def pieces_of(rows):
    return 2 if rows // 2 % 32 == 0 else 1


def scatter_scratch(shards, rows, width, pieces=None):
    return [
        pltpu.VMEM((2, rows // 2, width), BF16),
        pltpu.VMEM((shards - 1, 2, rows // 2, width), BF16),
    ] + ring_sems(shards, pieces or pieces_of(rows))


def share_scratch(rows, width, chunks):
    return [
        pltpu.VMEM((rows, width), BF16),
        pltpu.SemaphoreType.DMA((3, chunks)),
        pltpu.SemaphoreType.DMA((3, chunks)),
        pltpu.SemaphoreType.DMA((chunks,)),
    ]


def gather_mlp(shards, inside, count, *refs):
    refs = list(refs)
    take = lambda number: [refs.pop(0) for _ in range(number)]
    source_refs = take(count)
    heads_ref, w_out_ref, tokens_ref, live_ref, gain_ref = take(5)
    all_ref, normed_ref, mixed_ref = take(3)
    if inside:
        (sum_ref,) = take(1)
    core_ref, cross_ref, came_ref, ex_send, ex_recv = take(5)
    own_ref, sh_send, sh_recv, sh_local = take(4)
    part_ref, share_ref, pack_sem, send, recv = take(5)

    ring, pair = Ring(shards), Pair()
    depth, wide = share_ref.shape
    if count == 1:
        packs = [pltpu.make_async_copy(source_refs[0], share_ref, pack_sem.at[0])]
    else:
        units = wide // (2 * shards)
        packs = [
            pltpu.make_async_copy(
                ref.at[:, pl.ds(pl.multiple_of((shard * 4 + pair.rep) * units, LANES), units)],
                share_ref.at[:, pl.ds((which * shards + shard) * units, units)],
                pack_sem.at[which * shards + shard],
            )
            for which, ref in enumerate(source_refs)
            for shard in range(shards)
        ]
    for pack in packs:
        pack.start()
    greet(ring, pair)
    for pack in packs:
        pack.wait()
    keep = pltpu.make_async_copy(share_ref, all_ref.at[ring.index], pack_sem.at[0])
    keep.start()
    quarter = depth // 4
    rows = lambda number: pl.ds(number * quarter, quarter)
    piece = lambda number: (
        share_ref.at[rows(number)],
        lambda index: all_ref.at[index, rows(number)],
    )
    gather = Gather(ring, ([piece(0), piece(1)], [piece(2), piece(3)]), send, recv)
    exchange = Exchange(
        pair, CHUNKS, part_ref, core_ref, cross_ref, came_ref, (ex_send, ex_recv)
    )
    share = Share(pair, CHUNKS, own_ref, normed_ref, (sh_send, sh_recv, sh_local))
    length = part_ref.shape[1]

    def partial(number):
        left = heads_ref[pl.ds(number * length, length)]
        for lane in range(0, part_ref.shape[2], WIDE):
            lanes = slice(lane, lane + WIDE)
            part_ref[number, :, lanes] = dot(left, w_out_ref[:, lanes]).astype(BF16)

    def middle(chunk):
        rows = exchange.rows(chunk)
        branch = exchange.sum(chunk)
        mixed = tokens_ref[rows].astype(F32) + live_ref[rows, 0:1] * branch
        mixed_ref[rows] = mixed
        own_ref[rows] = (mixed * norm_scale(mixed) * gain_ref[0:1]).astype(BF16)
        share.start(chunk)

    def add(index, fresh=False):
        if not inside:
            return
        deep = pl.ds(pl.multiple_of(index * depth, LANES), depth)

        def body(number, carry):
            left = normed_ref[number, :, deep]
            rows = pl.ds(pl.multiple_of(number * length, length), length)
            for lane in range(0, wide, WIDE):
                lanes = slice(lane, lane + WIDE)
                term = dot(left, all_ref[index, :, lanes])
                sum_ref[rows, lanes] = term if fresh else sum_ref[rows, lanes] + term
            return carry

        lax.fori_loop(0, 4, body, 0)

    gather.start()
    for number in (3, 2, 1, 0):
        partial(number)
        if number > 1:
            exchange.start_one(number - 2)
    exchange.middle(0)
    exchange.middle(1)
    gather.advance(2)
    middle(0)
    gather.advance(3)
    middle(1)
    gather.advance(4)
    share.pass_on(0)
    gather.advance(5)
    share.pass_on(1)
    gather.advance(6)
    share.finish()
    keep.wait()
    half_way = shards // 2
    add(ring.index, True)
    if half_way < 6:
        add(ring.at(half_way))
    gather.run(7, shards)
    if half_way >= 6:
        add(ring.at(half_way))
    if inside:

        def body(far, carry):
            add(ring.at(far))
            add(ring.at(-far))
            return carry

        lax.fori_loop(2, half_way, body, 0)
    gather.finish()
    add(ring.at(1))
    add(ring.at(-1))
    exchange.finish()


def gather_mlp_call(shards, inside, sources, wide, heads, w_out, tokens, live, gain):
    length, width = tokens.shape
    depth = sources[0].shape[0]
    hbm = pl.BlockSpec(memory_space=pl.ANY)
    vmem = pl.BlockSpec(memory_space=pltpu.VMEM)
    rows = heads.shape[0]
    return pl.pallas_call(
        functools.partial(gather_mlp, shards, inside, len(sources)),
        out_shape=[
            jax.ShapeDtypeStruct((shards, depth, wide), BF16),
            jax.ShapeDtypeStruct((4, length, width), BF16),
            jax.ShapeDtypeStruct((length, width), F32),
        ]
        + [jax.ShapeDtypeStruct((rows, wide), F32)] * inside,
        in_specs=[hbm] * len(sources) + [vmem] * 5,
        out_specs=[vmem] * (3 + inside),
        scratch_shapes=exchange_scratch(length, width)
        + share_scratch(length, width, CHUNKS)
        + [
            pltpu.VMEM((4, length, width), BF16),
            pltpu.VMEM((depth, wide), BF16),
            pltpu.SemaphoreType.DMA((2 * shards,)),
        ]
        + ring_sems(shards, 2),
        compiler_params=pltpu.CompilerParams(
            collective_id=2, has_side_effects=True, vmem_limit_bytes=56 * MIB
        ),
        name="gather_mlp",
    )(*sources, heads, w_out, tokens, live, gain)


TILE = 256
WIDE = 512


def product_tn(left_ref, right_ref, out_ref, number):
    rows = pl.ds(pl.multiple_of(number * TILE, TILE), TILE)
    left = left_ref[:, rows].T
    for lane in range(0, out_ref.shape[1], WIDE):
        lanes = slice(lane, lane + WIDE)
        out_ref[rows, lanes] = dot(left, right_ref[:, lanes]).astype(out_ref.dtype)


def product(left_ref, right_ref, out_ref, number):
    rows = pl.ds(pl.multiple_of(number * TILE, TILE), TILE)
    for lane in range(0, out_ref.shape[1], WIDE):
        lanes = slice(lane, lane + WIDE)
        out_ref[rows, lanes] = dot(left_ref[rows], right_ref[:, lanes]).astype(out_ref.dtype)


def mlp_back(gate_up_ref, branch_ref, w_down_ref, w_mlp_ref, active_ref, d_ref, part_ref):
    half = active_ref.shape[1]
    for lane in range(0, half, WIDE):
        gates, ups = slice(lane, lane + WIDE), slice(half + lane, half + lane + WIDE)
        d_active = dot_nt(branch_ref[...], w_down_ref[gates])
        gate, up = gate_up_ref[:, gates], gate_up_ref[:, ups]
        sig = sigmoid(gate)
        active = gate * sig
        active_ref[:, gates] = (active * up).astype(BF16)
        d_ref[:, gates] = (d_active * up * silu_slope(gate, sig)).astype(BF16)
        d_ref[:, ups] = (d_active * active).astype(BF16)
    for lane in range(0, part_ref.shape[1], WIDE):
        lanes = slice(lane, lane + WIDE)
        part_ref[:, lanes] = dot_nt(d_ref[...], w_mlp_ref[lanes]).astype(BF16)


def mlp_back_call(gate_up, branch, w_down, w_mlp):
    rows, wide = gate_up.shape
    half, width = w_down.shape
    tall = 2 * TILE
    tile = lambda lanes: pl.BlockSpec((tall, lanes), lambda i: (i, 0))
    whole = lambda shape: pl.BlockSpec(shape, lambda i: (0, 0))
    return pl.pallas_call(
        mlp_back,
        grid=(rows // tall,),
        out_shape=[
            jax.ShapeDtypeStruct((rows, half), BF16),
            jax.ShapeDtypeStruct((rows, wide), BF16),
            jax.ShapeDtypeStruct((rows, width), BF16),
        ],
        in_specs=[tile(wide), tile(width), whole(w_down.shape), whole(w_mlp.shape)],
        out_specs=[tile(half), tile(wide), tile(width)],
        compiler_params=pltpu.CompilerParams(vmem_limit_bytes=56 * MIB),
        name="mlp_back",
    )(gate_up, branch, w_down, w_mlp)


def scatter_down(
    shards,
    part_ref,
    branch_two_ref,
    normed_ref,
    d_mlp_ref,
    active_ref,
    w_down_ref,
    mixed_ref,
    cot_ref,
    live_ref,
    gain_ref,
    branch_ref,
    down_own_ref,
    mlp_ref,
    ffn_ref,
    d_mixed_ref,
    gain_sum_ref,
    core_ref,
    cross_ref,
    came_ref,
    ex_send,
    ex_recv,
    own_ref,
    sh_send,
    sh_recv,
    sh_local,
    first_ref,
    slots_ref,
    send,
    recv,
    down_ref,
):
    ring, pair = Ring(shards), Pair()
    greet(ring, pair)
    units = slots_ref.shape[2] * 2

    def down_term(index, rows):
        start = pl.multiple_of(index * units + rows.start, 16)
        return down_ref[pl.ds(start, rows.size)].astype(F32)

    scatter = Scatter(ring, pieces_of(units), down_term, first_ref, slots_ref, send, recv)
    exchange = Exchange(
        pair, CHUNKS, part_ref, core_ref, cross_ref, came_ref, (ex_send, ex_recv)
    )
    share = Share(pair, CHUNKS, own_ref, branch_ref, (sh_send, sh_recv, sh_local))
    gain_sum_ref[...] = jnp.zeros_like(gain_sum_ref)

    def middle(chunk):
        rows = exchange.rows(chunk)
        grad = exchange.sum(chunk)
        values = mixed_ref[rows]
        d_values, gain_sum = norm_back(values, norm_scale(values), gain_ref[0:1], grad)
        gain_sum_ref[0:1] += gain_sum
        d_mixed = cot_ref[rows].astype(F32) + d_values
        d_mixed_ref[rows] = d_mixed
        own_ref[rows] = (live_ref[rows, 0:1] * d_mixed).astype(BF16)
        share.start(chunk)

    def work(first, stop):
        def body(number, carry):
            product_tn(normed_ref, d_mlp_ref, mlp_ref, number)
            return carry

        lax.fori_loop(first, stop, body, 0)

    tiles = mlp_ref.shape[0] // TILE
    exchange.start()

    def down(number, carry):
        product_tn(active_ref, branch_two_ref, down_ref, number)
        return carry

    lax.fori_loop(0, down_ref.shape[0] // TILE, down, 0)
    scatter.start()
    exchange.middle(0)
    exchange.middle(1)
    scatter.advance(2)
    work(0, 3)
    scatter.advance(3)
    work(3, 5)
    middle(0)
    scatter.advance(4)
    work(5, 6)
    scatter.advance(5)
    middle(1)
    scatter.advance(6)
    work(6, tiles)
    scatter.run(7, shards)

    def rest(number, carry):
        product(active_ref, w_down_ref, ffn_ref, number)
        return carry

    lax.fori_loop(0, ffn_ref.shape[0] // TILE, rest, 0)
    scatter.result(down_own_ref)
    share.pass_on(0)
    share.pass_on(1)
    scatter.finish()
    exchange.finish()
    share.finish()


def scatter_down_call(
    shards, part, branch_two, normed, d_mlp, active, w_down, mixed, cot, live, gain
):
    length, width = mixed.shape
    hbm = pl.BlockSpec(memory_space=pl.ANY)
    vmem = pl.BlockSpec(memory_space=pltpu.VMEM)
    units = active.shape[1] // shards
    return pl.pallas_call(
        functools.partial(scatter_down, shards),
        out_shape=[
            jax.ShapeDtypeStruct((4, length, width), BF16),
            jax.ShapeDtypeStruct((units, width), BF16),
            jax.ShapeDtypeStruct((normed.shape[1], d_mlp.shape[1]), BF16),
            jax.ShapeDtypeStruct((4 * length, width), BF16),
            jax.ShapeDtypeStruct((length, width), F32),
            jax.ShapeDtypeStruct((8, width), F32),
        ],
        in_specs=[vmem] * 10,
        out_specs=[hbm] + [vmem] * 5,
        scratch_shapes=exchange_scratch(length, width)
        + share_scratch(length, width, CHUNKS)
        + scatter_scratch(shards, units, width)
        + [pltpu.VMEM((units * shards, width), BF16)],
        compiler_params=pltpu.CompilerParams(
            collective_id=3, has_side_effects=True, vmem_limit_bytes=60 * MIB
        ),
        name="scatter_down",
    )(part, branch_two, normed, d_mlp, active, w_down, mixed, cot, live, gain)


def scatter_mlp(
    shards,
    cut,
    length,
    mlp_ref,
    out_ref,
    proj_ref,
    step_ref,
    grad_ref,
    conv_ref,
    head_ref,
    chan_ref,
    cos_ref,
    sin_ref,
    down_ref,
    ffn_ref,
    down_all_ref,
    ffn_came_ref,
    mlp_own_ref,
    out_own_ref,
    d_ref,
    d_t_ref,
    conv_sum_ref,
    head_sum_ref,
    chan_sum_ref,
    act_ref,
    d_act_ref,
    d_pair_ref,
    col_ref,
    first_ref,
    slots_ref,
    send,
    recv,
    out_first_ref,
    out_slots_ref,
    out_send,
    out_recv,
    sh_send,
    sh_recv,
    sh_local,
    ffn_send,
    ffn_recv,
    shared_ref,
    shared_came_ref,
    add_sem,
):
    ring, pair = Ring(shards), Pair()
    greet(ring, pair, pair.corner)
    share = Share(pair, 1, down_ref, down_all_ref, (sh_send, sh_recv, sh_local))
    ffn = [
        remote(
            ffn_ref.at[1 + which],
            ffn_came_ref.at[which],
            ffn_send.at[which],
            ffn_recv.at[which],
            peer,
        )
        for which, peer in enumerate(pair.peers + (pair.corner,))
    ]
    mlp = Scatter(
        ring, pieces_of(mlp_ref.shape[1]), stored(mlp_ref), first_ref, slots_ref, send, recv
    )
    tall = out_slots_ref.shape[2] * 2
    mamba = cut.inner // shards

    def out_rows(index, rows):
        if rows.start < mamba:
            start = index * mamba + rows.start
        else:
            start = cut.inner + index * (tall - mamba) + rows.start - mamba
        return out_ref[pl.ds(pl.multiple_of(start, 16), rows.size)].astype(F32)

    out = Scatter(
        ring,
        pieces_of(tall),
        stored(out_ref) if len(out_ref.shape) == 3 else out_rows,
        out_first_ref,
        out_slots_ref,
        out_send,
        out_recv,
    )
    mlp.start()
    out.start()
    share.start(0)
    for copy in ffn:
        copy.start()
    for ref in (conv_sum_ref, head_sum_ref, chan_sum_ref):
        ref[...] = jnp.zeros_like(ref)
    count = proj_ref.shape[0] // length

    def body(number, carry):
        rows = pl.ds(pl.multiple_of(number * length, length), length)
        mixer_backward(
            cut,
            proj_ref.at[rows],
            step_ref.at[rows],
            grad_ref.at[rows],
            conv_ref,
            head_ref,
            chan_ref,
            cos_ref,
            sin_ref,
            d_ref.at[rows],
            conv_sum_ref,
            head_sum_ref,
            chan_sum_ref,
            act_ref,
            d_act_ref,
            d_pair_ref,
            col_ref,
        )
        mlp.advance(number + 2)
        out.advance(number + 2)
        half = LANES // 2
        for lane in range(0, cut.width, LANES):
            turned = d_ref[rows, lane : lane + LANES].T
            if lane >= cut.maps:
                shared_ref[lane - cut.maps : lane - cut.maps + LANES, rows] = turned
                continue
            for part in range(2):
                to = cut.ring_row(lane + part * half)
                d_t_ref[to : to + half, rows] = turned[part * half : (part + 1) * half]
        return carry

    lax.fori_loop(0, count, body, 0)
    core = pair.rep % 2
    of_core = lambda which: pl.multiple_of(which * cut.shared, 16)
    add = remote(
        shared_ref.at[pl.ds(of_core(1 - core), cut.shared)],
        shared_came_ref,
        add_sem.at[0],
        add_sem.at[1],
        pair.peers[1],
    )
    add.start()
    share.pass_on(0)
    mlp.advance(count + 2)
    out.advance(count + 2)
    add.wait()
    half = cut.shared // 2
    for way in range(2):
        rows = pl.ds(pl.multiple_of(of_core(core) + way * half, 16), half)
        to = way * cut.way + cut.maps // 2
        middle = 2 * length
        for here, there in ((0, middle), (middle, 0)):
            total = shared_ref[rows, here : here + middle].astype(F32)
            total = total + shared_came_ref[
                way * half : (way + 1) * half, there : there + middle
            ].astype(F32)
            d_t_ref[to : to + half, here : here + middle] = total.astype(BF16)

    def rest(step, carry):
        mlp.advance(step)
        out.advance(step)
        return carry

    lax.fori_loop(count + 3, shards, rest, 0)
    mlp.result(mlp_own_ref)
    out.result(out_own_ref)
    mlp.finish()
    out.finish()
    share.finish()
    for copy in ffn:
        copy.wait()


def scatter_mlp_call(
    shards, cut, length, mlp, out, proj, steps, grad, conv, head, chan, cosine, sine, down, ffn
):
    hbm = pl.BlockSpec(memory_space=pl.ANY)
    rows = proj.shape[0]
    vmem = pl.BlockSpec(memory_space=pltpu.VMEM)
    depth, wide = mlp.shape[1:]
    width = out.shape[-1]
    tall = out.size // width // shards
    return pl.pallas_call(
        functools.partial(scatter_mlp, shards, cut, length),
        out_shape=[
            jax.ShapeDtypeStruct((4,) + down.shape, BF16),
            jax.ShapeDtypeStruct((3, length, width), BF16),
            jax.ShapeDtypeStruct((depth, wide), BF16),
            jax.ShapeDtypeStruct((tall, width), BF16),
            jax.ShapeDtypeStruct((rows, cut.width), BF16),
            jax.ShapeDtypeStruct((2 * cut.way, rows), BF16),
            jax.ShapeDtypeStruct(conv.shape, F32),
            jax.ShapeDtypeStruct(head.shape, F32),
            jax.ShapeDtypeStruct(chan.shape, F32),
        ],
        in_specs=[vmem] * 11 + [hbm],
        out_specs=[hbm] * 2 + [vmem] * 7,
        scratch_shapes=[
            pltpu.VMEM((length, cut.conv), F32),
            pltpu.VMEM((length, cut.conv), F32),
            pltpu.VMEM((length, length), F32),
            pltpu.VMEM((LANES, length), F32),
        ]
        + scatter_scratch(shards, depth, wide)
        + scatter_scratch(shards, tall, width)
        + share_sems(1)
        + [pltpu.SemaphoreType.DMA((3,))] * 2
        + [
            pltpu.VMEM((2 * cut.shared, rows), BF16),
            pltpu.VMEM((cut.shared, rows), BF16),
            pltpu.SemaphoreType.DMA((2,)),
        ],
        compiler_params=pltpu.CompilerParams(
            collective_id=4, has_side_effects=True, vmem_limit_bytes=60 * MIB
        ),
        name="scatter_mlp",
    )(mlp, out, proj, steps, grad, conv, head, chan, cosine, sine, down, ffn)


GROUPS = 2
PIECES = 6


def scatter_in(shards, inside, *refs):
    refs = list(refs)
    take = lambda count: [refs.pop(0) for _ in range(count)]
    if inside:
        d_t_ref, normed_ref, d_hbm, w_hbm = take(4)
    else:
        in_ref, part_ref = take(2)
    small_ref, tokens_ref, d_mixed_ref, gain_ref, mlp_ref, out_ref = take(6)
    in_all_ref, small_all_ref, mlp_all_ref, out_all_ref, grad_ref = take(5)
    core_ref, cross_ref, came_ref, ex_send, ex_recv = take(5)
    in_scratch, small_scratch = take(4), take(4)
    own_ref, sh_send, sh_recv, sh_local = take(4)
    small_own_ref, sm_send, sm_recv, sm_local = take(4)
    mlp_sems, out_sems = take(3), take(3)
    move_ref, move_sem = take(2)
    if inside:
        d_ref, w_ref, part_ref, small_all, gain_sum_ref, load_sem = take(6)

    ring, pair = Ring(shards), Pair()
    if inside:
        loads = [
            pltpu.make_async_copy(src, dst, load_sem.at[number])
            for number, (src, dst) in enumerate(((d_hbm, d_ref), (w_hbm, w_ref)))
        ]
        for load in loads:
            load.start()
        depth = w_ref.shape[1] // shards

        def term(index, rows):
            lanes = pl.ds(pl.multiple_of(index * depth, LANES), depth)
            return dot(d_t_ref[rows], normed_ref[:, lanes])

        small_term = stored(small_all)
    else:
        term, small_term = stored(in_ref), stored(small_ref)
    group = shards // 4
    here, rep = ring.index, pair.rep
    to = (group * rep + here // 4, here % 4)
    by = (4 * (here % group) + rep, here // group)
    far = to[0] * 4 + to[1] - here * 4 - rep
    limit = (4 * shards) ** 2
    moves = (far * far + limit - 1) // limit
    peer = {"fsdp": to[0], "rep": to[1]}
    move = remote(out_ref, move_ref, move_sem.at[0], move_sem.at[1], peer)
    stay = pltpu.make_async_copy(out_ref, move_ref, move_sem.at[2])
    greet(ring, pair, maybe=(peer, {"fsdp": by[0], "rep": by[1]}), are=moves)

    @pl.when(moves == 1)
    def _():
        move.start()

    @pl.when(moves == 0)
    def _():
        stay.start()

    pieces = PIECES
    scatter = Scatter(ring, pieces, term, *in_scratch, groups=GROUPS)
    small = Scatter(ring, 1, small_term, *small_scratch)
    exchange = Exchange(
        pair, CHUNKS, part_ref, core_ref, cross_ref, came_ref, (ex_send, ex_recv)
    )
    share = Share(pair, 2 * pieces, own_ref, in_all_ref, (sh_send, sh_recv, sh_local))
    small_share = Share(pair, 2, small_own_ref, small_all_ref, (sm_send, sm_recv, sm_local))
    mlp_share = Share(pair, CHUNKS, mlp_ref, mlp_all_ref, mlp_sems)
    out_share = Share(pair, 1, move_ref, out_all_ref, out_sems)

    def middle(chunk):
        rows = exchange.rows(chunk)
        grad = exchange.sum(chunk)
        values = tokens_ref[rows].astype(F32)
        d_values, _ = norm_back(values, norm_scale(values), gain_ref[0:1], grad)
        grad_ref[rows] = (d_mixed_ref[rows] + d_values).astype(BF16)

    def partial(number):
        length = part_ref.shape[1]
        wide = 4 * LANES
        rows = pl.ds(number * length, length)

        def body(tile, carry):
            lanes = pl.ds(pl.multiple_of(tile * wide, wide), wide)
            grad = dot(d_ref[rows], w_ref[:, lanes])
            part_ref[number, :, lanes] = grad.astype(BF16)
            gain_sum_ref[0:1, lanes] += jnp.sum(
                grad * normed_ref[rows, lanes].astype(F32), axis=0, keepdims=True
            )
            return carry

        lax.fori_loop(0, w_ref.shape[1] // wide, body, 0)

    scatter.start(0)
    for chunk in range(CHUNKS):
        mlp_share.start(chunk)
    if inside:
        gain_sum_ref[...] = jnp.zeros_like(gain_sum_ref)
        for load in loads:
            load.wait()
    for number in range(4):
        if inside:
            partial(number)
        scatter.advance(number + 2, 0)
    if inside:
        small_all[...] = small_ref[...]
        gain_sum = gain_sum_ref[0:1] / gain_ref[0:1]
        for index in range(shards):
            for row in range(depth // LANES):
                at = index * depth + row * LANES
                small_all[index, row : row + 1] = gain_sum[:, at : at + LANES].astype(BF16)
    exchange.start()
    small.start()
    scatter.advance(6, 0)
    exchange.middle(0)
    small.advance(2)
    exchange.middle(1)

    @pl.when(moves == 1)
    def _():
        move.wait()

    @pl.when(moves == 0)
    def _():
        stay.wait()

    out_share.start(0)
    scatter.run(7, shards, 0)
    small.advance(3)
    scatter.start(1)
    scatter.result(own_ref, share, 0)
    for step in range(2, 6):
        scatter.advance(step, 1)
        small.advance(step + 2)
        if step in (3, 4):
            middle(step - 3)
    small.run(8, shards)
    for chunk in range(CHUNKS):
        mlp_share.pass_on(chunk)
    scatter.advance(6, 1)
    out_share.pass_on(0)
    small.result(small_own_ref, small_share)
    for chunk in scatter.chunks(0):
        share.pass_on(chunk)
    scatter.run(7, shards, 1)
    scatter.result(own_ref, share, 1)
    for chunk in range(2):
        small_share.pass_on(chunk)
    for chunk in scatter.chunks(1):
        share.pass_on(chunk)
    scatter.finish()
    small.finish()
    exchange.finish()
    share.finish()
    small_share.finish()
    mlp_share.finish()
    out_share.finish()


def scatter_in_call(shards, depth, inside, given, small, tokens, d_mixed, gain, mlp, out):
    length, width = tokens.shape
    hbm = pl.BlockSpec(memory_space=pl.ANY)
    vmem = pl.BlockSpec(memory_space=pltpu.VMEM)
    wide = given[0].shape[0] if inside else given[0].shape[-2]
    tall, lanes = small.shape[1:]
    extra = []
    if inside:
        extra = [
            pltpu.VMEM(given[2].shape, BF16),
            pltpu.VMEM(given[3].shape, BF16),
            pltpu.VMEM((4, length, width), BF16),
            pltpu.VMEM(small.shape, BF16),
            pltpu.VMEM((8, width), F32),
            pltpu.SemaphoreType.DMA((2,)),
        ]
    return pl.pallas_call(
        functools.partial(scatter_in, shards, inside),
        out_shape=[
            jax.ShapeDtypeStruct((4, wide, depth), BF16),
            jax.ShapeDtypeStruct((4, tall, lanes), BF16),
            jax.ShapeDtypeStruct((4,) + mlp.shape, BF16),
            jax.ShapeDtypeStruct((4,) + out.shape, BF16),
            jax.ShapeDtypeStruct((length, width), BF16),
        ],
        in_specs=([vmem] * 2 + [hbm] * 2 if inside else [vmem] * 2) + [vmem] * 6,
        out_specs=[hbm] * 4 + [vmem],
        scratch_shapes=exchange_scratch(length, width)
        + scatter_scratch(shards, wide, depth, PIECES)
        + scatter_scratch(shards, tall, lanes, 1)
        + share_scratch(wide, depth, 2 * PIECES)
        + share_scratch(tall, lanes, 2)
        + share_sems(CHUNKS)
        + share_sems(1)
        + [pltpu.VMEM(out.shape, BF16), pltpu.SemaphoreType.DMA((3,))]
        + extra,
        compiler_params=pltpu.CompilerParams(
            collective_id=5, has_side_effects=True, vmem_limit_bytes=60 * MIB
        ),
        name="scatter_in",
    )(*given, small, tokens, d_mixed, gain, mlp, out)


def columns(array, start, width):
    return lax.dynamic_slice_in_dim(array, start, width, axis=array.ndim - 1)


def norm_scale(values):
    return lax.rsqrt(jnp.mean(values * values, axis=-1, keepdims=True) + epsilon)


def norm_back(values, scale, gain, grad):
    inner = jnp.mean(gain * grad * values, axis=-1, keepdims=True)
    d_values = scale * gain * grad - values * (scale * scale * scale) * inner
    return d_values, jnp.sum(grad * values * scale, axis=0, keepdims=True)


def ring_at(position, shards):
    place = (position + 2 * shards) % shards
    back = place // (shards // 2)
    return (1 - back) * 2 * place + back * (2 * (shards - 1 - place) + 1)


def ring_place(index, shards):
    odd = index % 2
    return (1 - odd) * (index // 2) + odd * (shards - 1 - index // 2)


def after(value, *others):
    return lax.optimization_barrier((value,) + others)[0]


def rep_order(reps):
    order = [0]
    bit = reps // 2
    while bit:
        order = order + [member ^ bit for member in order]
        bit //= 2
    return order


def on_device(
    sizes,
    tokens,
    lengths,
    mixer_gain,
    in_proj,
    conv_weight,
    conv_bias,
    decay_log,
    step_bias,
    skip_gain,
    query_weight,
    key_weight,
    value_weight,
    mamba_out,
    attn_out,
    mlp_gain,
    gate_weight,
    up_weight,
    down_weight,
    cotangent,
):
    shards, reps = sizes
    cut = Cut(reps)
    rep = lax.axis_index("rep")
    fsdp = lax.axis_index("fsdp")
    place = ring_place(fsdp, shards)
    assert reps == 4
    length, width = tokens.shape
    depth = in_proj.shape[0]
    own = conv_weight.shape[1]
    channels = own * shards
    low = lambda v: v.astype(BF16)

    in_t = in_proj.T
    extra = 16
    aux = jnp.concatenate([mixer_gain, mlp_gain, conv_weight.reshape(-1), conv_bias], axis=0)
    aux_size = aux.shape[0]
    aux = jnp.pad(aux, (0, extra * 2 * LANES - aux_size)).reshape(extra, 2 * LANES)
    group = shards // reps
    pairs = [
        (g * reps + part, (reps * (g % group) + part) * reps + g // group)
        for g in range(shards)
        for part in range(reps)
    ]
    mamba_rows = mamba_out.shape[0] // reps
    attn_rows = attn_out.shape[0] // reps
    out_rows = mamba_rows + attn_rows
    share_out = jnp.concatenate(
        [
            lax.dynamic_slice_in_dim(mamba_out, mamba_rows * rep, mamba_rows, axis=0),
            lax.dynamic_slice_in_dim(attn_out, attn_rows * rep, attn_rows, axis=0),
        ],
        axis=0,
    )
    units = down_weight.shape[0] // reps
    if units % LANES:
        pick = lambda w: lax.dynamic_index_in_dim(
            w.reshape(depth, shards, reps, units), rep, axis=2, keepdims=False
        ).reshape(depth, shards * units)
        sources = (jnp.concatenate([pick(gate_weight), pick(up_weight)], axis=1),)
    else:
        sources = (gate_weight, up_weight)
    share_down = lax.dynamic_slice_in_dim(down_weight, units * rep, units, axis=0)

    live = (jnp.arange(length) < lengths[0]).astype(F32)[:, None]
    stream = tokens.astype(F32)
    live_wide = jnp.broadcast_to(live, (length, LANES))
    w_in, aux_all, branch_two, *made = gather_in_call(
        shards,
        cut,
        in_t,
        query_weight,
        key_weight,
        value_weight,
        aux,
        tokens,
        cotangent,
        live_wide,
    )
    if w_in.ndim == 3:
        w_in = jnp.moveaxis(w_in, 0, 1).reshape(cut.width, width)
    branch_two = branch_two.reshape(reps * length, width)
    share_out = lax.ppermute(share_out, ("fsdp", "rep"), pairs)

    put = lax.dynamic_update_slice
    inner_rows = mamba_rows * shards
    half_ff = shards * units

    aux_all = aux_all.reshape(shards, -1)[:, :aux_size].astype(F32)
    gain_one = aux_all[:, :depth].reshape(1, width)
    gain_two = aux_all[:, depth : 2 * depth].reshape(1, width)
    conv_all = aux_all[:, 2 * depth :].reshape(shards, CONV + 1, own)
    conv_all = conv_all.transpose(1, 0, 2).reshape(CONV + 1, channels)
    conv_own = jnp.concatenate(
        [columns(conv_all, cut.inner * rep, cut.inner), conv_all[:, INNER:]], axis=1
    )
    conv_own = jnp.pad(conv_own, ((0, 7 - CONV), (0, 0)))
    of_heads = lambda v: jnp.pad(
        lax.dynamic_slice_in_dim(v, cut.heads * rep, cut.heads), (0, LANES - cut.heads)
    )
    head_own = jnp.stack([of_heads(decay_log), of_heads(step_bias)])
    head_own = jnp.pad(head_own, ((0, 6), (0, 0)))
    chan_own = lax.dynamic_slice_in_dim(skip_gain, cut.heads * rep, cut.heads)
    chan_own = jnp.pad(jnp.repeat(chan_own, HDIM)[None, :], ((0, 7), (0, 0)))
    cosine, sine = turn_tables(length)

    if len(made) == 3:
        normed, proj, steps = made
    else:
        stream_all = made[0].reshape(reps * length, width).astype(F32)
        scale_all = norm_scale(stream_all)
        normed = low(stream_all * scale_all * gain_one)
        proj = dot_nt(normed, w_in)
        steps = proj[:, cut.step : cut.step + LANES]
        proj = low(proj)
    inside = depth % LANES == 0
    ordered = mamba_rows % 16 == 0 and attn_rows % 16 == 0
    w_out, w_down, mixed_heads = gather_rows_call(
        shards,
        cut,
        length,
        ordered,
        share_out,
        share_down,
        proj,
        steps,
        conv_own,
        head_own,
        chan_own,
        cosine,
        sine,
    )
    if not ordered:
        w_out = jnp.concatenate(
            [
                w_out[:, :mamba_rows].reshape(-1, width),
                w_out[:, mamba_rows:].reshape(-1, width),
            ],
            axis=0,
        )
    w_down = w_down.reshape(-1, width)
    gain_rows = jnp.broadcast_to(gain_two, (8, width))
    w_mlp, normed_two, mixed, *gate_up = gather_mlp_call(
        shards, inside, sources, 2 * half_ff, mixed_heads, w_out, tokens, live_wide, gain_rows
    )
    w_mlp = w_mlp.reshape(width, -1)
    normed_two = normed_two.reshape(reps * length, width)
    gate_up = gate_up[0] if inside else dot(normed_two, w_mlp)
    activated, d_gate_up, d_two = mlp_back_call(gate_up, branch_two, w_down, w_mlp)
    d_two = d_two.reshape(reps, length, width)
    branch_one, s_down, g_mlp, ffn, d_mixed, gain_two_sum = scatter_down_call(
        shards,
        d_two,
        branch_two,
        normed_two,
        d_gate_up,
        activated,
        w_down,
        mixed,
        cotangent,
        live_wide,
        gain_rows,
    )
    g_mlp = g_mlp.reshape(shards, depth, -1)
    ffn = ffn.reshape(reps, length, width)

    branch_one = branch_one.reshape(reps * length, width)
    d_heads = dot_nt(branch_one, w_out)
    g_out = low(dot_tn(mixed_heads, branch_one))
    if not ordered:
        g_out = jnp.concatenate(
            [
                g_out[:inner_rows].reshape(shards, mamba_rows, width),
                g_out[inner_rows:].reshape(shards, attn_rows, width),
            ],
            axis=1,
        )
    downs, came, s_mlp, s_out, d_proj, d_proj_t, conv_sum, head_sum, chan_sum = scatter_mlp_call(
        shards,
        cut,
        length,
        g_mlp,
        g_out,
        proj,
        steps,
        d_heads,
        conv_own,
        head_own,
        chan_own,
        cosine,
        sine,
        s_down,
        ffn,
    )
    ffn_sum = ffn[0].astype(F32) + came.astype(F32).sum(axis=0)
    output = low(mixed + live * ffn_sum)
    if inside:
        given = (d_proj_t, normed, d_proj, w_in)
        gain_one_sum = jnp.zeros((width,), F32)
    else:
        g_in = low(dot(d_proj_t, normed))
        g_in = jnp.moveaxis(g_in.reshape(2 * cut.way, shards, depth), 1, 0)
        d_one = dot(d_proj, w_in)
        gain_one_sum = jnp.sum(d_one * stream_all * scale_all, axis=0)
        given = (g_in, low(d_one).reshape(reps, length, width))

    conv_sums = jnp.zeros((CONV + 1, channels), F32)
    conv_sums = put(conv_sums, conv_sum[: CONV + 1, : cut.inner], (0, cut.inner * rep))
    conv_sums = put(conv_sums, conv_sum[: CONV + 1, cut.inner :], (0, INNER))
    head_sums = jnp.zeros((3, HEADS), F32)
    own_sums = jnp.stack(
        [
            head_sum[0, : cut.heads],
            head_sum[1, : cut.heads],
            jnp.sum(chan_sum[0].reshape(cut.heads, HDIM), axis=1),
        ]
    )
    head_sums = put(head_sums, own_sums, (0, cut.heads * rep))
    small = jnp.concatenate(
        [
            gain_one_sum.reshape(shards, depth),
            gain_two_sum[0].reshape(shards, depth),
            conv_sums.reshape(CONV + 1, shards, own).transpose(1, 0, 2).reshape(shards, -1),
            jnp.broadcast_to(head_sums.reshape(1, -1), (shards, 3 * HEADS)),
        ],
        axis=1,
    )
    small_size = small.shape[1]
    tall = 32
    small = jnp.pad(low(small), ((0, 0), (0, tall * LANES - small_size)))
    small = small.reshape(shards, tall, LANES)
    ins, smalls, mlps, outs, grad_tokens = scatter_in_call(
        shards,
        depth,
        inside,
        given,
        small,
        tokens,
        d_mixed,
        jnp.broadcast_to(gain_one, (8, width)),
        s_mlp,
        s_out,
    )

    places = jnp.stack([rep ^ member for member in rep_order(reps)]).astype(jnp.int32)
    spread = functools.partial(spread_call, places)
    out_mamba, out_attn = spread(
        outs,
        [(mamba_rows * reps, width), (attn_rows * reps, width)],
        [
            (0, slice(0, mamba_rows), slice(0, width), mamba_rows, 0, 0),
            (1, slice(mamba_rows, out_rows), slice(0, width), attn_rows, 0, 0),
        ],
    )
    (out_down,) = spread(
        downs,
        [(units * reps, width)],
        [(0, slice(0, units), slice(0, width), units, 0, 0)],
    )
    out_gate, out_up = spread(
        mlps,
        [(depth, half_ff * reps)] * 2,
        [
            (
                which,
                slice(0, depth),
                slice(which * half_ff + shard * units, which * half_ff + (shard + 1) * units),
                0,
                units,
                shard * units * reps,
            )
            for which in range(2)
            for shard in range(shards)
        ],
    )
    out_wide, out_query, out_key, out_value = spread_in_call(cut, places, ins)
    out_proj = out_wide.T
    small = smalls.astype(F32).sum(axis=0).reshape(-1)[:small_size]
    out_gain_one = small[:depth]
    out_gain_two = small[depth : 2 * depth]
    conv_sums = small[2 * depth : 2 * depth + (CONV + 1) * own].reshape(CONV + 1, own)
    out_decay, out_step, out_skip = small[2 * depth + (CONV + 1) * own :].reshape(3, HEADS)
    return (
        output,
        grad_tokens,
        out_gain_one,
        out_proj,
        conv_sums[:CONV],
        conv_sums[CONV],
        out_decay,
        out_step,
        out_skip,
        out_query,
        out_key,
        out_value,
        out_mamba,
        out_attn,
        out_gain_two,
        out_gate,
        out_up,
        out_down,
    )


def solution(mesh):
    rows = P(("fsdp", "rep"), None)
    shard = P("fsdp", None)
    in_specs = (
        rows,
        P(("fsdp", "rep")),
        P("fsdp"),
        shard,
        P(None, "fsdp"),
        P("fsdp"),
        P(),
        P(),
        P(),
        shard,
        shard,
        shard,
        shard,
        shard,
        P("fsdp"),
        shard,
        shard,
        shard,
        rows,
    )
    out_specs = (
        rows,
        rows,
        P("fsdp"),
        shard,
        P(None, "fsdp"),
        P("fsdp"),
        P(),
        P(),
        P(),
        shard,
        shard,
        shard,
        shard,
        shard,
        P("fsdp"),
        shard,
        shard,
        shard,
    )
    sizes = (mesh.shape["fsdp"], mesh.shape["rep"])
    return jax.shard_map(
        functools.partial(on_device, sizes),
        mesh=mesh,
        in_specs=in_specs,
        out_specs=out_specs,
        check_vma=False,
    )
```

```python
import functools

import jax
import jax.numpy as jnp
from jax import lax
from jax.experimental import pallas as pl
from jax.experimental.pallas import tpu as pltpu
from jax.sharding import PartitionSpec as P

HEADS = 48
HDIM = 64
STATE = 256
CONV = 4
QH = 8
KVH = 2
HEAD_WIDTH = 128
INNER = HEADS * HDIM
LANES = 128
ROWS = 128
MIB = 1 << 20
MESH = pl.DeviceIdType.MESH

epsilon = 1e-05
BF16 = jnp.bfloat16
F32 = jnp.float32
HIGHEST = lax.Precision.HIGHEST


def dot(left, right, contract=((1,), (0,)), precision=None):
    return lax.dot_general(
        left, right, (contract, ((), ())), preferred_element_type=F32, precision=precision
    )


def dot_tn(left, right, precision=None):
    return dot(left, right, ((0,), (0,)), precision)


def dot_nt(left, right, precision=None):
    return dot(left, right, ((1,), (1,)), precision)


def sigmoid(v):
    return 1.0 / (1.0 + jnp.exp(-v))


def silu_slope(v, sig):
    return sig * (1.0 + v * (1.0 - sig))


def softplus(v):
    return jnp.maximum(v, 0.0) + jnp.log1p(jnp.exp(-jnp.abs(v)))


def shift_down(v, by):
    if by == 0:
        return v
    return jnp.concatenate([jnp.zeros((by, v.shape[1]), v.dtype), v[:-by]], axis=0)


def shift_up(v, by):
    if by == 0:
        return v
    return jnp.concatenate([v[by:], jnp.zeros((by, v.shape[1]), v.dtype)], axis=0)


class Cut:
    def __init__(self, reps):
        self.heads = HEADS // reps
        self.inner = INNER // reps
        self.qheads = QH // reps
        self.qwidth = self.qheads * HEAD_WIDTH
        self.q = 0
        self.step = self.qwidth
        self.z = self.step + LANES
        self.x = self.z + self.inner
        self.maps = self.x + self.inner
        self.k = self.maps + 2 * STATE
        self.v = self.k + HEAD_WIDTH
        self.width = self.v + HEAD_WIDTH
        self.conv = self.inner + 2 * STATE
        self.shared = (self.width - self.maps) // 2
        self.way = (self.maps + self.shared) // 2

    def ring_row(self, column):
        half = self.maps // 2
        return column if column < half else column - half + self.way


def conv_out_of(ref, lanes, start, conv_ref):
    width = lanes.stop - lanes.start
    given = ref[:, start : start + width].astype(F32)
    total = conv_ref[CONV : CONV + 1, lanes]
    for tap in range(CONV):
        total = total + conv_ref[tap : tap + 1, lanes] * shift_down(given, CONV - 1 - tap)
    return total, given


def conv_back(d_out, given, conv_ref, lanes, sums_ref):
    d_given = jnp.zeros_like(d_out)
    for tap in range(CONV):
        back = CONV - 1 - tap
        d_given = d_given + conv_ref[tap : tap + 1, lanes] * shift_up(d_out, back)
        sums_ref[tap : tap + 1, lanes] += jnp.sum(
            d_out * shift_down(given, back), axis=0, keepdims=True
        )
    sums_ref[CONV : CONV + 1, lanes] += jnp.sum(d_out, axis=0, keepdims=True)
    return d_given


def ones_triangle(length, upper):
    row = lax.broadcasted_iota(jnp.int32, (length, length), 0)
    col = lax.broadcasted_iota(jnp.int32, (length, length), 1)
    return jnp.where(col >= row if upper else col <= row, 1.0, 0.0).astype(F32)


def steps_of(step_ref, head_ref):
    raw = step_ref[...] + head_ref[1:2, :]
    step = softplus(raw)
    decay = -step * jnp.exp(head_ref[0:1, :])
    running = dot(ones_triangle(raw.shape[0], False), decay, precision=HIGHEST)
    return raw, step, decay, running


def decay_block(running, running_t, head, block):
    top, width = block * ROWS, (block + 1) * ROWS
    gap = running[top:width, head : head + 1] - running_t[head : head + 1, :width]
    row = lax.broadcasted_iota(jnp.int32, (ROWS, width), 0) + top
    col = lax.broadcasted_iota(jnp.int32, (ROWS, width), 1)
    return jnp.where(row >= col, jnp.exp(gap), 0.0)


def turn(v, cos_ref, sin_ref):
    half = HEAD_WIDTH // 2
    return v * cos_ref[...] + pltpu.roll(v, half, 1) * sin_ref[...]


def turn_back(v, cos_ref, sin_ref):
    half = HEAD_WIDTH // 2
    return v * cos_ref[...] - pltpu.roll(v, half, 1) * sin_ref[...]


def softmax_rows(q, k):
    scores = dot_nt(q, k) * HEAD_WIDTH ** (-0.5)
    row = lax.broadcasted_iota(jnp.int32, scores.shape, 0)
    col = lax.broadcasted_iota(jnp.int32, scores.shape, 1)
    scores = jnp.where(row >= col, scores, -1e30)
    top = jnp.max(scores, axis=1, keepdims=True)
    weight = jnp.exp(scores - top)
    return weight / jnp.sum(weight, axis=1, keepdims=True)


def mixer_forward(
    cut, proj_ref, step_ref, conv_ref, head_ref, chan_ref, cos_ref, sin_ref, out_ref, act_ref
):
    length = proj_ref.shape[0]
    for lane in range(0, cut.conv, 2 * LANES):
        lanes = slice(lane, min(lane + 2 * LANES, cut.conv))
        total, _ = conv_out_of(proj_ref, lanes, cut.x + lane, conv_ref)
        act_ref[:, lanes] = total * sigmoid(total)
    _, step, _, running = steps_of(step_ref, head_ref)
    step_t, running_t = step.T, running.T
    in_map = act_ref[:, cut.inner : cut.inner + STATE].astype(BF16)
    out_map = act_ref[:, cut.inner + STATE : cut.inner + 2 * STATE].astype(BF16)
    pairing = dot_nt(out_map, in_map)
    first = lax.broadcasted_iota(jnp.int32, (ROWS, LANES), 1) < HDIM
    for pair in range(cut.heads // 2):
        lanes = slice(pair * LANES, (pair + 1) * LANES)
        given = act_ref[:, lanes].astype(BF16)
        for block in range(length // ROWS):
            rows = slice(block * ROWS, (block + 1) * ROWS)
            parts = []
            for head in (2 * pair, 2 * pair + 1):
                mixing = (
                    pairing[rows, : rows.stop]
                    * decay_block(running, running_t, head, block)
                    * step_t[head : head + 1, : rows.stop]
                )
                parts.append(dot(mixing.astype(BF16), given[: rows.stop]))
            ssm = jnp.where(first, parts[0], parts[1])
            ssm = ssm + chan_ref[0:1, lanes] * act_ref[rows, lanes]
            gate = proj_ref[rows, cut.z + lanes.start : cut.z + lanes.stop].astype(F32)
            out_ref[rows, lanes] = (ssm * gate * sigmoid(gate)).astype(BF16)
    key = turn(proj_ref[:, cut.k : cut.k + HEAD_WIDTH].astype(F32), cos_ref, sin_ref).astype(BF16)
    value = proj_ref[:, cut.v : cut.v + HEAD_WIDTH].astype(BF16)
    for head in range(cut.qheads):
        at = cut.q + head * HEAD_WIDTH
        query = turn(proj_ref[:, at : at + HEAD_WIDTH].astype(F32), cos_ref, sin_ref).astype(BF16)
        probs = softmax_rows(query, key).astype(BF16)
        to = cut.inner + head * HEAD_WIDTH
        out_ref[:, to : to + HEAD_WIDTH] = dot(probs, value).astype(BF16)


def mixer_backward(
    cut,
    proj_ref,
    step_ref,
    grad_ref,
    conv_ref,
    head_ref,
    chan_ref,
    cos_ref,
    sin_ref,
    d_ref,
    conv_sum_ref,
    head_sum_ref,
    chan_sum_ref,
    act_ref,
    d_act_ref,
    d_pair_ref,
    col_ref,
):
    length = proj_ref.shape[0]

    for lane in range(0, cut.conv, 2 * LANES):
        lanes = slice(lane, min(lane + 2 * LANES, cut.conv))
        total, _ = conv_out_of(proj_ref, lanes, cut.x + lane, conv_ref)
        act_ref[:, lanes] = total * sigmoid(total)
    raw, step, decay, running = steps_of(step_ref, head_ref)
    step_t, running_t = step.T, running.T
    in_map = act_ref[:, cut.inner : cut.inner + STATE].astype(BF16)
    out_map = act_ref[:, cut.inner + STATE : cut.inner + 2 * STATE].astype(BF16)
    pairing = dot_nt(out_map, in_map)
    d_pair_ref[...] = jnp.zeros_like(d_pair_ref)
    col_ref[...] = jnp.zeros_like(col_ref)
    first = lax.broadcasted_iota(jnp.int32, (ROWS, LANES), 1) < HDIM
    lane_of = lax.broadcasted_iota(jnp.int32, (ROWS, LANES), 1)
    row_sums = [jnp.zeros((ROWS, LANES), F32) for _ in range(length // ROWS)]
    for pair in range(cut.heads // 2):
        lanes = slice(pair * LANES, (pair + 1) * LANES)
        given_f = act_ref[:, lanes]
        given = given_f.astype(BF16)
        skip = chan_ref[0:1, lanes]
        skip_sum = jnp.zeros((1, LANES), F32)
        for block in range(length // ROWS):
            rows = slice(block * ROWS, (block + 1) * ROWS)
            width = rows.stop
            z_lanes = slice(cut.z + lanes.start, cut.z + lanes.stop)
            gate = proj_ref[rows, z_lanes].astype(F32)
            sig = sigmoid(gate)
            d_mixed = grad_ref[rows, lanes].astype(F32)
            d_ssm = d_mixed * gate * sig
            skip_sum = skip_sum + jnp.sum(d_ssm * given_f[rows], axis=0, keepdims=True)
            parts = []
            d_given = jnp.zeros((width, LANES), F32)
            for which in range(2):
                head = 2 * pair + which
                d_head = jnp.where(first if which == 0 else ~first, d_ssm, 0.0).astype(BF16)
                fall = decay_block(running, running_t, head, block)
                step_row = step_t[head : head + 1, :width]
                d_mixing = dot_nt(d_head, given[:width])
                stepped = fall * step_row
                mixing = pairing[rows, :width] * stepped
                mixing_low = mixing.astype(BF16)
                parts.append(dot(mixing_low, given[:width]))
                d_given = d_given + dot_tn(mixing_low, d_head)
                d_pair_ref[rows, :width] += d_mixing * stepped
                flow = d_mixing * mixing
                row_sums[block] = jnp.where(
                    lane_of == head,
                    jnp.sum(flow, axis=1, keepdims=True),
                    row_sums[block],
                )
                col_ref[head : head + 1, :width] += jnp.sum(
                    d_mixing * pairing[rows, :width] * fall, axis=0, keepdims=True
                )
            if block == 0:
                d_act_ref[:, lanes] = jnp.zeros((length, LANES), F32)
            d_act_ref[:width, lanes] += d_given
            d_act_ref[rows, lanes] += d_ssm * skip
            ssm = jnp.where(first, parts[0], parts[1]) + skip * given_f[rows]
            d_ref[rows, z_lanes] = (d_mixed * ssm * silu_slope(gate, sig)).astype(BF16)
        chan_sum_ref[0:1, lanes] += skip_sum
    d_pair = d_pair_ref[...].astype(BF16)
    d_act_ref[:, cut.inner : cut.inner + STATE] = dot_tn(d_pair, out_map)
    d_act_ref[:, cut.inner + STATE : cut.inner + 2 * STATE] = dot(d_pair, in_map)
    col_sum = col_ref[...].T
    d_running = jnp.concatenate(row_sums, axis=0) - step * col_sum
    d_decay = dot(ones_triangle(length, True), d_running, precision=HIGHEST)
    d_step = col_sum - d_decay * jnp.exp(head_ref[0:1, :])
    d_raw = d_step * sigmoid(raw)
    valid = lax.broadcasted_iota(jnp.int32, d_raw.shape, 1) < cut.heads
    d_raw = jnp.where(valid, d_raw, 0.0)
    d_ref[:, cut.step : cut.step + LANES] = d_raw.astype(BF16)
    head_sum_ref[0:1, :] += jnp.sum(d_decay * decay, axis=0, keepdims=True)
    head_sum_ref[1:2, :] += jnp.sum(d_raw, axis=0, keepdims=True)
    for lane in range(0, cut.conv, 2 * LANES):
        lanes = slice(lane, min(lane + 2 * LANES, cut.conv))
        total, given = conv_out_of(proj_ref, lanes, cut.x + lane, conv_ref)
        d_out = d_act_ref[:, lanes] * silu_slope(total, sigmoid(total))
        d_given = conv_back(d_out, given, conv_ref, lanes, conv_sum_ref)
        d_ref[:, cut.x + lane : cut.x + lanes.stop] = d_given.astype(BF16)
    key = turn(proj_ref[:, cut.k : cut.k + HEAD_WIDTH].astype(F32), cos_ref, sin_ref).astype(BF16)
    value = proj_ref[:, cut.v : cut.v + HEAD_WIDTH].astype(BF16)
    d_key = jnp.zeros((length, HEAD_WIDTH), F32)
    d_value = jnp.zeros((length, HEAD_WIDTH), F32)
    for head in range(cut.qheads):
        at = cut.q + head * HEAD_WIDTH
        query = turn(proj_ref[:, at : at + HEAD_WIDTH].astype(F32), cos_ref, sin_ref).astype(BF16)
        probs = softmax_rows(query, key)
        to = cut.inner + head * HEAD_WIDTH
        d_attended = grad_ref[:, to : to + HEAD_WIDTH].astype(BF16)
        d_probs = dot_nt(d_attended, value)
        inner = jnp.sum(probs * d_probs, axis=1, keepdims=True)
        d_scores = (probs * (d_probs - inner)).astype(BF16)
        d_query = dot(d_scores, key) * HEAD_WIDTH ** (-0.5)
        d_key = d_key + dot_tn(d_scores, query) * HEAD_WIDTH ** (-0.5)
        d_value = d_value + dot_tn(probs.astype(BF16), d_attended)
        d_ref[:, at : at + HEAD_WIDTH] = turn_back(d_query, cos_ref, sin_ref).astype(BF16)
    d_ref[:, cut.k : cut.k + HEAD_WIDTH] = turn_back(d_key, cos_ref, sin_ref).astype(BF16)
    d_ref[:, cut.v : cut.v + HEAD_WIDTH] = d_value.astype(BF16)


def spread(moves, places_ref, blocks_ref, *refs):
    for which in range(4):
        at = places_ref[which]
        for out, rows, lanes, row_by, lane_by, lane_from in moves:
            height, width = rows.stop - rows.start, lanes.stop - lanes.start
            row, lane = at * row_by, lane_from + at * lane_by
            if row_by:
                row = pl.multiple_of(row, row_by)
            if lane_by and lane_by % LANES == 0:
                lane = pl.multiple_of(lane, LANES)
            refs[out][pl.ds(row, height), pl.ds(lane, width)] = blocks_ref[
                which, rows, lanes
            ].astype(F32)


def spread_call(places, blocks, outs, moves):
    if any(move[4] % LANES for move in moves):
        return spread_plain(places, blocks, outs, moves)
    return pl.pallas_call(
        functools.partial(spread, moves),
        out_shape=[jax.ShapeDtypeStruct(shape, F32) for shape in outs],
        in_specs=[pl.BlockSpec(memory_space=pltpu.SMEM)]
        + [pl.BlockSpec(memory_space=pltpu.VMEM)],
        out_specs=[pl.BlockSpec(memory_space=pltpu.VMEM)] * len(outs),
        compiler_params=pltpu.CompilerParams(vmem_limit_bytes=40 * MIB),
        name="spread",
    )(places, blocks)


def spread_plain(places, blocks, outs, moves):
    result = [jnp.zeros(shape, F32) for shape in outs]
    for which in range(4):
        block, at = blocks[which], places[which]
        for out, rows, lanes, row_by, lane_by, lane_from in moves:
            result[out] = lax.dynamic_update_slice(
                result[out],
                block[rows, lanes].astype(F32),
                (at * row_by, lane_from + at * lane_by),
            )
    return result


def spread_in(cut, places_ref, *refs):
    blocks_ref, wide_ref, query_ref, key_ref, value_ref = refs
    key_ref[...] = jnp.zeros_like(key_ref)
    value_ref[...] = jnp.zeros_like(value_ref)
    split = cut.maps // 2
    first = split - cut.z
    maps = 2 * INNER
    for which in range(4):
        block = blocks_ref.at[which]
        at = places_ref[which]
        lanes = pl.ds(pl.multiple_of(at * cut.qwidth, LANES), cut.qwidth)
        query_ref[:, lanes] = block[: cut.qwidth].astype(F32).T
        to = pl.multiple_of(at * cut.inner, ROWS)
        wide_ref[pl.ds(to, first)] = block[cut.z : split].astype(F32)
        wide_ref[pl.ds(pl.multiple_of(to + first, 64), cut.inner - first)] = block[
            cut.way : cut.way + cut.inner - first
        ].astype(F32)
        wide_ref[pl.ds(INNER + to, cut.inner)] = block[
            cut.way + cut.inner - first : cut.way + split
        ].astype(F32)
    halves = [
        jnp.concatenate(
            [
                blocks_ref[which, split : cut.way].astype(F32),
                blocks_ref[which, cut.way + split :].astype(F32),
            ],
            axis=0,
        )
        for which in range(4)
    ]
    ones = [places_ref[which] % 2 for which in range(4)]
    low_half = sum(jnp.where(one == 0, half, 0.0) for one, half in zip(ones, halves))
    wide_ref[maps : maps + cut.shared] = low_half
    rest = 2 * STATE - cut.shared
    high = [jnp.where(one == 1, half, 0.0) for one, half in zip(ones, halves)]
    wide_ref[maps + cut.shared : maps + 2 * STATE] = sum(half[:rest] for half in high)
    for which, half in enumerate(high):
        lanes = pl.ds(
            pl.multiple_of(places_ref[which] * KVH // 4 * HEAD_WIDTH, LANES), HEAD_WIDTH
        )
        key_ref[:, lanes] += half[rest : rest + HEAD_WIDTH].T
        value_ref[:, lanes] += half[rest + HEAD_WIDTH :].T
    for rep in range(4):
        steps = sum(
            jnp.where(places_ref[which] == rep, 1.0, 0.0)
            * blocks_ref[which, cut.step : cut.step + LANES].astype(F32)
            for which in range(4)
        )
        to = maps + 2 * STATE + rep * cut.heads
        wide_ref[to : to + cut.heads] = steps[: cut.heads]


def spread_in_call(cut, places, blocks):
    depth = blocks.shape[2]
    vmem = pl.BlockSpec(memory_space=pltpu.VMEM)
    columns_in = 2 * INNER + 2 * STATE + HEADS
    return pl.pallas_call(
        functools.partial(spread_in, cut),
        out_shape=[
            jax.ShapeDtypeStruct((columns_in, depth), F32),
            jax.ShapeDtypeStruct((depth, QH * HEAD_WIDTH), F32),
            jax.ShapeDtypeStruct((depth, KVH * HEAD_WIDTH), F32),
            jax.ShapeDtypeStruct((depth, KVH * HEAD_WIDTH), F32),
        ],
        in_specs=[pl.BlockSpec(memory_space=pltpu.SMEM), vmem],
        out_specs=[vmem] * 4,
        compiler_params=pltpu.CompilerParams(vmem_limit_bytes=40 * MIB),
        name="spread_in",
    )(places, blocks)


def turn_tables(length):
    half = HEAD_WIDTH // 2
    position = jnp.arange(length).astype(F32)
    freqs = 10000.0 ** (-jnp.arange(half).astype(F32) * 2.0 / HEAD_WIDTH)
    angles = position[:, None] * freqs[None, :]
    cosine, sine = jnp.cos(angles), jnp.sin(angles)
    return (
        jnp.concatenate([cosine, cosine], axis=1),
        jnp.concatenate([-sine, sine], axis=1),
    )


class Ring:
    def __init__(self, shards):
        self.shards = shards
        self.index = lax.axis_index("fsdp")
        self.place = ring_place(self.index, shards)

    def at(self, offset):
        return ring_at(self.place + offset, self.shards)

    def peer(self, way):
        return {"fsdp": self.at(1 - 2 * way)}


class Pair:
    def __init__(self):
        self.rep = lax.axis_index("rep")
        across, core = self.rep // 2, self.rep % 2
        self.peers = ({"rep": (1 - across) * 2 + core}, {"rep": across * 2 + 1 - core})
        self.corner = {"rep": (1 - across) * 2 + 1 - core}


def greet(ring, pair, *more, maybe=(), are=None):
    barrier = pltpu.get_barrier_semaphore()

    def signal(peers):
        for peer in peers:
            pl.semaphore_signal(barrier, inc=1, device_id=peer, device_id_type=MESH)

    peers = (ring.peer(0), ring.peer(1)) + pair.peers + more
    signal(peers)
    if not maybe:
        pl.semaphore_wait(barrier, len(peers))
        return
    pl.when(are == 1)(lambda: signal(maybe))
    pl.semaphore_wait(barrier, len(peers) + len(maybe) * are)


class Gather:
    def __init__(self, ring, ways, send, recv, hook=None):
        self.ring, self.ways, self.send, self.recv = ring, ways, send, recv
        self.hook = hook or (lambda step, way, piece: None)

    def pieces(self):
        for piece in range(max(len(way) for way in self.ways)):
            for way in range(2):
                if piece < len(self.ways[way]):
                    yield way, piece

    def copy(self, step, way, piece, first=False):
        own, place = self.ways[way][piece]
        there = place(self.ring.at((2 * way - 1) * (step - 1)))
        return pltpu.make_async_remote_copy(
            src_ref=own if first else there,
            dst_ref=there,
            send_sem=self.send.at[step - 1, way, piece],
            recv_sem=self.recv.at[step - 1, way, piece],
            device_id=self.ring.peer(way),
            device_id_type=MESH,
        )

    def landed(self, step, way, piece):
        here = self.ways[way][piece][1](self.ring.at((2 * way - 1) * step))
        return pltpu.make_async_remote_copy(
            src_ref=here,
            dst_ref=here,
            send_sem=self.send.at[step - 1, way, piece],
            recv_sem=self.recv.at[step - 1, way, piece],
            device_id=self.ring.peer(way),
            device_id_type=MESH,
        )

    def start(self):
        for way, piece in self.pieces():
            self.copy(1, way, piece, True).start()

    def advance(self, step):
        for way, piece in self.pieces():
            self.landed(step - 1, way, piece).wait_recv()
            self.copy(step, way, piece).start()
            self.hook(step - 1, way, piece)

    def run(self, first, stop):
        def body(step, carry):
            self.advance(step)
            return carry

        lax.fori_loop(first, stop, body, 0)

    def finish(self):
        for way, piece in self.pieces():
            self.landed(self.ring.shards - 1, way, piece).wait_recv()
            self.hook(self.ring.shards - 1, way, piece)
            self.copy(1, way, piece, True).wait_send()

        def body(step, carry):
            for way, piece in self.pieces():
                self.copy(step, way, piece).wait_send()
            return carry

        lax.fori_loop(2, self.ring.shards, body, 0)


def ring_sems(shards, pieces):
    return [pltpu.SemaphoreType.DMA((shards - 1, 2, pieces))] * 2


def remote(src, dst, send, recv, peer):
    return pltpu.make_async_remote_copy(
        src_ref=src, dst_ref=dst, send_sem=send, recv_sem=recv, device_id=peer, device_id_type=MESH
    )


def block_at(ref, index, rows, lanes):
    if len(ref.shape) == 2:
        return ref.at[rows, pl.ds(pl.multiple_of(index * lanes, LANES), lanes)]
    return ref.at[index, rows]


def gather_in(shards, cut, *refs):
    refs = list(refs)
    take = lambda number: [refs.pop(0) for _ in range(number)]
    in_ref, query_ref, key_ref, value_ref, aux_ref, tokens_ref, cot_ref, live_ref = take(8)
    w_ref, aux_all_ref, branch_all_ref, tokens_all_ref = take(4)
    share_ref, turn_ref, rows_ref, branch_ref = take(4)
    pack_sem, send, recv, core_send, core_recv = take(5)
    token_sems, branch_sems = take(3), take(3)

    ring, pair = Ring(shards), Pair()
    rep, core = pair.rep, pair.rep % 2
    depth = in_ref.shape[1]
    copies = (
        (
            in_ref.at[pl.ds(pl.multiple_of(cut.inner * rep, ROWS), cut.inner)],
            share_ref.at[pl.ds(cut.z, cut.inner)],
        ),
        (
            in_ref.at[pl.ds(pl.multiple_of(INNER + cut.inner * rep, ROWS), cut.inner)],
            share_ref.at[pl.ds(cut.x, cut.inner)],
        ),
        (
            in_ref.at[pl.ds(2 * INNER, 2 * STATE)],
            share_ref.at[pl.ds(cut.maps, 2 * STATE)],
        ),
        (in_ref.at[pl.ds(2 * INNER + 2 * STATE, HEADS)], rows_ref),
        (
            query_ref.at[:, pl.ds(pl.multiple_of(cut.qwidth * rep, LANES), cut.qwidth)],
            turn_ref.at[:, pl.ds(0, cut.qwidth)],
        ),
    ) + tuple(
        (
            ref.at[:, pl.ds(pl.multiple_of(rep * KVH // 4 * HEAD_WIDTH, LANES), HEAD_WIDTH)],
            turn_ref.at[:, pl.ds(cut.qwidth + number * HEAD_WIDTH, HEAD_WIDTH)],
        )
        for number, ref in enumerate((key_ref, value_ref))
    )
    packs = [
        pltpu.make_async_copy(src, dst, pack_sem.at[number])
        for number, (src, dst) in enumerate(copies)
    ]
    for pack in packs:
        pack.start()
    greet(ring, pair)
    branch_ref[...] = (cot_ref[...].astype(F32) * live_ref[:, 0:1]).astype(BF16)
    for pack in packs:
        pack.wait()
    share_ref[: cut.qwidth] = turn_ref[:, : cut.qwidth].T
    share_ref[cut.k :] = turn_ref[:, cut.qwidth :].T
    row = lax.broadcasted_iota(jnp.int32, (LANES, HEADS), 0)
    column = lax.broadcasted_iota(jnp.int32, (LANES, HEADS), 1)
    chosen = jnp.logical_and(column == row + cut.heads * rep, row < cut.heads)
    chosen = jnp.where(chosen, 1.0, 0.0).astype(BF16)
    share_ref[cut.step : cut.z] = dot(chosen, rows_ref[...]).astype(BF16)
    every = pl.ds(0, cut.width)
    keeps = [
        pltpu.make_async_copy(src, dst, pack_sem.at[len(packs) + number])
        for number, (src, dst) in enumerate(
            (
                (share_ref, block_at(w_ref, ring.index, every, depth)),
                (aux_ref, aux_all_ref.at[ring.index]),
            )
        )
    ]
    quarter = cut.maps // 4
    half = cut.shared // 2
    rows = lambda number: pl.ds(number * quarter, quarter)

    def shared(which, way):
        return pl.ds(pl.multiple_of(cut.maps + which * cut.shared + way * half, 16), half)

    def piece(rows):
        return share_ref.at[rows], lambda index: block_at(w_ref, index, rows, depth)

    ways = (
        [
            piece(rows(0)),
            piece(rows(1)),
            piece(shared(core, 0)),
            (aux_ref, lambda index: aux_all_ref.at[index]),
        ],
        [piece(rows(2)), piece(rows(3)), piece(shared(core, 1))],
    )

    def over_core(step, way, which):
        here = block_at(w_ref, ring.at((2 * way - 1) * step), shared(which, way), depth)
        return remote(
            here, here, core_send.at[step - 1, way], core_recv.at[step - 1, way], pair.peers[1]
        )

    def hook(step, way, piece):
        if piece == 2:
            over_core(step, way, core).start()

    gather = Gather(ring, ways, send, recv, hook)
    gather.start()
    tokens = Share(pair, 1, tokens_ref, tokens_all_ref, token_sems)
    branch = Share(pair, 1, branch_ref, branch_all_ref, branch_sems)
    tokens.start(0)
    branch.start(0)
    for keep in keeps:
        keep.start()
    gather.run(2, 4)
    tokens.pass_on(0)
    gather.advance(4)
    branch.pass_on(0)
    gather.run(5, shards)
    gather.finish()
    tokens.finish()
    branch.finish()
    for keep in keeps:
        keep.wait()

    def rest(step, carry):
        for way in range(2):
            over_core(step, way, 1 - core).wait_recv()
            over_core(step, way, core).wait_send()
        return carry

    lax.fori_loop(1, shards, rest, 0)


def share_sems(chunks):
    return [
        pltpu.SemaphoreType.DMA((3, chunks)),
        pltpu.SemaphoreType.DMA((3, chunks)),
        pltpu.SemaphoreType.DMA((chunks,)),
    ]


def gather_in_call(shards, cut, in_t, query, key, value, aux, tokens, cot, live):
    depth = in_t.shape[1]
    length, width = tokens.shape
    hbm = pl.BlockSpec(memory_space=pl.ANY)
    vmem = pl.BlockSpec(memory_space=pltpu.VMEM)
    out_shape = [
        jax.ShapeDtypeStruct((shards,) + aux.shape, BF16),
        jax.ShapeDtypeStruct((4, length, width), BF16),
    ]
    scratch = [
        pltpu.VMEM((cut.width, depth), BF16),
        pltpu.VMEM((depth, cut.qwidth + 2 * HEAD_WIDTH), BF16),
        pltpu.VMEM((HEADS, depth), BF16),
        pltpu.VMEM((length, width), BF16),
        pltpu.SemaphoreType.DMA((9,)),
        *ring_sems(shards, 4),
        pltpu.SemaphoreType.DMA((shards - 1, 2)),
        pltpu.SemaphoreType.DMA((shards - 1, 2)),
        *share_sems(1),
        *share_sems(1),
    ]
    if depth % LANES:
        w_shape = (shards, cut.width, depth)
    else:
        w_shape = (cut.width, width)
    return pl.pallas_call(
        functools.partial(gather_in, shards, cut),
        out_shape=[
            jax.ShapeDtypeStruct(w_shape, BF16),
            *out_shape,
            jax.ShapeDtypeStruct((4, length, width), BF16),
        ],
        in_specs=[hbm] * 6 + [vmem] * 2,
        out_specs=[hbm] * 4,
        scratch_shapes=scratch,
        compiler_params=pltpu.CompilerParams(
            collective_id=0, has_side_effects=True, vmem_limit_bytes=40 * MIB
        ),
        name="gather_in",
    )(in_t, query, key, value, aux, tokens, cot, live)


def gather_rows(
    shards,
    cut,
    length,
    heads_ref,
    down_ref,
    w_ref,
    tokens_ref,
    gain_ref,
    conv_ref,
    head_ref,
    chan_ref,
    cos_ref,
    sin_ref,
    heads_all_ref,
    down_all_ref,
    out_ref,
    normed_ref,
    proj_ref,
    step_ref,
    act_ref,
    pack_sem,
    send,
    recv,
):
    ring, pair = Ring(shards), Pair()
    half = down_ref.shape[0] // 2
    rows = lambda number: pl.ds(number * half, half)
    down_way = [
        (
            down_ref.at[rows(number)],
            lambda index, number=number: down_all_ref.at[index, rows(number)],
        )
        for number in range(2)
    ]
    if len(heads_all_ref.shape) == 2:
        mamba = cut.inner // shards
        attn = heads_ref.shape[0] - mamba

        def mamba_place(index):
            return heads_all_ref.at[pl.ds(pl.multiple_of(index * mamba, 16), mamba)]

        def attn_place(index):
            start = pl.multiple_of(cut.inner + index * attn, 16)
            return heads_all_ref.at[pl.ds(start, attn)]

        heads_way = [
            (heads_ref.at[pl.ds(0, mamba)], mamba_place),
            (heads_ref.at[pl.ds(mamba, attn)], attn_place),
        ]
    else:
        heads_way = [
            (
                heads_ref.at[rows(number)],
                lambda index, number=number: heads_all_ref.at[index, rows(number)],
            )
            for number in range(2)
        ]
    ways = (heads_way, down_way)
    packs = [
        pltpu.make_async_copy(own, place(ring.index), pack_sem.at[2 * way + number])
        for way in range(2)
        for number, (own, place) in enumerate(ways[way])
    ]
    for pack in packs:
        pack.start()
    greet(ring, pair)
    gather = Gather(ring, ways, send, recv)
    gather.start()
    count = proj_ref.shape[0] // length
    wide = cut.width // 7

    def norm(number, carry):
        rows = pl.ds(pl.multiple_of(number * length, length), length)
        values = tokens_ref[number].astype(F32)
        normed_ref[rows] = (values * norm_scale(values) * gain_ref[0:1]).astype(BF16)
        return carry

    def project(tile, carry):
        out = pl.ds(pl.multiple_of(tile * wide, LANES), wide)
        proj_ref[:, out] = dot_nt(normed_ref[...], w_ref[out]).astype(BF16)
        return carry

    lax.fori_loop(0, count, norm, 0)
    first = dot_nt(normed_ref[...], w_ref[:wide])
    proj_ref[:, :wide] = first.astype(BF16)
    step_ref[...] = first[:, cut.step : cut.step + LANES]
    lax.fori_loop(1, 4, project, 0)
    gather.advance(2)
    lax.fori_loop(4, 7, project, 0)
    gather.advance(3)

    def body(number, carry):
        rows = pl.ds(pl.multiple_of(number * length, length), length)
        mixer_forward(
            cut,
            proj_ref.at[rows],
            step_ref.at[rows],
            conv_ref,
            head_ref,
            chan_ref,
            cos_ref,
            sin_ref,
            out_ref.at[rows],
            act_ref,
        )
        gather.advance(number + 4)
        return carry

    lax.fori_loop(0, count, body, 0)
    gather.run(count + 4, shards)
    gather.finish()
    for pack in packs:
        pack.wait()


def gather_rows_call(
    shards, cut, length, ordered, heads, down, w, tokens, gain, conv, head, chan, cosine, sine
):
    rows = 4 * length
    tall, width = heads.shape
    hbm = pl.BlockSpec(memory_space=pl.ANY)
    vmem = pl.BlockSpec(memory_space=pltpu.VMEM)
    return pl.pallas_call(
        functools.partial(gather_rows, shards, cut, length),
        out_shape=[
            jax.ShapeDtypeStruct(
                (shards * tall, width) if ordered else (shards, tall, width), BF16
            ),
            jax.ShapeDtypeStruct((shards,) + down.shape, BF16),
            jax.ShapeDtypeStruct((rows, cut.inner + cut.qwidth), BF16),
            jax.ShapeDtypeStruct((rows, width), BF16),
            jax.ShapeDtypeStruct((rows, cut.width), BF16),
            jax.ShapeDtypeStruct((rows, LANES), F32),
        ],
        in_specs=[vmem] * 10,
        out_specs=[hbm] * 2 + [vmem] * 4,
        scratch_shapes=[
            pltpu.VMEM((length, cut.conv), F32),
            pltpu.SemaphoreType.DMA((4,)),
        ]
        + ring_sems(shards, 2),
        compiler_params=pltpu.CompilerParams(
            collective_id=1, has_side_effects=True, vmem_limit_bytes=48 * MIB
        ),
        name="gather_rows",
    )(heads, down, w, tokens, gain, conv, head, chan, cosine, sine)


class Exchange:
    def __init__(self, pair, chunks, part_ref, core_ref, cross_ref, came_ref, sems):
        self.pair, self.chunks = pair, chunks
        self.part, self.core, self.cross, self.came = part_ref, core_ref, cross_ref, came_ref
        self.send, self.recv = sems
        self.tall = part_ref.shape[1] // chunks

    def rows(self, chunk):
        return pl.ds(chunk * self.tall, self.tall)

    def over_core(self, chunk, which):
        return remote(
            self.part.at[2 + which, self.rows(chunk)],
            self.core.at[which, self.rows(chunk)],
            self.send.at[0, which, chunk],
            self.recv.at[0, which, chunk],
            self.pair.peers[1],
        )

    def over_x(self, chunk):
        return remote(
            self.cross.at[self.rows(chunk)],
            self.came.at[self.rows(chunk)],
            self.send.at[1, 0, chunk],
            self.recv.at[1, 0, chunk],
            self.pair.peers[0],
        )

    def start_one(self, which):
        for chunk in range(self.chunks):
            self.over_core(chunk, which).start()

    def start(self):
        self.start_one(1)
        self.start_one(0)

    def middle(self, chunk):
        self.over_core(chunk, 1).wait_recv()
        rows = self.rows(chunk)
        total = self.part[1, rows].astype(F32) + self.core[1, rows].astype(F32)
        self.cross[rows] = total.astype(BF16)
        self.over_x(chunk).start()

    def sum(self, chunk):
        self.over_core(chunk, 0).wait_recv()
        self.over_x(chunk).wait_recv()
        rows = self.rows(chunk)
        return (
            self.part[0, rows].astype(F32)
            + self.core[0, rows].astype(F32)
            + self.came[rows].astype(F32)
        )

    def finish(self):
        for chunk in range(self.chunks):
            for which in range(2):
                self.over_core(chunk, which).wait_send()
            self.over_x(chunk).wait_send()


class Share:
    def __init__(self, pair, chunks, own_ref, all_ref, sems):
        self.pair, self.chunks, self.own, self.all = pair, chunks, own_ref, all_ref
        self.send, self.recv, self.local = sems
        self.tall = own_ref.shape[0] // chunks

    def rows(self, chunk):
        return pl.ds(chunk * self.tall, self.tall)

    def direct(self, chunk, which):
        return remote(
            self.own.at[self.rows(chunk)],
            self.all.at[1 + which, self.rows(chunk)],
            self.send.at[which, chunk],
            self.recv.at[which, chunk],
            self.pair.peers[which],
        )

    def onward(self, chunk):
        return remote(
            self.all.at[1, self.rows(chunk)],
            self.all.at[3, self.rows(chunk)],
            self.send.at[2, chunk],
            self.recv.at[2, chunk],
            self.pair.peers[1],
        )

    def keep(self, chunk):
        return pltpu.make_async_copy(
            self.own.at[self.rows(chunk)], self.all.at[0, self.rows(chunk)], self.local.at[chunk]
        )

    def start(self, chunk):
        self.direct(chunk, 0).start()
        self.direct(chunk, 1).start()
        self.keep(chunk).start()

    def pass_on(self, chunk):
        self.direct(chunk, 0).wait_recv()
        self.onward(chunk).start()

    def finish(self):
        for chunk in range(self.chunks):
            self.direct(chunk, 0).wait_send()
            self.direct(chunk, 1).wait()
            self.onward(chunk).wait()
            self.keep(chunk).wait()


CHUNKS = 2


def exchange_scratch(length, width):
    return [
        pltpu.VMEM((2, length, width), BF16),
        pltpu.VMEM((length, width), BF16),
        pltpu.VMEM((length, width), BF16),
        pltpu.SemaphoreType.DMA((2, 2, CHUNKS)),
        pltpu.SemaphoreType.DMA((2, 2, CHUNKS)),
    ]


class Scatter:
    def __init__(
        self, ring, pieces, term, first_ref, slots_ref, send, recv, groups=1, made_ref=None
    ):
        self.made = made_ref
        self.ring, self.pieces, self.groups, self.term = ring, pieces, groups, term
        self.first, self.slots, self.send, self.recv = first_ref, slots_ref, send, recv
        self.half = slots_ref.shape[2]
        self.tall = self.half // pieces

    def each(self, group):
        size = self.pieces // self.groups
        for piece in range(group * size, (group + 1) * size):
            for way in range(2):
                yield way, piece

    def rows(self, way, piece):
        return pl.ds(way * self.half + piece * self.tall, self.tall)

    def local(self, piece):
        return pl.ds(piece * self.tall, self.tall)

    def due(self, step, way, piece):
        if self.made is not None:
            at = piece % (self.pieces // self.groups) * self.tall
            return self.made[way, at : at + self.tall]
        return self.term(self.ring.at((2 * way - 1) * step), self.rows(way, piece))

    def copy(self, step, way, piece, first=False):
        src = self.first.at[way] if first else self.slots.at[step - 2, way]
        return remote(
            src.at[self.local(piece)],
            self.slots.at[step - 1, way, self.local(piece)],
            self.send.at[step - 1, way, piece],
            self.recv.at[step - 1, way, piece],
            self.ring.peer(way),
        )

    def landed(self, step, way, piece):
        here = self.slots.at[step - 1, way, self.local(piece)]
        return remote(
            here,
            here,
            self.send.at[step - 1, way, piece],
            self.recv.at[step - 1, way, piece],
            self.ring.peer(way),
        )

    def make(self, step, group):
        if self.made is None:
            return
        tall = self.half // self.groups
        for way in range(2):
            index = self.ring.at((2 * way - 1) * step)
            self.made[way] = self.term(index, pl.ds(way * self.half + group * tall, tall))

    def start(self, group=0):
        self.make(1, group)
        for way, piece in self.each(group):
            self.first[way, self.local(piece)] = self.due(1, way, piece).astype(BF16)
            self.copy(1, way, piece, True).start()

    def total(self, step, way, piece):
        term = self.due(step, way, piece)
        self.landed(step - 1, way, piece).wait_recv()
        return self.slots[step - 2, way, self.local(piece)].astype(F32) + term

    def advance(self, step, group=0):
        self.make(step, group)
        for way, piece in self.each(group):
            total = self.total(step, way, piece)
            self.slots[step - 2, way, self.local(piece)] = total.astype(BF16)
            self.copy(step, way, piece).start()

    def run(self, first, stop, group=0):
        def body(step, carry):
            self.advance(step, group)
            return carry

        lax.fori_loop(first, stop, body, 0)

    def result(self, own_ref, share=None, group=0):
        self.make(self.ring.shards, group)
        for way, piece in self.each(group):
            total = self.total(self.ring.shards, way, piece)
            own_ref[self.rows(way, piece)] = total.astype(BF16)
            if share is not None:
                share.start(way * self.pieces + piece)

    def chunks(self, group):
        return [way * self.pieces + piece for way, piece in self.each(group)]

    def finish(self):
        for group in range(self.groups):
            for way, piece in self.each(group):
                self.copy(1, way, piece, True).wait_send()

        def body(step, carry):
            for group in range(self.groups):
                for way, piece in self.each(group):
                    self.copy(step, way, piece).wait_send()
            return carry

        lax.fori_loop(2, self.ring.shards, body, 0)


def stored(ref):
    return lambda index, rows: ref[index, rows].astype(F32)


def pieces_of(rows):
    return 2 if rows // 2 % 32 == 0 else 1


def scatter_scratch(shards, rows, width, pieces=None):
    return [
        pltpu.VMEM((2, rows // 2, width), BF16),
        pltpu.VMEM((shards - 1, 2, rows // 2, width), BF16),
    ] + ring_sems(shards, pieces or pieces_of(rows))


def share_scratch(rows, width, chunks):
    return [
        pltpu.VMEM((rows, width), BF16),
        pltpu.SemaphoreType.DMA((3, chunks)),
        pltpu.SemaphoreType.DMA((3, chunks)),
        pltpu.SemaphoreType.DMA((chunks,)),
    ]


def gather_mlp(shards, inside, count, *refs):
    refs = list(refs)
    take = lambda number: [refs.pop(0) for _ in range(number)]
    source_refs = take(count)
    heads_ref, w_out_ref, tokens_ref, live_ref, gain_ref = take(5)
    all_ref, normed_ref, mixed_ref = take(3)
    if inside:
        (sum_ref,) = take(1)
    core_ref, cross_ref, came_ref, ex_send, ex_recv = take(5)
    own_ref, sh_send, sh_recv, sh_local = take(4)
    part_ref, share_ref, pack_sem, send, recv = take(5)

    ring, pair = Ring(shards), Pair()
    depth, wide = share_ref.shape
    if count == 1:
        packs = [pltpu.make_async_copy(source_refs[0], share_ref, pack_sem.at[0])]
    else:
        units = wide // (2 * shards)
        packs = [
            pltpu.make_async_copy(
                ref.at[:, pl.ds(pl.multiple_of((shard * 4 + pair.rep) * units, LANES), units)],
                share_ref.at[:, pl.ds((which * shards + shard) * units, units)],
                pack_sem.at[which * shards + shard],
            )
            for which, ref in enumerate(source_refs)
            for shard in range(shards)
        ]
    for pack in packs:
        pack.start()
    greet(ring, pair)
    for pack in packs:
        pack.wait()
    keep = pltpu.make_async_copy(share_ref, all_ref.at[ring.index], pack_sem.at[0])
    keep.start()
    quarter = depth // 4
    rows = lambda number: pl.ds(number * quarter, quarter)
    piece = lambda number: (
        share_ref.at[rows(number)],
        lambda index: all_ref.at[index, rows(number)],
    )
    gather = Gather(ring, ([piece(0), piece(1)], [piece(2), piece(3)]), send, recv)
    exchange = Exchange(
        pair, CHUNKS, part_ref, core_ref, cross_ref, came_ref, (ex_send, ex_recv)
    )
    share = Share(pair, CHUNKS, own_ref, normed_ref, (sh_send, sh_recv, sh_local))
    length = part_ref.shape[1]

    def partial(number):
        left = heads_ref[pl.ds(number * length, length)]
        for lane in range(0, part_ref.shape[2], WIDE):
            lanes = slice(lane, lane + WIDE)
            part_ref[number, :, lanes] = dot(left, w_out_ref[:, lanes]).astype(BF16)

    def middle(chunk):
        rows = exchange.rows(chunk)
        branch = exchange.sum(chunk)
        mixed = tokens_ref[rows].astype(F32) + live_ref[rows, 0:1] * branch
        mixed_ref[rows] = mixed
        own_ref[rows] = (mixed * norm_scale(mixed) * gain_ref[0:1]).astype(BF16)
        share.start(chunk)

    def add(offsets, fresh=False):
        if not inside:
            return
        blocks = [ring.at(offset) for offset in offsets]

        def body(tile, carry):
            lanes = pl.ds(pl.multiple_of(tile * WIDE, LANES), WIDE)
            left = jnp.concatenate(
                [
                    normed_ref[
                        :, :, pl.ds(pl.multiple_of(index * depth, LANES), depth)
                    ].reshape(4 * length, depth)
                    for index in blocks
                ],
                axis=1,
            )
            right = jnp.concatenate([all_ref[index, :, lanes] for index in blocks], axis=0)
            term = dot(left, right)
            sum_ref[:, lanes] = term if fresh else sum_ref[:, lanes] + term
            return carry

        lax.fori_loop(0, wide // WIDE, body, 0)

    gather.start()
    for number in (3, 2, 1, 0):
        partial(number)
        if number > 1:
            exchange.start_one(number - 2)
    exchange.middle(0)
    exchange.middle(1)
    gather.advance(2)
    middle(0)
    gather.advance(3)
    middle(1)
    gather.advance(4)
    share.pass_on(0)
    gather.advance(5)
    share.pass_on(1)
    gather.advance(6)
    share.finish()
    keep.wait()
    half_way = shards // 2
    if half_way < 6:
        add((0, half_way), True)
    gather.run(7, shards)
    if half_way >= 6:
        add((0, half_way), True)
    if inside:

        def body(far, carry):
            add((far, -far))
            return carry

        lax.fori_loop(2, half_way, body, 0)
    gather.finish()
    add((1, -1))
    exchange.finish()


def gather_mlp_call(shards, inside, sources, wide, heads, w_out, tokens, live, gain):
    length, width = tokens.shape
    depth = sources[0].shape[0]
    hbm = pl.BlockSpec(memory_space=pl.ANY)
    vmem = pl.BlockSpec(memory_space=pltpu.VMEM)
    rows = heads.shape[0]
    return pl.pallas_call(
        functools.partial(gather_mlp, shards, inside, len(sources)),
        out_shape=[
            jax.ShapeDtypeStruct((shards, depth, wide), BF16),
            jax.ShapeDtypeStruct((4, length, width), BF16),
            jax.ShapeDtypeStruct((length, width), F32),
        ]
        + [jax.ShapeDtypeStruct((rows, wide), F32)] * inside,
        in_specs=[hbm] * len(sources) + [vmem] * 5,
        out_specs=[vmem] * (3 + inside),
        scratch_shapes=exchange_scratch(length, width)
        + share_scratch(length, width, CHUNKS)
        + [
            pltpu.VMEM((4, length, width), BF16),
            pltpu.VMEM((depth, wide), BF16),
            pltpu.SemaphoreType.DMA((2 * shards,)),
        ]
        + ring_sems(shards, 2),
        compiler_params=pltpu.CompilerParams(
            collective_id=2, has_side_effects=True, vmem_limit_bytes=56 * MIB
        ),
        name="gather_mlp",
    )(*sources, heads, w_out, tokens, live, gain)


TILE = 256
WIDE = 512


def product_tn(left_ref, right_ref, out_ref, number):
    rows = pl.ds(pl.multiple_of(number * TILE, TILE), TILE)
    left = left_ref[:, rows].T
    for lane in range(0, out_ref.shape[1], WIDE):
        lanes = slice(lane, lane + WIDE)
        out_ref[rows, lanes] = dot(left, right_ref[:, lanes]).astype(out_ref.dtype)


def product(left_ref, right_ref, out_ref, number):
    rows = pl.ds(pl.multiple_of(number * TILE, TILE), TILE)
    for lane in range(0, out_ref.shape[1], WIDE):
        lanes = slice(lane, lane + WIDE)
        out_ref[rows, lanes] = dot(left_ref[rows], right_ref[:, lanes]).astype(out_ref.dtype)


def mlp_back(gate_up_ref, branch_ref, w_down_ref, w_mlp_ref, active_ref, d_ref, part_ref):
    half = active_ref.shape[1]
    for lane in range(0, half, WIDE):
        gates, ups = slice(lane, lane + WIDE), slice(half + lane, half + lane + WIDE)
        d_active = dot_nt(branch_ref[...], w_down_ref[gates])
        gate, up = gate_up_ref[:, gates], gate_up_ref[:, ups]
        sig = sigmoid(gate)
        active = gate * sig
        active_ref[:, gates] = (active * up).astype(BF16)
        d_ref[:, gates] = (d_active * up * silu_slope(gate, sig)).astype(BF16)
        d_ref[:, ups] = (d_active * active).astype(BF16)
    for lane in range(0, part_ref.shape[1], WIDE):
        lanes = slice(lane, lane + WIDE)
        part_ref[:, lanes] = dot_nt(d_ref[...], w_mlp_ref[lanes]).astype(BF16)


def mlp_back_call(gate_up, branch, w_down, w_mlp):
    rows, wide = gate_up.shape
    half, width = w_down.shape
    tall = 2 * TILE
    tile = lambda lanes: pl.BlockSpec((tall, lanes), lambda i: (i, 0))
    whole = lambda shape: pl.BlockSpec(shape, lambda i: (0, 0))
    return pl.pallas_call(
        mlp_back,
        grid=(rows // tall,),
        out_shape=[
            jax.ShapeDtypeStruct((rows, half), BF16),
            jax.ShapeDtypeStruct((rows, wide), BF16),
            jax.ShapeDtypeStruct((rows, width), BF16),
        ],
        in_specs=[tile(wide), tile(width), whole(w_down.shape), whole(w_mlp.shape)],
        out_specs=[tile(half), tile(wide), tile(width)],
        compiler_params=pltpu.CompilerParams(vmem_limit_bytes=56 * MIB),
        name="mlp_back",
    )(gate_up, branch, w_down, w_mlp)


def scatter_down(
    shards,
    part_ref,
    branch_two_ref,
    normed_ref,
    d_mlp_ref,
    active_ref,
    w_down_ref,
    mixed_ref,
    cot_ref,
    live_ref,
    gain_ref,
    branch_ref,
    down_own_ref,
    mlp_ref,
    ffn_ref,
    d_mixed_ref,
    gain_sum_ref,
    core_ref,
    cross_ref,
    came_ref,
    ex_send,
    ex_recv,
    own_ref,
    sh_send,
    sh_recv,
    sh_local,
    first_ref,
    slots_ref,
    send,
    recv,
    down_ref,
):
    ring, pair = Ring(shards), Pair()
    greet(ring, pair)
    units = slots_ref.shape[2] * 2

    def down_term(index, rows):
        start = pl.multiple_of(index * units + rows.start, 16)
        return down_ref[pl.ds(start, rows.size)].astype(F32)

    scatter = Scatter(ring, pieces_of(units), down_term, first_ref, slots_ref, send, recv)
    exchange = Exchange(
        pair, CHUNKS, part_ref, core_ref, cross_ref, came_ref, (ex_send, ex_recv)
    )
    share = Share(pair, CHUNKS, own_ref, branch_ref, (sh_send, sh_recv, sh_local))
    gain_sum_ref[...] = jnp.zeros_like(gain_sum_ref)

    def middle(chunk):
        rows = exchange.rows(chunk)
        grad = exchange.sum(chunk)
        values = mixed_ref[rows]
        d_values, gain_sum = norm_back(values, norm_scale(values), gain_ref[0:1], grad)
        gain_sum_ref[0:1] += gain_sum
        d_mixed = cot_ref[rows].astype(F32) + d_values
        d_mixed_ref[rows] = d_mixed
        own_ref[rows] = (live_ref[rows, 0:1] * d_mixed).astype(BF16)
        share.start(chunk)

    def work(first, stop):
        def body(number, carry):
            product_tn(normed_ref, d_mlp_ref, mlp_ref, number)
            return carry

        lax.fori_loop(first, stop, body, 0)

    tiles = mlp_ref.shape[0] // TILE
    exchange.start()

    def down(number, carry):
        product_tn(active_ref, branch_two_ref, down_ref, number)
        return carry

    lax.fori_loop(0, down_ref.shape[0] // TILE, down, 0)
    scatter.start()
    exchange.middle(0)
    exchange.middle(1)
    scatter.advance(2)
    work(0, 3)
    scatter.advance(3)
    work(3, 5)
    middle(0)
    scatter.advance(4)
    work(5, 6)
    scatter.advance(5)
    middle(1)
    scatter.advance(6)
    work(6, tiles)
    scatter.run(7, shards)

    def rest(number, carry):
        product(active_ref, w_down_ref, ffn_ref, number)
        return carry

    lax.fori_loop(0, ffn_ref.shape[0] // TILE, rest, 0)
    scatter.result(down_own_ref)
    share.pass_on(0)
    share.pass_on(1)
    scatter.finish()
    exchange.finish()
    share.finish()


def scatter_down_call(
    shards, part, branch_two, normed, d_mlp, active, w_down, mixed, cot, live, gain
):
    length, width = mixed.shape
    hbm = pl.BlockSpec(memory_space=pl.ANY)
    vmem = pl.BlockSpec(memory_space=pltpu.VMEM)
    units = active.shape[1] // shards
    return pl.pallas_call(
        functools.partial(scatter_down, shards),
        out_shape=[
            jax.ShapeDtypeStruct((4, length, width), BF16),
            jax.ShapeDtypeStruct((units, width), BF16),
            jax.ShapeDtypeStruct((normed.shape[1], d_mlp.shape[1]), BF16),
            jax.ShapeDtypeStruct((4 * length, width), BF16),
            jax.ShapeDtypeStruct((length, width), F32),
            jax.ShapeDtypeStruct((8, width), F32),
        ],
        in_specs=[vmem] * 10,
        out_specs=[hbm] + [vmem] * 5,
        scratch_shapes=exchange_scratch(length, width)
        + share_scratch(length, width, CHUNKS)
        + scatter_scratch(shards, units, width)
        + [pltpu.VMEM((units * shards, width), BF16)],
        compiler_params=pltpu.CompilerParams(
            collective_id=3, has_side_effects=True, vmem_limit_bytes=60 * MIB
        ),
        name="scatter_down",
    )(part, branch_two, normed, d_mlp, active, w_down, mixed, cot, live, gain)


def scatter_mlp(
    shards,
    cut,
    length,
    mlp_ref,
    out_ref,
    proj_ref,
    step_ref,
    grad_ref,
    conv_ref,
    head_ref,
    chan_ref,
    cos_ref,
    sin_ref,
    down_ref,
    ffn_ref,
    down_all_ref,
    ffn_came_ref,
    mlp_own_ref,
    out_own_ref,
    d_ref,
    d_t_ref,
    conv_sum_ref,
    head_sum_ref,
    chan_sum_ref,
    act_ref,
    d_act_ref,
    d_pair_ref,
    col_ref,
    first_ref,
    slots_ref,
    send,
    recv,
    out_first_ref,
    out_slots_ref,
    out_send,
    out_recv,
    sh_send,
    sh_recv,
    sh_local,
    ffn_send,
    ffn_recv,
    shared_ref,
    shared_came_ref,
    add_sem,
):
    ring, pair = Ring(shards), Pair()
    greet(ring, pair, pair.corner)
    share = Share(pair, 1, down_ref, down_all_ref, (sh_send, sh_recv, sh_local))
    ffn = [
        remote(
            ffn_ref.at[1 + which],
            ffn_came_ref.at[which],
            ffn_send.at[which],
            ffn_recv.at[which],
            peer,
        )
        for which, peer in enumerate(pair.peers + (pair.corner,))
    ]
    mlp = Scatter(
        ring, pieces_of(mlp_ref.shape[1]), stored(mlp_ref), first_ref, slots_ref, send, recv
    )
    tall = out_slots_ref.shape[2] * 2
    mamba = cut.inner // shards

    def out_rows(index, rows):
        if rows.start < mamba:
            start = index * mamba + rows.start
        else:
            start = cut.inner + index * (tall - mamba) + rows.start - mamba
        return out_ref[pl.ds(pl.multiple_of(start, 16), rows.size)].astype(F32)

    out = Scatter(
        ring,
        pieces_of(tall),
        stored(out_ref) if len(out_ref.shape) == 3 else out_rows,
        out_first_ref,
        out_slots_ref,
        out_send,
        out_recv,
    )
    mlp.start()
    out.start()
    share.start(0)
    for copy in ffn:
        copy.start()
    for ref in (conv_sum_ref, head_sum_ref, chan_sum_ref):
        ref[...] = jnp.zeros_like(ref)
    count = proj_ref.shape[0] // length

    def body(number, carry):
        rows = pl.ds(pl.multiple_of(number * length, length), length)
        mixer_backward(
            cut,
            proj_ref.at[rows],
            step_ref.at[rows],
            grad_ref.at[rows],
            conv_ref,
            head_ref,
            chan_ref,
            cos_ref,
            sin_ref,
            d_ref.at[rows],
            conv_sum_ref,
            head_sum_ref,
            chan_sum_ref,
            act_ref,
            d_act_ref,
            d_pair_ref,
            col_ref,
        )
        mlp.advance(number + 2)
        out.advance(number + 2)
        half = LANES // 2
        for lane in range(0, cut.width, LANES):
            turned = d_ref[rows, lane : lane + LANES].T
            if lane >= cut.maps:
                shared_ref[lane - cut.maps : lane - cut.maps + LANES, rows] = turned
                continue
            for part in range(2):
                to = cut.ring_row(lane + part * half)
                d_t_ref[to : to + half, rows] = turned[part * half : (part + 1) * half]
        return carry

    lax.fori_loop(0, count, body, 0)
    core = pair.rep % 2
    of_core = lambda which: pl.multiple_of(which * cut.shared, 16)
    add = remote(
        shared_ref.at[pl.ds(of_core(1 - core), cut.shared)],
        shared_came_ref,
        add_sem.at[0],
        add_sem.at[1],
        pair.peers[1],
    )
    add.start()
    share.pass_on(0)
    mlp.advance(count + 2)
    out.advance(count + 2)
    add.wait()
    half = cut.shared // 2
    for way in range(2):
        rows = pl.ds(pl.multiple_of(of_core(core) + way * half, 16), half)
        to = way * cut.way + cut.maps // 2
        middle = 2 * length
        for here, there in ((0, middle), (middle, 0)):
            total = shared_ref[rows, here : here + middle].astype(F32)
            total = total + shared_came_ref[
                way * half : (way + 1) * half, there : there + middle
            ].astype(F32)
            d_t_ref[to : to + half, here : here + middle] = total.astype(BF16)

    def rest(step, carry):
        mlp.advance(step)
        out.advance(step)
        return carry

    lax.fori_loop(count + 3, shards, rest, 0)
    mlp.result(mlp_own_ref)
    out.result(out_own_ref)
    mlp.finish()
    out.finish()
    share.finish()
    for copy in ffn:
        copy.wait()


def scatter_mlp_call(
    shards, cut, length, mlp, out, proj, steps, grad, conv, head, chan, cosine, sine, down, ffn
):
    hbm = pl.BlockSpec(memory_space=pl.ANY)
    rows = proj.shape[0]
    vmem = pl.BlockSpec(memory_space=pltpu.VMEM)
    depth, wide = mlp.shape[1:]
    width = out.shape[-1]
    tall = out.size // width // shards
    return pl.pallas_call(
        functools.partial(scatter_mlp, shards, cut, length),
        out_shape=[
            jax.ShapeDtypeStruct((4,) + down.shape, BF16),
            jax.ShapeDtypeStruct((3, length, width), BF16),
            jax.ShapeDtypeStruct((depth, wide), BF16),
            jax.ShapeDtypeStruct((tall, width), BF16),
            jax.ShapeDtypeStruct((rows, cut.width), BF16),
            jax.ShapeDtypeStruct((2 * cut.way, rows), BF16),
            jax.ShapeDtypeStruct(conv.shape, F32),
            jax.ShapeDtypeStruct(head.shape, F32),
            jax.ShapeDtypeStruct(chan.shape, F32),
        ],
        in_specs=[vmem] * 11 + [hbm],
        out_specs=[hbm] * 2 + [vmem] * 7,
        scratch_shapes=[
            pltpu.VMEM((length, cut.conv), F32),
            pltpu.VMEM((length, cut.conv), F32),
            pltpu.VMEM((length, length), F32),
            pltpu.VMEM((LANES, length), F32),
        ]
        + scatter_scratch(shards, depth, wide)
        + scatter_scratch(shards, tall, width)
        + share_sems(1)
        + [pltpu.SemaphoreType.DMA((3,))] * 2
        + [
            pltpu.VMEM((2 * cut.shared, rows), BF16),
            pltpu.VMEM((cut.shared, rows), BF16),
            pltpu.SemaphoreType.DMA((2,)),
        ],
        compiler_params=pltpu.CompilerParams(
            collective_id=4, has_side_effects=True, vmem_limit_bytes=60 * MIB
        ),
        name="scatter_mlp",
    )(mlp, out, proj, steps, grad, conv, head, chan, cosine, sine, down, ffn)


GROUPS = 2
PIECES = 6


def scatter_in(shards, inside, *refs):
    refs = list(refs)
    take = lambda count: [refs.pop(0) for _ in range(count)]
    if inside:
        d_t_ref, normed_ref, d_hbm, w_hbm = take(4)
    else:
        in_ref, part_ref = take(2)
    small_ref, tokens_ref, d_mixed_ref, gain_ref, mlp_ref, out_ref = take(6)
    in_all_ref, small_all_ref, mlp_all_ref, out_all_ref, grad_ref = take(5)
    core_ref, cross_ref, came_ref, ex_send, ex_recv = take(5)
    in_scratch, small_scratch = take(4), take(4)
    own_ref, sh_send, sh_recv, sh_local = take(4)
    small_own_ref, sm_send, sm_recv, sm_local = take(4)
    mlp_sems, out_sems = take(3), take(3)
    move_ref, move_sem = take(2)
    if inside:
        d_ref, w_ref, part_ref, small_all, gain_sum_ref, load_sem, made_ref = take(7)

    ring, pair = Ring(shards), Pair()
    if inside:
        loads = [
            pltpu.make_async_copy(src, dst, load_sem.at[number])
            for number, (src, dst) in enumerate(((d_hbm, d_ref), (w_hbm, w_ref)))
        ]
        for load in loads:
            load.start()
        depth = w_ref.shape[1] // shards

        def term(index, rows):
            lanes = pl.ds(pl.multiple_of(index * depth, LANES), depth)
            return dot(d_t_ref[rows], normed_ref[:, lanes])

        small_term = stored(small_all)
    else:
        term, small_term = stored(in_ref), stored(small_ref)
    group = shards // 4
    here, rep = ring.index, pair.rep
    to = (group * rep + here // 4, here % 4)
    by = (4 * (here % group) + rep, here // group)
    far = to[0] * 4 + to[1] - here * 4 - rep
    limit = (4 * shards) ** 2
    moves = (far * far + limit - 1) // limit
    peer = {"fsdp": to[0], "rep": to[1]}
    move = remote(out_ref, move_ref, move_sem.at[0], move_sem.at[1], peer)
    stay = pltpu.make_async_copy(out_ref, move_ref, move_sem.at[2])
    greet(ring, pair, maybe=(peer, {"fsdp": by[0], "rep": by[1]}), are=moves)

    @pl.when(moves == 1)
    def _():
        move.start()

    @pl.when(moves == 0)
    def _():
        stay.start()

    pieces = PIECES
    scatter = Scatter(
        ring,
        pieces,
        term,
        *in_scratch,
        groups=GROUPS,
        made_ref=made_ref if inside else None,
    )
    small = Scatter(ring, 1, small_term, *small_scratch)
    exchange = Exchange(
        pair, CHUNKS, part_ref, core_ref, cross_ref, came_ref, (ex_send, ex_recv)
    )
    share = Share(pair, 2 * pieces, own_ref, in_all_ref, (sh_send, sh_recv, sh_local))
    small_share = Share(pair, 2, small_own_ref, small_all_ref, (sm_send, sm_recv, sm_local))
    mlp_share = Share(pair, CHUNKS, mlp_ref, mlp_all_ref, mlp_sems)
    out_share = Share(pair, 1, move_ref, out_all_ref, out_sems)

    def middle(chunk):
        rows = exchange.rows(chunk)
        grad = exchange.sum(chunk)
        values = tokens_ref[rows].astype(F32)
        d_values, _ = norm_back(values, norm_scale(values), gain_ref[0:1], grad)
        grad_ref[rows] = (d_mixed_ref[rows] + d_values).astype(BF16)

    def partial(tile):
        length = part_ref.shape[1]
        wide = part_ref.shape[2] // 4
        lanes = slice(tile * wide, (tile + 1) * wide)
        grad = dot(d_ref[...], w_ref[:, lanes])
        for number in range(4):
            rows = slice(number * length, (number + 1) * length)
            part_ref[number, :, lanes] = grad[rows].astype(BF16)
        gain_sum_ref[0:1, lanes] = jnp.sum(
            grad * normed_ref[:, lanes].astype(F32), axis=0, keepdims=True
        )

    scatter.start(0)
    for chunk in range(CHUNKS):
        mlp_share.start(chunk)
    if inside:
        gain_sum_ref[...] = jnp.zeros_like(gain_sum_ref)
        for load in loads:
            load.wait()
    for number in range(4):
        if inside:
            partial(number)
        scatter.advance(number + 2, 0)
    if inside:
        small_all[...] = small_ref[...]
        gain_sum = gain_sum_ref[0:1] / gain_ref[0:1]
        for index in range(shards):
            for row in range(depth // LANES):
                at = index * depth + row * LANES
                small_all[index, row : row + 1] = gain_sum[:, at : at + LANES].astype(BF16)
    exchange.start()
    small.start()
    scatter.advance(6, 0)
    exchange.middle(0)
    small.advance(2)
    exchange.middle(1)

    @pl.when(moves == 1)
    def _():
        move.wait()

    @pl.when(moves == 0)
    def _():
        stay.wait()

    out_share.start(0)
    scatter.run(7, shards, 0)
    small.advance(3)
    scatter.start(1)
    scatter.result(own_ref, share, 0)
    for step in range(2, 6):
        scatter.advance(step, 1)
        small.advance(step + 2)
        if step in (3, 4):
            middle(step - 3)
    small.run(8, shards)
    for chunk in range(CHUNKS):
        mlp_share.pass_on(chunk)
    scatter.advance(6, 1)
    out_share.pass_on(0)
    small.result(small_own_ref, small_share)
    for chunk in scatter.chunks(0):
        share.pass_on(chunk)
    scatter.run(7, shards, 1)
    scatter.result(own_ref, share, 1)
    for chunk in range(2):
        small_share.pass_on(chunk)
    for chunk in scatter.chunks(1):
        share.pass_on(chunk)
    scatter.finish()
    small.finish()
    exchange.finish()
    share.finish()
    small_share.finish()
    mlp_share.finish()
    out_share.finish()


def scatter_in_call(shards, depth, inside, given, small, tokens, d_mixed, gain, mlp, out):
    length, width = tokens.shape
    hbm = pl.BlockSpec(memory_space=pl.ANY)
    vmem = pl.BlockSpec(memory_space=pltpu.VMEM)
    wide = given[0].shape[0] if inside else given[0].shape[-2]
    tall, lanes = small.shape[1:]
    extra = []
    if inside:
        extra = [
            pltpu.VMEM(given[2].shape, BF16),
            pltpu.VMEM(given[3].shape, BF16),
            pltpu.VMEM((4, length, width), BF16),
            pltpu.VMEM(small.shape, BF16),
            pltpu.VMEM((8, width), F32),
            pltpu.SemaphoreType.DMA((2,)),
            pltpu.VMEM((2, wide // (2 * GROUPS), depth), F32),
        ]
    return pl.pallas_call(
        functools.partial(scatter_in, shards, inside),
        out_shape=[
            jax.ShapeDtypeStruct((4, wide, depth), BF16),
            jax.ShapeDtypeStruct((4, tall, lanes), BF16),
            jax.ShapeDtypeStruct((4,) + mlp.shape, BF16),
            jax.ShapeDtypeStruct((4,) + out.shape, BF16),
            jax.ShapeDtypeStruct((length, width), BF16),
        ],
        in_specs=([vmem] * 2 + [hbm] * 2 if inside else [vmem] * 2) + [vmem] * 6,
        out_specs=[hbm] * 4 + [vmem],
        scratch_shapes=exchange_scratch(length, width)
        + scatter_scratch(shards, wide, depth, PIECES)
        + scatter_scratch(shards, tall, lanes, 1)
        + share_scratch(wide, depth, 2 * PIECES)
        + share_scratch(tall, lanes, 2)
        + share_sems(CHUNKS)
        + share_sems(1)
        + [pltpu.VMEM(out.shape, BF16), pltpu.SemaphoreType.DMA((3,))]
        + extra,
        compiler_params=pltpu.CompilerParams(
            collective_id=5, has_side_effects=True, vmem_limit_bytes=60 * MIB
        ),
        name="scatter_in",
    )(*given, small, tokens, d_mixed, gain, mlp, out)


def columns(array, start, width):
    return lax.dynamic_slice_in_dim(array, start, width, axis=array.ndim - 1)


def norm_scale(values):
    return lax.rsqrt(jnp.mean(values * values, axis=-1, keepdims=True) + epsilon)


def norm_back(values, scale, gain, grad):
    inner = jnp.mean(gain * grad * values, axis=-1, keepdims=True)
    d_values = scale * gain * grad - values * (scale * scale * scale) * inner
    return d_values, jnp.sum(grad * values * scale, axis=0, keepdims=True)


def ring_at(position, shards):
    place = (position + 2 * shards) % shards
    back = place // (shards // 2)
    return (1 - back) * 2 * place + back * (2 * (shards - 1 - place) + 1)


def ring_place(index, shards):
    odd = index % 2
    return (1 - odd) * (index // 2) + odd * (shards - 1 - index // 2)


def after(value, *others):
    return lax.optimization_barrier((value,) + others)[0]


def rep_order(reps):
    order = [0]
    bit = reps // 2
    while bit:
        order = order + [member ^ bit for member in order]
        bit //= 2
    return order


def on_device(
    sizes,
    tokens,
    lengths,
    mixer_gain,
    in_proj,
    conv_weight,
    conv_bias,
    decay_log,
    step_bias,
    skip_gain,
    query_weight,
    key_weight,
    value_weight,
    mamba_out,
    attn_out,
    mlp_gain,
    gate_weight,
    up_weight,
    down_weight,
    cotangent,
):
    shards, reps = sizes
    cut = Cut(reps)
    rep = lax.axis_index("rep")
    fsdp = lax.axis_index("fsdp")
    place = ring_place(fsdp, shards)
    assert reps == 4
    length, width = tokens.shape
    depth = in_proj.shape[0]
    own = conv_weight.shape[1]
    channels = own * shards
    low = lambda v: v.astype(BF16)

    in_t = in_proj.T
    extra = 16
    aux = jnp.concatenate([mixer_gain, mlp_gain, conv_weight.reshape(-1), conv_bias], axis=0)
    aux_size = aux.shape[0]
    aux = jnp.pad(aux, (0, extra * 2 * LANES - aux_size)).reshape(extra, 2 * LANES)
    group = shards // reps
    pairs = [
        (g * reps + part, (reps * (g % group) + part) * reps + g // group)
        for g in range(shards)
        for part in range(reps)
    ]
    mamba_rows = mamba_out.shape[0] // reps
    attn_rows = attn_out.shape[0] // reps
    out_rows = mamba_rows + attn_rows
    share_out = jnp.concatenate(
        [
            lax.dynamic_slice_in_dim(mamba_out, mamba_rows * rep, mamba_rows, axis=0),
            lax.dynamic_slice_in_dim(attn_out, attn_rows * rep, attn_rows, axis=0),
        ],
        axis=0,
    )
    units = down_weight.shape[0] // reps
    if units % LANES:
        pick = lambda w: lax.dynamic_index_in_dim(
            w.reshape(depth, shards, reps, units), rep, axis=2, keepdims=False
        ).reshape(depth, shards * units)
        sources = (jnp.concatenate([pick(gate_weight), pick(up_weight)], axis=1),)
    else:
        sources = (gate_weight, up_weight)
    share_down = lax.dynamic_slice_in_dim(down_weight, units * rep, units, axis=0)

    live = (jnp.arange(length) < lengths[0]).astype(F32)[:, None]
    stream = tokens.astype(F32)
    live_wide = jnp.broadcast_to(live, (length, LANES))
    w_in, aux_all, branch_two, tokens_all = gather_in_call(
        shards,
        cut,
        in_t,
        query_weight,
        key_weight,
        value_weight,
        aux,
        tokens,
        cotangent,
        live_wide,
    )
    if w_in.ndim == 3:
        w_in = jnp.moveaxis(w_in, 0, 1).reshape(cut.width, width)
    branch_two = branch_two.reshape(reps * length, width)
    share_out = lax.ppermute(share_out, ("fsdp", "rep"), pairs)

    put = lax.dynamic_update_slice
    inner_rows = mamba_rows * shards
    half_ff = shards * units

    aux_all = aux_all.reshape(shards, -1)[:, :aux_size].astype(F32)
    gain_one = aux_all[:, :depth].reshape(1, width)
    gain_two = aux_all[:, depth : 2 * depth].reshape(1, width)
    conv_all = aux_all[:, 2 * depth :].reshape(shards, CONV + 1, own)
    conv_all = conv_all.transpose(1, 0, 2).reshape(CONV + 1, channels)
    conv_own = jnp.concatenate(
        [columns(conv_all, cut.inner * rep, cut.inner), conv_all[:, INNER:]], axis=1
    )
    conv_own = jnp.pad(conv_own, ((0, 7 - CONV), (0, 0)))
    of_heads = lambda v: jnp.pad(
        lax.dynamic_slice_in_dim(v, cut.heads * rep, cut.heads), (0, LANES - cut.heads)
    )
    head_own = jnp.stack([of_heads(decay_log), of_heads(step_bias)])
    head_own = jnp.pad(head_own, ((0, 6), (0, 0)))
    chan_own = lax.dynamic_slice_in_dim(skip_gain, cut.heads * rep, cut.heads)
    chan_own = jnp.pad(jnp.repeat(chan_own, HDIM)[None, :], ((0, 7), (0, 0)))
    cosine, sine = turn_tables(length)

    inside = depth % LANES == 0
    ordered = mamba_rows % 16 == 0 and attn_rows % 16 == 0
    w_out, w_down, mixed_heads, normed, proj, steps = gather_rows_call(
        shards,
        cut,
        length,
        ordered,
        share_out,
        share_down,
        w_in,
        tokens_all,
        jnp.broadcast_to(gain_one, (8, width)),
        conv_own,
        head_own,
        chan_own,
        cosine,
        sine,
    )
    if not ordered:
        w_out = jnp.concatenate(
            [
                w_out[:, :mamba_rows].reshape(-1, width),
                w_out[:, mamba_rows:].reshape(-1, width),
            ],
            axis=0,
        )
    w_down = w_down.reshape(-1, width)
    gain_rows = jnp.broadcast_to(gain_two, (8, width))
    w_mlp, normed_two, mixed, *gate_up = gather_mlp_call(
        shards, inside, sources, 2 * half_ff, mixed_heads, w_out, tokens, live_wide, gain_rows
    )
    w_mlp = w_mlp.reshape(width, -1)
    normed_two = normed_two.reshape(reps * length, width)
    gate_up = gate_up[0] if inside else dot(normed_two, w_mlp)
    activated, d_gate_up, d_two = mlp_back_call(gate_up, branch_two, w_down, w_mlp)
    d_two = d_two.reshape(reps, length, width)
    branch_one, s_down, g_mlp, ffn, d_mixed, gain_two_sum = scatter_down_call(
        shards,
        d_two,
        branch_two,
        normed_two,
        d_gate_up,
        activated,
        w_down,
        mixed,
        cotangent,
        live_wide,
        gain_rows,
    )
    g_mlp = g_mlp.reshape(shards, depth, -1)
    ffn = ffn.reshape(reps, length, width)

    branch_one = branch_one.reshape(reps * length, width)
    d_heads = dot_nt(branch_one, w_out)
    g_out = low(dot_tn(mixed_heads, branch_one))
    if not ordered:
        g_out = jnp.concatenate(
            [
                g_out[:inner_rows].reshape(shards, mamba_rows, width),
                g_out[inner_rows:].reshape(shards, attn_rows, width),
            ],
            axis=1,
        )
    downs, came, s_mlp, s_out, d_proj, d_proj_t, conv_sum, head_sum, chan_sum = scatter_mlp_call(
        shards,
        cut,
        length,
        g_mlp,
        g_out,
        proj,
        steps,
        d_heads,
        conv_own,
        head_own,
        chan_own,
        cosine,
        sine,
        s_down,
        ffn,
    )
    ffn_sum = ffn[0].astype(F32) + came.astype(F32).sum(axis=0)
    output = low(mixed + live * ffn_sum)
    if inside:
        given = (d_proj_t, normed, d_proj, w_in)
        gain_one_sum = jnp.zeros((width,), F32)
    else:
        g_in = low(dot(d_proj_t, normed))
        g_in = jnp.moveaxis(g_in.reshape(2 * cut.way, shards, depth), 1, 0)
        d_one = dot(d_proj, w_in)
        stream_all = tokens_all.reshape(reps * length, width).astype(F32)
        scale_all = norm_scale(stream_all)
        gain_one_sum = jnp.sum(d_one * stream_all * scale_all, axis=0)
        given = (g_in, low(d_one).reshape(reps, length, width))

    conv_sums = jnp.zeros((CONV + 1, channels), F32)
    conv_sums = put(conv_sums, conv_sum[: CONV + 1, : cut.inner], (0, cut.inner * rep))
    conv_sums = put(conv_sums, conv_sum[: CONV + 1, cut.inner :], (0, INNER))
    head_sums = jnp.zeros((3, HEADS), F32)
    own_sums = jnp.stack(
        [
            head_sum[0, : cut.heads],
            head_sum[1, : cut.heads],
            jnp.sum(chan_sum[0].reshape(cut.heads, HDIM), axis=1),
        ]
    )
    head_sums = put(head_sums, own_sums, (0, cut.heads * rep))
    small = jnp.concatenate(
        [
            gain_one_sum.reshape(shards, depth),
            gain_two_sum[0].reshape(shards, depth),
            conv_sums.reshape(CONV + 1, shards, own).transpose(1, 0, 2).reshape(shards, -1),
            jnp.broadcast_to(head_sums.reshape(1, -1), (shards, 3 * HEADS)),
        ],
        axis=1,
    )
    small_size = small.shape[1]
    tall = 32
    small = jnp.pad(low(small), ((0, 0), (0, tall * LANES - small_size)))
    small = small.reshape(shards, tall, LANES)
    ins, smalls, mlps, outs, grad_tokens = scatter_in_call(
        shards,
        depth,
        inside,
        given,
        small,
        tokens,
        d_mixed,
        jnp.broadcast_to(gain_one, (8, width)),
        s_mlp,
        s_out,
    )

    places = jnp.stack([rep ^ member for member in rep_order(reps)]).astype(jnp.int32)
    spread = functools.partial(spread_call, places)
    out_mamba, out_attn = spread(
        outs,
        [(mamba_rows * reps, width), (attn_rows * reps, width)],
        [
            (0, slice(0, mamba_rows), slice(0, width), mamba_rows, 0, 0),
            (1, slice(mamba_rows, out_rows), slice(0, width), attn_rows, 0, 0),
        ],
    )
    (out_down,) = spread(
        downs,
        [(units * reps, width)],
        [(0, slice(0, units), slice(0, width), units, 0, 0)],
    )
    out_gate, out_up = spread(
        mlps,
        [(depth, half_ff * reps)] * 2,
        [
            (
                which,
                slice(0, depth),
                slice(which * half_ff + shard * units, which * half_ff + (shard + 1) * units),
                0,
                units,
                shard * units * reps,
            )
            for which in range(2)
            for shard in range(shards)
        ],
    )
    out_wide, out_query, out_key, out_value = spread_in_call(cut, places, ins)
    out_proj = out_wide.T
    small = smalls.astype(F32).sum(axis=0).reshape(-1)[:small_size]
    out_gain_one = small[:depth]
    out_gain_two = small[depth : 2 * depth]
    conv_sums = small[2 * depth : 2 * depth + (CONV + 1) * own].reshape(CONV + 1, own)
    out_decay, out_step, out_skip = small[2 * depth + (CONV + 1) * own :].reshape(3, HEADS)
    return (
        output,
        grad_tokens,
        out_gain_one,
        out_proj,
        conv_sums[:CONV],
        conv_sums[CONV],
        out_decay,
        out_step,
        out_skip,
        out_query,
        out_key,
        out_value,
        out_mamba,
        out_attn,
        out_gain_two,
        out_gate,
        out_up,
        out_down,
    )


def solution(mesh):
    rows = P(("fsdp", "rep"), None)
    shard = P("fsdp", None)
    in_specs = (
        rows,
        P(("fsdp", "rep")),
        P("fsdp"),
        shard,
        P(None, "fsdp"),
        P("fsdp"),
        P(),
        P(),
        P(),
        shard,
        shard,
        shard,
        shard,
        shard,
        P("fsdp"),
        shard,
        shard,
        shard,
        rows,
    )
    out_specs = (
        rows,
        rows,
        P("fsdp"),
        shard,
        P(None, "fsdp"),
        P("fsdp"),
        P(),
        P(),
        P(),
        shard,
        shard,
        shard,
        shard,
        shard,
        P("fsdp"),
        shard,
        shard,
        shard,
    )
    sizes = (mesh.shape["fsdp"], mesh.shape["rep"])
    return jax.shard_map(
        functools.partial(on_device, sizes),
        mesh=mesh,
        in_specs=in_specs,
        out_specs=out_specs,
        check_vma=False,
    )
```

```python
import functools

import jax
import jax.numpy as jnp
from jax import lax
from jax.experimental import pallas as pl
from jax.experimental.pallas import tpu as pltpu
from jax.sharding import PartitionSpec as P

HEADS = 48
HDIM = 64
STATE = 256
CONV = 4
QH = 8
KVH = 2
HEAD_WIDTH = 128
INNER = HEADS * HDIM
LANES = 128
ROWS = 128
MIB = 1 << 20
MESH = pl.DeviceIdType.MESH

epsilon = 1e-05
BF16 = jnp.bfloat16
F32 = jnp.float32
HIGHEST = lax.Precision.HIGHEST


def dot(left, right, contract=((1,), (0,)), precision=None):
    return lax.dot_general(
        left, right, (contract, ((), ())), preferred_element_type=F32, precision=precision
    )


def dot_tn(left, right, precision=None):
    return dot(left, right, ((0,), (0,)), precision)


def dot_nt(left, right, precision=None):
    return dot(left, right, ((1,), (1,)), precision)


def sigmoid(v):
    return 1.0 / (1.0 + jnp.exp(-v))


def silu_slope(v, sig):
    return sig * (1.0 + v * (1.0 - sig))


def softplus(v):
    return jnp.maximum(v, 0.0) + jnp.log1p(jnp.exp(-jnp.abs(v)))


def shift_down(v, by):
    if by == 0:
        return v
    return jnp.concatenate([jnp.zeros((by, v.shape[1]), v.dtype), v[:-by]], axis=0)


def shift_up(v, by):
    if by == 0:
        return v
    return jnp.concatenate([v[by:], jnp.zeros((by, v.shape[1]), v.dtype)], axis=0)


class Cut:
    def __init__(self, reps):
        self.heads = HEADS // reps
        self.inner = INNER // reps
        self.qheads = QH // reps
        self.qwidth = self.qheads * HEAD_WIDTH
        self.q = 0
        self.step = self.qwidth
        self.z = self.step + LANES
        self.x = self.z + self.inner
        self.maps = self.x + self.inner
        self.k = self.maps + 2 * STATE
        self.v = self.k + HEAD_WIDTH
        self.width = self.v + HEAD_WIDTH
        self.conv = self.inner + 2 * STATE
        self.shared = (self.width - self.maps) // 2
        self.way = (self.maps + self.shared) // 2

    def ring_row(self, column):
        half = self.maps // 2
        return column if column < half else column - half + self.way


def conv_out_of(ref, lanes, start, conv_ref):
    width = lanes.stop - lanes.start
    given = ref[:, start : start + width].astype(F32)
    total = conv_ref[CONV : CONV + 1, lanes]
    for tap in range(CONV):
        total = total + conv_ref[tap : tap + 1, lanes] * shift_down(given, CONV - 1 - tap)
    return total, given


def conv_back(d_out, given, conv_ref, lanes, sums_ref):
    d_given = jnp.zeros_like(d_out)
    for tap in range(CONV):
        back = CONV - 1 - tap
        d_given = d_given + conv_ref[tap : tap + 1, lanes] * shift_up(d_out, back)
        sums_ref[tap : tap + 1, lanes] += jnp.sum(
            d_out * shift_down(given, back), axis=0, keepdims=True
        )
    sums_ref[CONV : CONV + 1, lanes] += jnp.sum(d_out, axis=0, keepdims=True)
    return d_given


def ones_triangle(length, upper):
    row = lax.broadcasted_iota(jnp.int32, (length, length), 0)
    col = lax.broadcasted_iota(jnp.int32, (length, length), 1)
    return jnp.where(col >= row if upper else col <= row, 1.0, 0.0).astype(F32)


def steps_of(step_ref, head_ref):
    raw = step_ref[...] + head_ref[1:2, :]
    step = softplus(raw)
    decay = -step * jnp.exp(head_ref[0:1, :])
    running = dot(ones_triangle(raw.shape[0], False), decay, precision=HIGHEST)
    return raw, step, decay, running


def decay_block(running, running_t, head, block):
    top, width = block * ROWS, (block + 1) * ROWS
    gap = running[top:width, head : head + 1] - running_t[head : head + 1, :width]
    row = lax.broadcasted_iota(jnp.int32, (ROWS, width), 0) + top
    col = lax.broadcasted_iota(jnp.int32, (ROWS, width), 1)
    return jnp.where(row >= col, jnp.exp(gap), 0.0)


def turn(v, cos_ref, sin_ref):
    half = HEAD_WIDTH // 2
    return v * cos_ref[...] + pltpu.roll(v, half, 1) * sin_ref[...]


def turn_back(v, cos_ref, sin_ref):
    half = HEAD_WIDTH // 2
    return v * cos_ref[...] - pltpu.roll(v, half, 1) * sin_ref[...]


def softmax_rows(q, k):
    scores = dot_nt(q, k) * HEAD_WIDTH ** (-0.5)
    row = lax.broadcasted_iota(jnp.int32, scores.shape, 0)
    col = lax.broadcasted_iota(jnp.int32, scores.shape, 1)
    scores = jnp.where(row >= col, scores, -1e30)
    top = jnp.max(scores, axis=1, keepdims=True)
    weight = jnp.exp(scores - top)
    return weight / jnp.sum(weight, axis=1, keepdims=True)


def mixer_forward(
    cut, proj_ref, step_ref, conv_ref, head_ref, chan_ref, cos_ref, sin_ref, out_ref, act_ref
):
    length = proj_ref.shape[0]
    for lane in range(0, cut.conv, 2 * LANES):
        lanes = slice(lane, min(lane + 2 * LANES, cut.conv))
        total, _ = conv_out_of(proj_ref, lanes, cut.x + lane, conv_ref)
        act_ref[:, lanes] = total * sigmoid(total)
    _, step, _, running = steps_of(step_ref, head_ref)
    step_t, running_t = step.T, running.T
    in_map = act_ref[:, cut.inner : cut.inner + STATE].astype(BF16)
    out_map = act_ref[:, cut.inner + STATE : cut.inner + 2 * STATE].astype(BF16)
    pairing = dot_nt(out_map, in_map)
    first = lax.broadcasted_iota(jnp.int32, (ROWS, LANES), 1) < HDIM
    for pair in range(cut.heads // 2):
        lanes = slice(pair * LANES, (pair + 1) * LANES)
        given = act_ref[:, lanes].astype(BF16)
        for block in range(length // ROWS):
            rows = slice(block * ROWS, (block + 1) * ROWS)
            parts = []
            for head in (2 * pair, 2 * pair + 1):
                mixing = (
                    pairing[rows, : rows.stop]
                    * decay_block(running, running_t, head, block)
                    * step_t[head : head + 1, : rows.stop]
                )
                parts.append(dot(mixing.astype(BF16), given[: rows.stop]))
            ssm = jnp.where(first, parts[0], parts[1])
            ssm = ssm + chan_ref[0:1, lanes] * act_ref[rows, lanes]
            gate = proj_ref[rows, cut.z + lanes.start : cut.z + lanes.stop].astype(F32)
            out_ref[rows, lanes] = (ssm * gate * sigmoid(gate)).astype(BF16)
    key = turn(proj_ref[:, cut.k : cut.k + HEAD_WIDTH].astype(F32), cos_ref, sin_ref).astype(BF16)
    value = proj_ref[:, cut.v : cut.v + HEAD_WIDTH].astype(BF16)
    for head in range(cut.qheads):
        at = cut.q + head * HEAD_WIDTH
        query = turn(proj_ref[:, at : at + HEAD_WIDTH].astype(F32), cos_ref, sin_ref).astype(BF16)
        probs = softmax_rows(query, key).astype(BF16)
        to = cut.inner + head * HEAD_WIDTH
        out_ref[:, to : to + HEAD_WIDTH] = dot(probs, value).astype(BF16)


def mixer_backward(
    cut,
    proj_ref,
    step_ref,
    grad_ref,
    conv_ref,
    head_ref,
    chan_ref,
    cos_ref,
    sin_ref,
    d_ref,
    conv_sum_ref,
    head_sum_ref,
    chan_sum_ref,
    act_ref,
    d_act_ref,
    d_pair_ref,
    col_ref,
):
    length = proj_ref.shape[0]

    for lane in range(0, cut.conv, 2 * LANES):
        lanes = slice(lane, min(lane + 2 * LANES, cut.conv))
        total, _ = conv_out_of(proj_ref, lanes, cut.x + lane, conv_ref)
        act_ref[:, lanes] = total * sigmoid(total)
    raw, step, decay, running = steps_of(step_ref, head_ref)
    step_t, running_t = step.T, running.T
    in_map = act_ref[:, cut.inner : cut.inner + STATE].astype(BF16)
    out_map = act_ref[:, cut.inner + STATE : cut.inner + 2 * STATE].astype(BF16)
    pairing = dot_nt(out_map, in_map)
    d_pair_ref[...] = jnp.zeros_like(d_pair_ref)
    col_ref[...] = jnp.zeros_like(col_ref)
    first = lax.broadcasted_iota(jnp.int32, (ROWS, LANES), 1) < HDIM
    lane_of = lax.broadcasted_iota(jnp.int32, (ROWS, LANES), 1)
    row_sums = [jnp.zeros((ROWS, LANES), F32) for _ in range(length // ROWS)]
    for pair in range(cut.heads // 2):
        lanes = slice(pair * LANES, (pair + 1) * LANES)
        given_f = act_ref[:, lanes]
        given = given_f.astype(BF16)
        skip = chan_ref[0:1, lanes]
        skip_sum = jnp.zeros((1, LANES), F32)
        for block in range(length // ROWS):
            rows = slice(block * ROWS, (block + 1) * ROWS)
            width = rows.stop
            z_lanes = slice(cut.z + lanes.start, cut.z + lanes.stop)
            gate = proj_ref[rows, z_lanes].astype(F32)
            sig = sigmoid(gate)
            d_mixed = grad_ref[rows, lanes].astype(F32)
            d_ssm = d_mixed * gate * sig
            skip_sum = skip_sum + jnp.sum(d_ssm * given_f[rows], axis=0, keepdims=True)
            parts = []
            d_given = jnp.zeros((width, LANES), F32)
            for which in range(2):
                head = 2 * pair + which
                d_head = jnp.where(first if which == 0 else ~first, d_ssm, 0.0).astype(BF16)
                fall = decay_block(running, running_t, head, block)
                step_row = step_t[head : head + 1, :width]
                d_mixing = dot_nt(d_head, given[:width])
                stepped = fall * step_row
                mixing = pairing[rows, :width] * stepped
                mixing_low = mixing.astype(BF16)
                parts.append(dot(mixing_low, given[:width]))
                d_given = d_given + dot_tn(mixing_low, d_head)
                d_pair_ref[rows, :width] += d_mixing * stepped
                flow = d_mixing * mixing
                row_sums[block] = jnp.where(
                    lane_of == head,
                    jnp.sum(flow, axis=1, keepdims=True),
                    row_sums[block],
                )
                col_ref[head : head + 1, :width] += jnp.sum(
                    d_mixing * pairing[rows, :width] * fall, axis=0, keepdims=True
                )
            if block == 0:
                d_act_ref[:, lanes] = jnp.zeros((length, LANES), F32)
            d_act_ref[:width, lanes] += d_given
            d_act_ref[rows, lanes] += d_ssm * skip
            ssm = jnp.where(first, parts[0], parts[1]) + skip * given_f[rows]
            d_ref[rows, z_lanes] = (d_mixed * ssm * silu_slope(gate, sig)).astype(BF16)
        chan_sum_ref[0:1, lanes] += skip_sum
    d_pair = d_pair_ref[...].astype(BF16)
    d_act_ref[:, cut.inner : cut.inner + STATE] = dot_tn(d_pair, out_map)
    d_act_ref[:, cut.inner + STATE : cut.inner + 2 * STATE] = dot(d_pair, in_map)
    col_sum = col_ref[...].T
    d_running = jnp.concatenate(row_sums, axis=0) - step * col_sum
    d_decay = dot(ones_triangle(length, True), d_running, precision=HIGHEST)
    d_step = col_sum - d_decay * jnp.exp(head_ref[0:1, :])
    d_raw = d_step * sigmoid(raw)
    valid = lax.broadcasted_iota(jnp.int32, d_raw.shape, 1) < cut.heads
    d_raw = jnp.where(valid, d_raw, 0.0)
    d_ref[:, cut.step : cut.step + LANES] = d_raw.astype(BF16)
    head_sum_ref[0:1, :] += jnp.sum(d_decay * decay, axis=0, keepdims=True)
    head_sum_ref[1:2, :] += jnp.sum(d_raw, axis=0, keepdims=True)
    for lane in range(0, cut.conv, 2 * LANES):
        lanes = slice(lane, min(lane + 2 * LANES, cut.conv))
        total, given = conv_out_of(proj_ref, lanes, cut.x + lane, conv_ref)
        d_out = d_act_ref[:, lanes] * silu_slope(total, sigmoid(total))
        d_given = conv_back(d_out, given, conv_ref, lanes, conv_sum_ref)
        d_ref[:, cut.x + lane : cut.x + lanes.stop] = d_given.astype(BF16)
    key = turn(proj_ref[:, cut.k : cut.k + HEAD_WIDTH].astype(F32), cos_ref, sin_ref).astype(BF16)
    value = proj_ref[:, cut.v : cut.v + HEAD_WIDTH].astype(BF16)
    d_key = jnp.zeros((length, HEAD_WIDTH), F32)
    d_value = jnp.zeros((length, HEAD_WIDTH), F32)
    for head in range(cut.qheads):
        at = cut.q + head * HEAD_WIDTH
        query = turn(proj_ref[:, at : at + HEAD_WIDTH].astype(F32), cos_ref, sin_ref).astype(BF16)
        probs = softmax_rows(query, key)
        to = cut.inner + head * HEAD_WIDTH
        d_attended = grad_ref[:, to : to + HEAD_WIDTH].astype(BF16)
        d_probs = dot_nt(d_attended, value)
        inner = jnp.sum(probs * d_probs, axis=1, keepdims=True)
        d_scores = (probs * (d_probs - inner)).astype(BF16)
        d_query = dot(d_scores, key) * HEAD_WIDTH ** (-0.5)
        d_key = d_key + dot_tn(d_scores, query) * HEAD_WIDTH ** (-0.5)
        d_value = d_value + dot_tn(probs.astype(BF16), d_attended)
        d_ref[:, at : at + HEAD_WIDTH] = turn_back(d_query, cos_ref, sin_ref).astype(BF16)
    d_ref[:, cut.k : cut.k + HEAD_WIDTH] = turn_back(d_key, cos_ref, sin_ref).astype(BF16)
    d_ref[:, cut.v : cut.v + HEAD_WIDTH] = d_value.astype(BF16)


def spread(moves, places_ref, blocks_ref, *refs):
    for which in range(4):
        at = places_ref[which]
        for out, rows, lanes, row_by, lane_by, lane_from in moves:
            height, width = rows.stop - rows.start, lanes.stop - lanes.start
            row, lane = at * row_by, lane_from + at * lane_by
            if row_by:
                row = pl.multiple_of(row, row_by)
            if lane_by and lane_by % LANES == 0:
                lane = pl.multiple_of(lane, LANES)
            refs[out][pl.ds(row, height), pl.ds(lane, width)] = blocks_ref[
                which, rows, lanes
            ].astype(F32)


def spread_call(places, blocks, outs, moves):
    if any(move[4] % LANES for move in moves):
        return spread_plain(places, blocks, outs, moves)
    return pl.pallas_call(
        functools.partial(spread, moves),
        out_shape=[jax.ShapeDtypeStruct(shape, F32) for shape in outs],
        in_specs=[pl.BlockSpec(memory_space=pltpu.SMEM)]
        + [pl.BlockSpec(memory_space=pltpu.VMEM)],
        out_specs=[pl.BlockSpec(memory_space=pltpu.VMEM)] * len(outs),
        compiler_params=pltpu.CompilerParams(vmem_limit_bytes=40 * MIB),
        name="spread",
    )(places, blocks)


def spread_plain(places, blocks, outs, moves):
    result = [jnp.zeros(shape, F32) for shape in outs]
    for which in range(4):
        block, at = blocks[which], places[which]
        for out, rows, lanes, row_by, lane_by, lane_from in moves:
            result[out] = lax.dynamic_update_slice(
                result[out],
                block[rows, lanes].astype(F32),
                (at * row_by, lane_from + at * lane_by),
            )
    return result


def spread_in(cut, places_ref, *refs):
    blocks_ref, wide_ref, query_ref, key_ref, value_ref = refs
    key_ref[...] = jnp.zeros_like(key_ref)
    value_ref[...] = jnp.zeros_like(value_ref)
    split = cut.maps // 2
    first = split - cut.z
    maps = 2 * INNER
    for which in range(4):
        block = blocks_ref.at[which]
        at = places_ref[which]
        lanes = pl.ds(pl.multiple_of(at * cut.qwidth, LANES), cut.qwidth)
        query_ref[:, lanes] = block[: cut.qwidth].astype(F32).T
        to = pl.multiple_of(at * cut.inner, ROWS)
        wide_ref[pl.ds(to, first)] = block[cut.z : split].astype(F32)
        wide_ref[pl.ds(pl.multiple_of(to + first, 64), cut.inner - first)] = block[
            cut.way : cut.way + cut.inner - first
        ].astype(F32)
        wide_ref[pl.ds(INNER + to, cut.inner)] = block[
            cut.way + cut.inner - first : cut.way + split
        ].astype(F32)
    halves = [
        jnp.concatenate(
            [
                blocks_ref[which, split : cut.way].astype(F32),
                blocks_ref[which, cut.way + split :].astype(F32),
            ],
            axis=0,
        )
        for which in range(4)
    ]
    ones = [places_ref[which] % 2 for which in range(4)]
    low_half = sum(jnp.where(one == 0, half, 0.0) for one, half in zip(ones, halves))
    wide_ref[maps : maps + cut.shared] = low_half
    rest = 2 * STATE - cut.shared
    high = [jnp.where(one == 1, half, 0.0) for one, half in zip(ones, halves)]
    wide_ref[maps + cut.shared : maps + 2 * STATE] = sum(half[:rest] for half in high)
    for which, half in enumerate(high):
        lanes = pl.ds(
            pl.multiple_of(places_ref[which] * KVH // 4 * HEAD_WIDTH, LANES), HEAD_WIDTH
        )
        key_ref[:, lanes] += half[rest : rest + HEAD_WIDTH].T
        value_ref[:, lanes] += half[rest + HEAD_WIDTH :].T
    for rep in range(4):
        steps = sum(
            jnp.where(places_ref[which] == rep, 1.0, 0.0)
            * blocks_ref[which, cut.step : cut.step + LANES].astype(F32)
            for which in range(4)
        )
        to = maps + 2 * STATE + rep * cut.heads
        wide_ref[to : to + cut.heads] = steps[: cut.heads]


def spread_in_call(cut, places, blocks):
    depth = blocks.shape[2]
    vmem = pl.BlockSpec(memory_space=pltpu.VMEM)
    columns_in = 2 * INNER + 2 * STATE + HEADS
    return pl.pallas_call(
        functools.partial(spread_in, cut),
        out_shape=[
            jax.ShapeDtypeStruct((columns_in, depth), F32),
            jax.ShapeDtypeStruct((depth, QH * HEAD_WIDTH), F32),
            jax.ShapeDtypeStruct((depth, KVH * HEAD_WIDTH), F32),
            jax.ShapeDtypeStruct((depth, KVH * HEAD_WIDTH), F32),
        ],
        in_specs=[pl.BlockSpec(memory_space=pltpu.SMEM), vmem],
        out_specs=[vmem] * 4,
        compiler_params=pltpu.CompilerParams(vmem_limit_bytes=40 * MIB),
        name="spread_in",
    )(places, blocks)


def turn_tables(length):
    half = HEAD_WIDTH // 2
    position = jnp.arange(length).astype(F32)
    freqs = 10000.0 ** (-jnp.arange(half).astype(F32) * 2.0 / HEAD_WIDTH)
    angles = position[:, None] * freqs[None, :]
    cosine, sine = jnp.cos(angles), jnp.sin(angles)
    return (
        jnp.concatenate([cosine, cosine], axis=1),
        jnp.concatenate([-sine, sine], axis=1),
    )


class Ring:
    def __init__(self, shards):
        self.shards = shards
        self.index = lax.axis_index("fsdp")
        self.place = ring_place(self.index, shards)

    def at(self, offset):
        return ring_at(self.place + offset, self.shards)

    def peer(self, way):
        return {"fsdp": self.at(1 - 2 * way)}


class Pair:
    def __init__(self):
        self.rep = lax.axis_index("rep")
        across, core = self.rep // 2, self.rep % 2
        self.peers = ({"rep": (1 - across) * 2 + core}, {"rep": across * 2 + 1 - core})
        self.corner = {"rep": (1 - across) * 2 + 1 - core}


def greet(ring, pair, *more, maybe=(), are=None):
    barrier = pltpu.get_barrier_semaphore()

    def signal(peers):
        for peer in peers:
            pl.semaphore_signal(barrier, inc=1, device_id=peer, device_id_type=MESH)

    peers = (ring.peer(0), ring.peer(1)) + pair.peers + more
    signal(peers)
    if not maybe:
        pl.semaphore_wait(barrier, len(peers))
        return
    pl.when(are == 1)(lambda: signal(maybe))
    pl.semaphore_wait(barrier, len(peers) + len(maybe) * are)


class Gather:
    def __init__(self, ring, ways, send, recv, hook=None):
        self.ring, self.ways, self.send, self.recv = ring, ways, send, recv
        self.hook = hook or (lambda step, way, piece: None)

    def pieces(self):
        for piece in range(max(len(way) for way in self.ways)):
            for way in range(2):
                if piece < len(self.ways[way]):
                    yield way, piece

    def copy(self, step, way, piece, first=False):
        own, place = self.ways[way][piece]
        there = place(self.ring.at((2 * way - 1) * (step - 1)))
        return pltpu.make_async_remote_copy(
            src_ref=own if first else there,
            dst_ref=there,
            send_sem=self.send.at[step - 1, way, piece],
            recv_sem=self.recv.at[step - 1, way, piece],
            device_id=self.ring.peer(way),
            device_id_type=MESH,
        )

    def landed(self, step, way, piece):
        here = self.ways[way][piece][1](self.ring.at((2 * way - 1) * step))
        return pltpu.make_async_remote_copy(
            src_ref=here,
            dst_ref=here,
            send_sem=self.send.at[step - 1, way, piece],
            recv_sem=self.recv.at[step - 1, way, piece],
            device_id=self.ring.peer(way),
            device_id_type=MESH,
        )

    def start(self):
        for way, piece in self.pieces():
            self.copy(1, way, piece, True).start()

    def advance(self, step):
        for way, piece in self.pieces():
            self.landed(step - 1, way, piece).wait_recv()
            self.copy(step, way, piece).start()
            self.hook(step - 1, way, piece)

    def run(self, first, stop):
        def body(step, carry):
            self.advance(step)
            return carry

        lax.fori_loop(first, stop, body, 0)

    def finish(self):
        for way, piece in self.pieces():
            self.landed(self.ring.shards - 1, way, piece).wait_recv()
            self.hook(self.ring.shards - 1, way, piece)
            self.copy(1, way, piece, True).wait_send()

        def body(step, carry):
            for way, piece in self.pieces():
                self.copy(step, way, piece).wait_send()
            return carry

        lax.fori_loop(2, self.ring.shards, body, 0)


def ring_sems(shards, pieces):
    return [pltpu.SemaphoreType.DMA((shards - 1, 2, pieces))] * 2


def remote(src, dst, send, recv, peer):
    return pltpu.make_async_remote_copy(
        src_ref=src, dst_ref=dst, send_sem=send, recv_sem=recv, device_id=peer, device_id_type=MESH
    )


def block_at(ref, index, rows, lanes):
    if len(ref.shape) == 2:
        return ref.at[rows, pl.ds(pl.multiple_of(index * lanes, LANES), lanes)]
    return ref.at[index, rows]


def gather_in(shards, cut, *refs):
    refs = list(refs)
    take = lambda number: [refs.pop(0) for _ in range(number)]
    in_ref, query_ref, key_ref, value_ref, aux_ref, tokens_ref, cot_ref, live_ref = take(8)
    w_ref, aux_all_ref, branch_all_ref, tokens_all_ref = take(4)
    share_ref, turn_ref, rows_ref, branch_ref = take(4)
    pack_sem, send, recv, core_send, core_recv = take(5)
    token_sems, branch_sems = take(3), take(3)

    ring, pair = Ring(shards), Pair()
    rep, core = pair.rep, pair.rep % 2
    depth = in_ref.shape[1]
    copies = (
        (
            in_ref.at[pl.ds(pl.multiple_of(cut.inner * rep, ROWS), cut.inner)],
            share_ref.at[pl.ds(cut.z, cut.inner)],
        ),
        (
            in_ref.at[pl.ds(pl.multiple_of(INNER + cut.inner * rep, ROWS), cut.inner)],
            share_ref.at[pl.ds(cut.x, cut.inner)],
        ),
        (
            in_ref.at[pl.ds(2 * INNER, 2 * STATE)],
            share_ref.at[pl.ds(cut.maps, 2 * STATE)],
        ),
        (in_ref.at[pl.ds(2 * INNER + 2 * STATE, HEADS)], rows_ref),
        (
            query_ref.at[:, pl.ds(pl.multiple_of(cut.qwidth * rep, LANES), cut.qwidth)],
            turn_ref.at[:, pl.ds(0, cut.qwidth)],
        ),
    ) + tuple(
        (
            ref.at[:, pl.ds(pl.multiple_of(rep * KVH // 4 * HEAD_WIDTH, LANES), HEAD_WIDTH)],
            turn_ref.at[:, pl.ds(cut.qwidth + number * HEAD_WIDTH, HEAD_WIDTH)],
        )
        for number, ref in enumerate((key_ref, value_ref))
    )
    packs = [
        pltpu.make_async_copy(src, dst, pack_sem.at[number])
        for number, (src, dst) in enumerate(copies)
    ]
    for pack in packs:
        pack.start()
    greet(ring, pair)
    branch_ref[...] = (cot_ref[...].astype(F32) * live_ref[:, 0:1]).astype(BF16)
    for pack in packs:
        pack.wait()
    share_ref[: cut.qwidth] = turn_ref[:, : cut.qwidth].T
    share_ref[cut.k :] = turn_ref[:, cut.qwidth :].T
    row = lax.broadcasted_iota(jnp.int32, (LANES, HEADS), 0)
    column = lax.broadcasted_iota(jnp.int32, (LANES, HEADS), 1)
    chosen = jnp.logical_and(column == row + cut.heads * rep, row < cut.heads)
    chosen = jnp.where(chosen, 1.0, 0.0).astype(BF16)
    share_ref[cut.step : cut.z] = dot(chosen, rows_ref[...]).astype(BF16)
    every = pl.ds(0, cut.width)
    keeps = [
        pltpu.make_async_copy(src, dst, pack_sem.at[len(packs) + number])
        for number, (src, dst) in enumerate(
            (
                (share_ref, block_at(w_ref, ring.index, every, depth)),
                (aux_ref, aux_all_ref.at[ring.index]),
            )
        )
    ]
    quarter = cut.maps // 4
    half = cut.shared // 2
    rows = lambda number: pl.ds(number * quarter, quarter)

    def shared(which, way):
        return pl.ds(pl.multiple_of(cut.maps + which * cut.shared + way * half, 16), half)

    def piece(rows):
        return share_ref.at[rows], lambda index: block_at(w_ref, index, rows, depth)

    ways = (
        [
            piece(shared(core, 0)),
            piece(rows(0)),
            piece(rows(1)),
            (aux_ref, lambda index: aux_all_ref.at[index]),
        ],
        [piece(shared(core, 1)), piece(rows(2)), piece(rows(3))],
    )

    def over_core(step, way, which):
        here = block_at(w_ref, ring.at((2 * way - 1) * step), shared(which, way), depth)
        return remote(
            here, here, core_send.at[step - 1, way], core_recv.at[step - 1, way], pair.peers[1]
        )

    def hook(step, way, piece):
        if piece == 0:
            over_core(step, way, core).start()

    gather = Gather(ring, ways, send, recv, hook)
    gather.start()
    tokens = Share(pair, 1, tokens_ref, tokens_all_ref, token_sems)
    branch = Share(pair, 1, branch_ref, branch_all_ref, branch_sems)
    tokens.start(0)
    branch.start(0)
    for keep in keeps:
        keep.start()
    gather.run(2, 4)
    tokens.pass_on(0)
    gather.advance(4)
    branch.pass_on(0)
    gather.run(5, shards)
    gather.finish()
    tokens.finish()
    branch.finish()
    for keep in keeps:
        keep.wait()

    def rest(step, carry):
        for way in range(2):
            over_core(step, way, 1 - core).wait_recv()
            over_core(step, way, core).wait_send()
        return carry

    lax.fori_loop(1, shards, rest, 0)


def share_sems(chunks):
    return [
        pltpu.SemaphoreType.DMA((3, chunks)),
        pltpu.SemaphoreType.DMA((3, chunks)),
        pltpu.SemaphoreType.DMA((chunks,)),
    ]


def gather_in_call(shards, cut, in_t, query, key, value, aux, tokens, cot, live):
    depth = in_t.shape[1]
    length, width = tokens.shape
    hbm = pl.BlockSpec(memory_space=pl.ANY)
    vmem = pl.BlockSpec(memory_space=pltpu.VMEM)
    out_shape = [
        jax.ShapeDtypeStruct((shards,) + aux.shape, BF16),
        jax.ShapeDtypeStruct((4, length, width), BF16),
    ]
    scratch = [
        pltpu.VMEM((cut.width, depth), BF16),
        pltpu.VMEM((depth, cut.qwidth + 2 * HEAD_WIDTH), BF16),
        pltpu.VMEM((HEADS, depth), BF16),
        pltpu.VMEM((length, width), BF16),
        pltpu.SemaphoreType.DMA((9,)),
        *ring_sems(shards, 4),
        pltpu.SemaphoreType.DMA((shards - 1, 2)),
        pltpu.SemaphoreType.DMA((shards - 1, 2)),
        *share_sems(1),
        *share_sems(1),
    ]
    if depth % LANES:
        w_shape = (shards, cut.width, depth)
    else:
        w_shape = (cut.width, width)
    return pl.pallas_call(
        functools.partial(gather_in, shards, cut),
        out_shape=[
            jax.ShapeDtypeStruct(w_shape, BF16),
            *out_shape,
            jax.ShapeDtypeStruct((4, length, width), BF16),
        ],
        in_specs=[hbm] * 6 + [vmem] * 2,
        out_specs=[hbm] * 4,
        scratch_shapes=scratch,
        compiler_params=pltpu.CompilerParams(
            collective_id=0, has_side_effects=True, vmem_limit_bytes=40 * MIB
        ),
        name="gather_in",
    )(in_t, query, key, value, aux, tokens, cot, live)


def gather_rows(
    shards,
    cut,
    length,
    heads_ref,
    down_ref,
    w_ref,
    tokens_ref,
    gain_ref,
    conv_ref,
    head_ref,
    chan_ref,
    cos_ref,
    sin_ref,
    heads_all_ref,
    down_all_ref,
    out_ref,
    normed_ref,
    proj_ref,
    step_ref,
    act_ref,
    pack_sem,
    send,
    recv,
):
    ring, pair = Ring(shards), Pair()
    half = down_ref.shape[0] // 2
    rows = lambda number: pl.ds(number * half, half)
    down_way = [
        (
            down_ref.at[rows(number)],
            lambda index, number=number: down_all_ref.at[index, rows(number)],
        )
        for number in range(2)
    ]
    if len(heads_all_ref.shape) == 2:
        mamba = cut.inner // shards
        attn = heads_ref.shape[0] - mamba

        def mamba_place(index):
            return heads_all_ref.at[pl.ds(pl.multiple_of(index * mamba, 16), mamba)]

        def attn_place(index):
            start = pl.multiple_of(cut.inner + index * attn, 16)
            return heads_all_ref.at[pl.ds(start, attn)]

        heads_way = [
            (heads_ref.at[pl.ds(0, mamba)], mamba_place),
            (heads_ref.at[pl.ds(mamba, attn)], attn_place),
        ]
    else:
        heads_way = [
            (
                heads_ref.at[rows(number)],
                lambda index, number=number: heads_all_ref.at[index, rows(number)],
            )
            for number in range(2)
        ]
    ways = (heads_way, down_way)
    packs = [
        pltpu.make_async_copy(own, place(ring.index), pack_sem.at[2 * way + number])
        for way in range(2)
        for number, (own, place) in enumerate(ways[way])
    ]
    for pack in packs:
        pack.start()
    greet(ring, pair)
    gather = Gather(ring, ways, send, recv)
    gather.start()
    count = proj_ref.shape[0] // length
    wide = cut.width // 7

    def norm(number, carry):
        rows = pl.ds(pl.multiple_of(number * length, length), length)
        values = tokens_ref[number].astype(F32)
        normed_ref[rows] = (values * norm_scale(values) * gain_ref[0:1]).astype(BF16)
        return carry

    def project(tile, carry):
        out = pl.ds(pl.multiple_of(tile * wide, LANES), wide)
        proj_ref[:, out] = dot_nt(normed_ref[...], w_ref[out]).astype(BF16)
        return carry

    lax.fori_loop(0, count, norm, 0)
    first = dot_nt(normed_ref[...], w_ref[:wide])
    proj_ref[:, :wide] = first.astype(BF16)
    step_ref[...] = first[:, cut.step : cut.step + LANES]
    lax.fori_loop(1, 4, project, 0)
    gather.advance(2)
    lax.fori_loop(4, 7, project, 0)
    gather.advance(3)

    def body(number, carry):
        rows = pl.ds(pl.multiple_of(number * length, length), length)
        mixer_forward(
            cut,
            proj_ref.at[rows],
            step_ref.at[rows],
            conv_ref,
            head_ref,
            chan_ref,
            cos_ref,
            sin_ref,
            out_ref.at[rows],
            act_ref,
        )
        gather.advance(number + 4)
        return carry

    lax.fori_loop(0, count, body, 0)
    gather.run(count + 4, shards)
    gather.finish()
    for pack in packs:
        pack.wait()


def gather_rows_call(
    shards, cut, length, ordered, heads, down, w, tokens, gain, conv, head, chan, cosine, sine
):
    rows = 4 * length
    tall, width = heads.shape
    hbm = pl.BlockSpec(memory_space=pl.ANY)
    vmem = pl.BlockSpec(memory_space=pltpu.VMEM)
    return pl.pallas_call(
        functools.partial(gather_rows, shards, cut, length),
        out_shape=[
            jax.ShapeDtypeStruct(
                (shards * tall, width) if ordered else (shards, tall, width), BF16
            ),
            jax.ShapeDtypeStruct((shards,) + down.shape, BF16),
            jax.ShapeDtypeStruct((rows, cut.inner + cut.qwidth), BF16),
            jax.ShapeDtypeStruct((rows, width), BF16),
            jax.ShapeDtypeStruct((rows, cut.width), BF16),
            jax.ShapeDtypeStruct((rows, LANES), F32),
        ],
        in_specs=[vmem] * 10,
        out_specs=[hbm] * 2 + [vmem] * 4,
        scratch_shapes=[
            pltpu.VMEM((length, cut.conv), F32),
            pltpu.SemaphoreType.DMA((4,)),
        ]
        + ring_sems(shards, 2),
        compiler_params=pltpu.CompilerParams(
            collective_id=1, has_side_effects=True, vmem_limit_bytes=48 * MIB
        ),
        name="gather_rows",
    )(heads, down, w, tokens, gain, conv, head, chan, cosine, sine)


class Exchange:
    def __init__(self, pair, chunks, part_ref, core_ref, cross_ref, came_ref, sems):
        self.pair, self.chunks = pair, chunks
        self.part, self.core, self.cross, self.came = part_ref, core_ref, cross_ref, came_ref
        self.send, self.recv = sems
        self.tall = part_ref.shape[1] // chunks

    def rows(self, chunk):
        return pl.ds(chunk * self.tall, self.tall)

    def over_core(self, chunk, which):
        return remote(
            self.part.at[2 + which, self.rows(chunk)],
            self.core.at[which, self.rows(chunk)],
            self.send.at[0, which, chunk],
            self.recv.at[0, which, chunk],
            self.pair.peers[1],
        )

    def over_x(self, chunk):
        return remote(
            self.cross.at[self.rows(chunk)],
            self.came.at[self.rows(chunk)],
            self.send.at[1, 0, chunk],
            self.recv.at[1, 0, chunk],
            self.pair.peers[0],
        )

    def start_one(self, which):
        for chunk in range(self.chunks):
            self.over_core(chunk, which).start()

    def start(self):
        self.start_one(1)
        self.start_one(0)

    def middle(self, chunk):
        self.over_core(chunk, 1).wait_recv()
        rows = self.rows(chunk)
        total = self.part[1, rows].astype(F32) + self.core[1, rows].astype(F32)
        self.cross[rows] = total.astype(BF16)
        self.over_x(chunk).start()

    def sum(self, chunk):
        self.over_core(chunk, 0).wait_recv()
        self.over_x(chunk).wait_recv()
        rows = self.rows(chunk)
        return (
            self.part[0, rows].astype(F32)
            + self.core[0, rows].astype(F32)
            + self.came[rows].astype(F32)
        )

    def finish(self):
        for chunk in range(self.chunks):
            for which in range(2):
                self.over_core(chunk, which).wait_send()
            self.over_x(chunk).wait_send()


class Share:
    def __init__(self, pair, chunks, own_ref, all_ref, sems):
        self.pair, self.chunks, self.own, self.all = pair, chunks, own_ref, all_ref
        self.send, self.recv, self.local = sems
        self.tall = own_ref.shape[0] // chunks

    def rows(self, chunk):
        return pl.ds(chunk * self.tall, self.tall)

    def direct(self, chunk, which):
        return remote(
            self.own.at[self.rows(chunk)],
            self.all.at[1 + which, self.rows(chunk)],
            self.send.at[which, chunk],
            self.recv.at[which, chunk],
            self.pair.peers[which],
        )

    def onward(self, chunk):
        return remote(
            self.all.at[1, self.rows(chunk)],
            self.all.at[3, self.rows(chunk)],
            self.send.at[2, chunk],
            self.recv.at[2, chunk],
            self.pair.peers[1],
        )

    def keep(self, chunk):
        return pltpu.make_async_copy(
            self.own.at[self.rows(chunk)], self.all.at[0, self.rows(chunk)], self.local.at[chunk]
        )

    def start(self, chunk):
        self.direct(chunk, 0).start()
        self.direct(chunk, 1).start()
        self.keep(chunk).start()

    def pass_on(self, chunk):
        self.direct(chunk, 0).wait_recv()
        self.onward(chunk).start()

    def finish(self):
        for chunk in range(self.chunks):
            self.direct(chunk, 0).wait_send()
            self.direct(chunk, 1).wait()
            self.onward(chunk).wait()
            self.keep(chunk).wait()


CHUNKS = 2


def exchange_scratch(length, width):
    return [
        pltpu.VMEM((2, length, width), BF16),
        pltpu.VMEM((length, width), BF16),
        pltpu.VMEM((length, width), BF16),
        pltpu.SemaphoreType.DMA((2, 2, CHUNKS)),
        pltpu.SemaphoreType.DMA((2, 2, CHUNKS)),
    ]


class Scatter:
    def __init__(
        self, ring, pieces, term, first_ref, slots_ref, send, recv, groups=1, made_ref=None
    ):
        self.made = made_ref
        self.ring, self.pieces, self.groups, self.term = ring, pieces, groups, term
        self.first, self.slots, self.send, self.recv = first_ref, slots_ref, send, recv
        self.half = slots_ref.shape[2]
        self.tall = self.half // pieces

    def each(self, group):
        size = self.pieces // self.groups
        for piece in range(group * size, (group + 1) * size):
            for way in range(2):
                yield way, piece

    def rows(self, way, piece):
        return pl.ds(way * self.half + piece * self.tall, self.tall)

    def local(self, piece):
        return pl.ds(piece * self.tall, self.tall)

    def due(self, step, way, piece):
        if self.made is not None:
            at = piece % (self.pieces // self.groups) * self.tall
            return self.made[way, at : at + self.tall]
        return self.term(self.ring.at((2 * way - 1) * step), self.rows(way, piece))

    def copy(self, step, way, piece, first=False):
        src = self.first.at[way] if first else self.slots.at[step - 2, way]
        return remote(
            src.at[self.local(piece)],
            self.slots.at[step - 1, way, self.local(piece)],
            self.send.at[step - 1, way, piece],
            self.recv.at[step - 1, way, piece],
            self.ring.peer(way),
        )

    def landed(self, step, way, piece):
        here = self.slots.at[step - 1, way, self.local(piece)]
        return remote(
            here,
            here,
            self.send.at[step - 1, way, piece],
            self.recv.at[step - 1, way, piece],
            self.ring.peer(way),
        )

    def make(self, step, group):
        if self.made is None:
            return
        tall = self.half // self.groups
        for way in range(2):
            index = self.ring.at((2 * way - 1) * step)
            self.made[way] = self.term(index, pl.ds(way * self.half + group * tall, tall))

    def start(self, group=0):
        self.make(1, group)
        for way, piece in self.each(group):
            self.first[way, self.local(piece)] = self.due(1, way, piece).astype(BF16)
            self.copy(1, way, piece, True).start()

    def total(self, step, way, piece):
        term = self.due(step, way, piece)
        self.landed(step - 1, way, piece).wait_recv()
        return self.slots[step - 2, way, self.local(piece)].astype(F32) + term

    def advance(self, step, group=0):
        self.make(step, group)
        for way, piece in self.each(group):
            total = self.total(step, way, piece)
            self.slots[step - 2, way, self.local(piece)] = total.astype(BF16)
            self.copy(step, way, piece).start()

    def run(self, first, stop, group=0):
        def body(step, carry):
            self.advance(step, group)
            return carry

        lax.fori_loop(first, stop, body, 0)

    def result(self, own_ref, share=None, group=0):
        self.make(self.ring.shards, group)
        for way, piece in self.each(group):
            total = self.total(self.ring.shards, way, piece)
            own_ref[self.rows(way, piece)] = total.astype(BF16)
            if share is not None:
                share.start(way * self.pieces + piece)

    def chunks(self, group):
        return [way * self.pieces + piece for way, piece in self.each(group)]

    def finish(self):
        for group in range(self.groups):
            for way, piece in self.each(group):
                self.copy(1, way, piece, True).wait_send()

        def body(step, carry):
            for group in range(self.groups):
                for way, piece in self.each(group):
                    self.copy(step, way, piece).wait_send()
            return carry

        lax.fori_loop(2, self.ring.shards, body, 0)


def stored(ref):
    return lambda index, rows: ref[index, rows].astype(F32)


def pieces_of(rows):
    return 2 if rows // 2 % 32 == 0 else 1


def scatter_scratch(shards, rows, width, pieces=None):
    return [
        pltpu.VMEM((2, rows // 2, width), BF16),
        pltpu.VMEM((shards - 1, 2, rows // 2, width), BF16),
    ] + ring_sems(shards, pieces or pieces_of(rows))


def share_scratch(rows, width, chunks):
    return [
        pltpu.VMEM((rows, width), BF16),
        pltpu.SemaphoreType.DMA((3, chunks)),
        pltpu.SemaphoreType.DMA((3, chunks)),
        pltpu.SemaphoreType.DMA((chunks,)),
    ]


def gather_mlp(shards, inside, count, *refs):
    refs = list(refs)
    take = lambda number: [refs.pop(0) for _ in range(number)]
    source_refs = take(count)
    heads_ref, w_out_ref, tokens_ref, live_ref, gain_ref = take(5)
    all_ref, normed_ref, mixed_ref = take(3)
    if inside:
        (sum_ref,) = take(1)
    core_ref, cross_ref, came_ref, ex_send, ex_recv = take(5)
    own_ref, sh_send, sh_recv, sh_local = take(4)
    part_ref, share_ref, pack_sem, send, recv = take(5)

    ring, pair = Ring(shards), Pair()
    depth, wide = share_ref.shape
    if count == 1:
        packs = [pltpu.make_async_copy(source_refs[0], share_ref, pack_sem.at[0])]
    else:
        units = wide // (2 * shards)
        packs = [
            pltpu.make_async_copy(
                ref.at[:, pl.ds(pl.multiple_of((shard * 4 + pair.rep) * units, LANES), units)],
                share_ref.at[:, pl.ds((which * shards + shard) * units, units)],
                pack_sem.at[which * shards + shard],
            )
            for which, ref in enumerate(source_refs)
            for shard in range(shards)
        ]
    for pack in packs:
        pack.start()
    greet(ring, pair)
    for pack in packs:
        pack.wait()
    keep = pltpu.make_async_copy(share_ref, all_ref.at[ring.index], pack_sem.at[0])
    keep.start()
    quarter = depth // 4
    rows = lambda number: pl.ds(number * quarter, quarter)
    piece = lambda number: (
        share_ref.at[rows(number)],
        lambda index: all_ref.at[index, rows(number)],
    )
    gather = Gather(ring, ([piece(0), piece(1)], [piece(2), piece(3)]), send, recv)
    exchange = Exchange(
        pair, CHUNKS, part_ref, core_ref, cross_ref, came_ref, (ex_send, ex_recv)
    )
    share = Share(pair, CHUNKS, own_ref, normed_ref, (sh_send, sh_recv, sh_local))
    length = part_ref.shape[1]

    def partial(number):
        left = heads_ref[pl.ds(number * length, length)]
        for lane in range(0, part_ref.shape[2], WIDE):
            lanes = slice(lane, lane + WIDE)
            part_ref[number, :, lanes] = dot(left, w_out_ref[:, lanes]).astype(BF16)

    def middle(chunk):
        rows = exchange.rows(chunk)
        branch = exchange.sum(chunk)
        mixed = tokens_ref[rows].astype(F32) + live_ref[rows, 0:1] * branch
        mixed_ref[rows] = mixed
        own_ref[rows] = (mixed * norm_scale(mixed) * gain_ref[0:1]).astype(BF16)
        share.start(chunk)

    def add(offsets, fresh=False):
        if not inside:
            return
        blocks = [ring.at(offset) for offset in offsets]

        def body(tile, carry):
            lanes = pl.ds(pl.multiple_of(tile * WIDE, LANES), WIDE)
            left = jnp.concatenate(
                [
                    normed_ref[
                        :, :, pl.ds(pl.multiple_of(index * depth, LANES), depth)
                    ].reshape(4 * length, depth)
                    for index in blocks
                ],
                axis=1,
            )
            right = jnp.concatenate([all_ref[index, :, lanes] for index in blocks], axis=0)
            term = dot(left, right)
            sum_ref[:, lanes] = term if fresh else sum_ref[:, lanes] + term
            return carry

        lax.fori_loop(0, wide // WIDE, body, 0)

    gather.start()
    for number in (3, 2, 1, 0):
        partial(number)
        if number > 1:
            exchange.start_one(number - 2)
    exchange.middle(0)
    exchange.middle(1)
    gather.advance(2)
    middle(0)
    gather.advance(3)
    middle(1)
    gather.advance(4)
    share.pass_on(0)
    gather.advance(5)
    share.pass_on(1)
    gather.advance(6)
    share.finish()
    keep.wait()
    half_way = shards // 2
    if half_way < 6:
        add((0, half_way), True)
    gather.run(7, shards)
    if half_way >= 6:
        add((0, half_way), True)
    if inside:

        def body(far, carry):
            add((far, -far))
            return carry

        lax.fori_loop(2, half_way, body, 0)
    gather.finish()
    add((1, -1))
    exchange.finish()


def gather_mlp_call(shards, inside, sources, wide, heads, w_out, tokens, live, gain):
    length, width = tokens.shape
    depth = sources[0].shape[0]
    hbm = pl.BlockSpec(memory_space=pl.ANY)
    vmem = pl.BlockSpec(memory_space=pltpu.VMEM)
    rows = heads.shape[0]
    return pl.pallas_call(
        functools.partial(gather_mlp, shards, inside, len(sources)),
        out_shape=[
            jax.ShapeDtypeStruct((shards, depth, wide), BF16),
            jax.ShapeDtypeStruct((4, length, width), BF16),
            jax.ShapeDtypeStruct((length, width), F32),
        ]
        + [jax.ShapeDtypeStruct((rows, wide), F32)] * inside,
        in_specs=[hbm] * len(sources) + [vmem] * 5,
        out_specs=[vmem] * (3 + inside),
        scratch_shapes=exchange_scratch(length, width)
        + share_scratch(length, width, CHUNKS)
        + [
            pltpu.VMEM((4, length, width), BF16),
            pltpu.VMEM((depth, wide), BF16),
            pltpu.SemaphoreType.DMA((2 * shards,)),
        ]
        + ring_sems(shards, 2),
        compiler_params=pltpu.CompilerParams(
            collective_id=2, has_side_effects=True, vmem_limit_bytes=56 * MIB
        ),
        name="gather_mlp",
    )(*sources, heads, w_out, tokens, live, gain)


TILE = 256
WIDE = 512


def product_tn(left_ref, right_ref, out_ref, number):
    rows = pl.ds(pl.multiple_of(number * TILE, TILE), TILE)
    left = left_ref[:, rows].T
    for lane in range(0, out_ref.shape[1], WIDE):
        lanes = slice(lane, lane + WIDE)
        out_ref[rows, lanes] = dot(left, right_ref[:, lanes]).astype(out_ref.dtype)


def product(left_ref, right_ref, out_ref, number):
    rows = pl.ds(pl.multiple_of(number * TILE, TILE), TILE)
    for lane in range(0, out_ref.shape[1], WIDE):
        lanes = slice(lane, lane + WIDE)
        out_ref[rows, lanes] = dot(left_ref[rows], right_ref[:, lanes]).astype(out_ref.dtype)


def mlp_back(gate_up_ref, branch_ref, w_down_ref, w_mlp_ref, active_ref, d_ref, part_ref):
    half = active_ref.shape[1]
    for lane in range(0, half, WIDE):
        gates, ups = slice(lane, lane + WIDE), slice(half + lane, half + lane + WIDE)
        d_active = dot_nt(branch_ref[...], w_down_ref[gates])
        gate, up = gate_up_ref[:, gates], gate_up_ref[:, ups]
        sig = sigmoid(gate)
        active = gate * sig
        active_ref[:, gates] = (active * up).astype(BF16)
        d_ref[:, gates] = (d_active * up * silu_slope(gate, sig)).astype(BF16)
        d_ref[:, ups] = (d_active * active).astype(BF16)
    for lane in range(0, part_ref.shape[1], WIDE):
        lanes = slice(lane, lane + WIDE)
        part_ref[:, lanes] = dot_nt(d_ref[...], w_mlp_ref[lanes]).astype(BF16)


def mlp_back_call(gate_up, branch, w_down, w_mlp):
    rows, wide = gate_up.shape
    half, width = w_down.shape
    tall = 2 * TILE
    tile = lambda lanes: pl.BlockSpec((tall, lanes), lambda i: (i, 0))
    whole = lambda shape: pl.BlockSpec(shape, lambda i: (0, 0))
    return pl.pallas_call(
        mlp_back,
        grid=(rows // tall,),
        out_shape=[
            jax.ShapeDtypeStruct((rows, half), BF16),
            jax.ShapeDtypeStruct((rows, wide), BF16),
            jax.ShapeDtypeStruct((rows, width), BF16),
        ],
        in_specs=[tile(wide), tile(width), whole(w_down.shape), whole(w_mlp.shape)],
        out_specs=[tile(half), tile(wide), tile(width)],
        compiler_params=pltpu.CompilerParams(vmem_limit_bytes=56 * MIB),
        name="mlp_back",
    )(gate_up, branch, w_down, w_mlp)


def scatter_down(
    shards,
    part_ref,
    branch_two_ref,
    normed_ref,
    d_mlp_ref,
    active_ref,
    w_down_ref,
    mixed_ref,
    cot_ref,
    live_ref,
    gain_ref,
    branch_ref,
    down_own_ref,
    mlp_ref,
    ffn_ref,
    d_mixed_ref,
    gain_sum_ref,
    core_ref,
    cross_ref,
    came_ref,
    ex_send,
    ex_recv,
    own_ref,
    sh_send,
    sh_recv,
    sh_local,
    first_ref,
    slots_ref,
    send,
    recv,
    down_ref,
):
    ring, pair = Ring(shards), Pair()
    greet(ring, pair)
    units = slots_ref.shape[2] * 2

    def down_term(index, rows):
        start = pl.multiple_of(index * units + rows.start, 16)
        return down_ref[pl.ds(start, rows.size)].astype(F32)

    scatter = Scatter(ring, pieces_of(units), down_term, first_ref, slots_ref, send, recv)
    exchange = Exchange(
        pair, CHUNKS, part_ref, core_ref, cross_ref, came_ref, (ex_send, ex_recv)
    )
    share = Share(pair, CHUNKS, own_ref, branch_ref, (sh_send, sh_recv, sh_local))
    gain_sum_ref[...] = jnp.zeros_like(gain_sum_ref)

    def middle(chunk):
        rows = exchange.rows(chunk)
        grad = exchange.sum(chunk)
        values = mixed_ref[rows]
        d_values, gain_sum = norm_back(values, norm_scale(values), gain_ref[0:1], grad)
        gain_sum_ref[0:1] += gain_sum
        d_mixed = cot_ref[rows].astype(F32) + d_values
        d_mixed_ref[rows] = d_mixed
        own_ref[rows] = (live_ref[rows, 0:1] * d_mixed).astype(BF16)
        share.start(chunk)

    def work(first, stop):
        def body(number, carry):
            product_tn(normed_ref, d_mlp_ref, mlp_ref, number)
            return carry

        lax.fori_loop(first, stop, body, 0)

    tiles = mlp_ref.shape[0] // TILE
    exchange.start()

    def down(number, carry):
        product_tn(active_ref, branch_two_ref, down_ref, number)
        return carry

    lax.fori_loop(0, down_ref.shape[0] // TILE, down, 0)
    scatter.start()
    exchange.middle(0)
    exchange.middle(1)
    scatter.advance(2)
    work(0, 3)
    scatter.advance(3)
    work(3, 5)
    middle(0)
    scatter.advance(4)
    work(5, 6)
    scatter.advance(5)
    middle(1)
    scatter.advance(6)
    work(6, tiles)
    scatter.run(7, shards)

    def rest(number, carry):
        product(active_ref, w_down_ref, ffn_ref, number)
        return carry

    lax.fori_loop(0, ffn_ref.shape[0] // TILE, rest, 0)
    scatter.result(down_own_ref)
    share.pass_on(0)
    share.pass_on(1)
    scatter.finish()
    exchange.finish()
    share.finish()


def scatter_down_call(
    shards, part, branch_two, normed, d_mlp, active, w_down, mixed, cot, live, gain
):
    length, width = mixed.shape
    hbm = pl.BlockSpec(memory_space=pl.ANY)
    vmem = pl.BlockSpec(memory_space=pltpu.VMEM)
    units = active.shape[1] // shards
    return pl.pallas_call(
        functools.partial(scatter_down, shards),
        out_shape=[
            jax.ShapeDtypeStruct((4, length, width), BF16),
            jax.ShapeDtypeStruct((units, width), BF16),
            jax.ShapeDtypeStruct((normed.shape[1], d_mlp.shape[1]), BF16),
            jax.ShapeDtypeStruct((4 * length, width), BF16),
            jax.ShapeDtypeStruct((length, width), F32),
            jax.ShapeDtypeStruct((8, width), F32),
        ],
        in_specs=[vmem] * 10,
        out_specs=[hbm] + [vmem] * 5,
        scratch_shapes=exchange_scratch(length, width)
        + share_scratch(length, width, CHUNKS)
        + scatter_scratch(shards, units, width)
        + [pltpu.VMEM((units * shards, width), BF16)],
        compiler_params=pltpu.CompilerParams(
            collective_id=3, has_side_effects=True, vmem_limit_bytes=60 * MIB
        ),
        name="scatter_down",
    )(part, branch_two, normed, d_mlp, active, w_down, mixed, cot, live, gain)


def scatter_mlp(
    shards,
    cut,
    length,
    mlp_ref,
    out_ref,
    proj_ref,
    step_ref,
    grad_ref,
    conv_ref,
    head_ref,
    chan_ref,
    cos_ref,
    sin_ref,
    down_ref,
    ffn_ref,
    down_all_ref,
    ffn_came_ref,
    mlp_own_ref,
    out_own_ref,
    d_ref,
    d_t_ref,
    conv_sum_ref,
    head_sum_ref,
    chan_sum_ref,
    act_ref,
    d_act_ref,
    d_pair_ref,
    col_ref,
    first_ref,
    slots_ref,
    send,
    recv,
    out_first_ref,
    out_slots_ref,
    out_send,
    out_recv,
    sh_send,
    sh_recv,
    sh_local,
    ffn_send,
    ffn_recv,
    shared_ref,
    shared_came_ref,
    add_sem,
):
    ring, pair = Ring(shards), Pair()
    greet(ring, pair, pair.corner)
    share = Share(pair, 1, down_ref, down_all_ref, (sh_send, sh_recv, sh_local))
    ffn = [
        remote(
            ffn_ref.at[1 + which],
            ffn_came_ref.at[which],
            ffn_send.at[which],
            ffn_recv.at[which],
            peer,
        )
        for which, peer in enumerate(pair.peers + (pair.corner,))
    ]
    mlp = Scatter(
        ring, pieces_of(mlp_ref.shape[1]), stored(mlp_ref), first_ref, slots_ref, send, recv
    )
    tall = out_slots_ref.shape[2] * 2
    mamba = cut.inner // shards

    def out_rows(index, rows):
        if rows.start < mamba:
            start = index * mamba + rows.start
        else:
            start = cut.inner + index * (tall - mamba) + rows.start - mamba
        return out_ref[pl.ds(pl.multiple_of(start, 16), rows.size)].astype(F32)

    out = Scatter(
        ring,
        pieces_of(tall),
        stored(out_ref) if len(out_ref.shape) == 3 else out_rows,
        out_first_ref,
        out_slots_ref,
        out_send,
        out_recv,
    )
    mlp.start()
    out.start()
    share.start(0)
    for copy in ffn:
        copy.start()
    for ref in (conv_sum_ref, head_sum_ref, chan_sum_ref):
        ref[...] = jnp.zeros_like(ref)
    count = proj_ref.shape[0] // length

    def body(number, carry):
        rows = pl.ds(pl.multiple_of(number * length, length), length)
        mixer_backward(
            cut,
            proj_ref.at[rows],
            step_ref.at[rows],
            grad_ref.at[rows],
            conv_ref,
            head_ref,
            chan_ref,
            cos_ref,
            sin_ref,
            d_ref.at[rows],
            conv_sum_ref,
            head_sum_ref,
            chan_sum_ref,
            act_ref,
            d_act_ref,
            d_pair_ref,
            col_ref,
        )
        mlp.advance(number + 2)
        out.advance(number + 2)
        half = LANES // 2
        for lane in range(0, cut.width, LANES):
            turned = d_ref[rows, lane : lane + LANES].T
            if lane >= cut.maps:
                shared_ref[lane - cut.maps : lane - cut.maps + LANES, rows] = turned
                continue
            for part in range(2):
                to = cut.ring_row(lane + part * half)
                d_t_ref[to : to + half, rows] = turned[part * half : (part + 1) * half]
        return carry

    lax.fori_loop(0, count, body, 0)
    core = pair.rep % 2
    of_core = lambda which: pl.multiple_of(which * cut.shared, 16)
    add = remote(
        shared_ref.at[pl.ds(of_core(1 - core), cut.shared)],
        shared_came_ref,
        add_sem.at[0],
        add_sem.at[1],
        pair.peers[1],
    )
    add.start()
    share.pass_on(0)
    mlp.advance(count + 2)
    out.advance(count + 2)
    add.wait()
    half = cut.shared // 2
    for way in range(2):
        rows = pl.ds(pl.multiple_of(of_core(core) + way * half, 16), half)
        to = way * cut.way + cut.maps // 2
        middle = 2 * length
        for here, there in ((0, middle), (middle, 0)):
            total = shared_ref[rows, here : here + middle].astype(F32)
            total = total + shared_came_ref[
                way * half : (way + 1) * half, there : there + middle
            ].astype(F32)
            d_t_ref[to : to + half, here : here + middle] = total.astype(BF16)

    def rest(step, carry):
        mlp.advance(step)
        out.advance(step)
        return carry

    lax.fori_loop(count + 3, shards, rest, 0)
    mlp.result(mlp_own_ref)
    out.result(out_own_ref)
    mlp.finish()
    out.finish()
    share.finish()
    for copy in ffn:
        copy.wait()


def scatter_mlp_call(
    shards, cut, length, mlp, out, proj, steps, grad, conv, head, chan, cosine, sine, down, ffn
):
    hbm = pl.BlockSpec(memory_space=pl.ANY)
    rows = proj.shape[0]
    vmem = pl.BlockSpec(memory_space=pltpu.VMEM)
    depth, wide = mlp.shape[1:]
    width = out.shape[-1]
    tall = out.size // width // shards
    return pl.pallas_call(
        functools.partial(scatter_mlp, shards, cut, length),
        out_shape=[
            jax.ShapeDtypeStruct((4,) + down.shape, BF16),
            jax.ShapeDtypeStruct((3, length, width), BF16),
            jax.ShapeDtypeStruct((depth, wide), BF16),
            jax.ShapeDtypeStruct((tall, width), BF16),
            jax.ShapeDtypeStruct((rows, cut.width), BF16),
            jax.ShapeDtypeStruct((2 * cut.way, rows), BF16),
            jax.ShapeDtypeStruct(conv.shape, F32),
            jax.ShapeDtypeStruct(head.shape, F32),
            jax.ShapeDtypeStruct(chan.shape, F32),
        ],
        in_specs=[vmem] * 11 + [hbm],
        out_specs=[hbm] * 2 + [vmem] * 7,
        scratch_shapes=[
            pltpu.VMEM((length, cut.conv), F32),
            pltpu.VMEM((length, cut.conv), F32),
            pltpu.VMEM((length, length), F32),
            pltpu.VMEM((LANES, length), F32),
        ]
        + scatter_scratch(shards, depth, wide)
        + scatter_scratch(shards, tall, width)
        + share_sems(1)
        + [pltpu.SemaphoreType.DMA((3,))] * 2
        + [
            pltpu.VMEM((2 * cut.shared, rows), BF16),
            pltpu.VMEM((cut.shared, rows), BF16),
            pltpu.SemaphoreType.DMA((2,)),
        ],
        compiler_params=pltpu.CompilerParams(
            collective_id=4, has_side_effects=True, vmem_limit_bytes=60 * MIB
        ),
        name="scatter_mlp",
    )(mlp, out, proj, steps, grad, conv, head, chan, cosine, sine, down, ffn)


GROUPS = 2
PIECES = 6


def scatter_in(shards, inside, *refs):
    refs = list(refs)
    take = lambda count: [refs.pop(0) for _ in range(count)]
    if inside:
        d_t_ref, normed_ref, d_hbm, w_hbm = take(4)
    else:
        in_ref, part_ref = take(2)
    small_ref, tokens_ref, d_mixed_ref, gain_ref, mlp_ref, out_ref = take(6)
    in_all_ref, small_all_ref, mlp_all_ref, out_all_ref, grad_ref = take(5)
    core_ref, cross_ref, came_ref, ex_send, ex_recv = take(5)
    in_scratch, small_scratch = take(4), take(4)
    own_ref, sh_send, sh_recv, sh_local = take(4)
    small_own_ref, sm_send, sm_recv, sm_local = take(4)
    mlp_sems, out_sems = take(3), take(3)
    move_ref, move_sem = take(2)
    if inside:
        d_ref, w_ref, part_ref, small_all, gain_sum_ref, load_sem, made_ref = take(7)

    ring, pair = Ring(shards), Pair()
    if inside:
        loads = [
            pltpu.make_async_copy(src, dst, load_sem.at[number])
            for number, (src, dst) in enumerate(((d_hbm, d_ref), (w_hbm, w_ref)))
        ]
        for load in loads:
            load.start()
        depth = w_ref.shape[1] // shards

        def term(index, rows):
            lanes = pl.ds(pl.multiple_of(index * depth, LANES), depth)
            return dot(d_t_ref[rows], normed_ref[:, lanes])

        small_term = stored(small_all)
    else:
        term, small_term = stored(in_ref), stored(small_ref)
    group = shards // 4
    here, rep = ring.index, pair.rep
    to = (group * rep + here // 4, here % 4)
    by = (4 * (here % group) + rep, here // group)
    far = to[0] * 4 + to[1] - here * 4 - rep
    limit = (4 * shards) ** 2
    moves = (far * far + limit - 1) // limit
    peer = {"fsdp": to[0], "rep": to[1]}
    move = remote(out_ref, move_ref, move_sem.at[0], move_sem.at[1], peer)
    stay = pltpu.make_async_copy(out_ref, move_ref, move_sem.at[2])
    greet(ring, pair, maybe=(peer, {"fsdp": by[0], "rep": by[1]}), are=moves)

    @pl.when(moves == 1)
    def _():
        move.start()

    @pl.when(moves == 0)
    def _():
        stay.start()

    pieces = PIECES
    scatter = Scatter(
        ring,
        pieces,
        term,
        *in_scratch,
        groups=GROUPS,
        made_ref=made_ref if inside else None,
    )
    small = Scatter(ring, 1, small_term, *small_scratch)
    exchange = Exchange(
        pair, CHUNKS, part_ref, core_ref, cross_ref, came_ref, (ex_send, ex_recv)
    )
    share = Share(pair, 2 * pieces, own_ref, in_all_ref, (sh_send, sh_recv, sh_local))
    small_share = Share(pair, 2, small_own_ref, small_all_ref, (sm_send, sm_recv, sm_local))
    mlp_share = Share(pair, CHUNKS, mlp_ref, mlp_all_ref, mlp_sems)
    out_share = Share(pair, 1, move_ref, out_all_ref, out_sems)

    def middle(chunk):
        rows = exchange.rows(chunk)
        grad = exchange.sum(chunk)
        values = tokens_ref[rows].astype(F32)
        d_values, _ = norm_back(values, norm_scale(values), gain_ref[0:1], grad)
        grad_ref[rows] = (d_mixed_ref[rows] + d_values).astype(BF16)

    def partial(tile):
        length = part_ref.shape[1]
        wide = part_ref.shape[2] // 4
        lanes = slice(tile * wide, (tile + 1) * wide)
        grad = dot(d_ref[...], w_ref[:, lanes])
        for number in range(4):
            rows = slice(number * length, (number + 1) * length)
            part_ref[number, :, lanes] = grad[rows].astype(BF16)
        gain_sum_ref[0:1, lanes] = jnp.sum(
            grad * normed_ref[:, lanes].astype(F32), axis=0, keepdims=True
        )

    scatter.start(0)
    for chunk in range(CHUNKS):
        mlp_share.start(chunk)
    if inside:
        gain_sum_ref[...] = jnp.zeros_like(gain_sum_ref)
        for load in loads:
            load.wait()
    for number in range(4):
        if inside:
            partial(number)
        scatter.advance(number + 2, 0)
    if inside:
        small_all[...] = small_ref[...]
        gain_sum = gain_sum_ref[0:1] / gain_ref[0:1]
        for index in range(shards):
            for row in range(depth // LANES):
                at = index * depth + row * LANES
                small_all[index, row : row + 1] = gain_sum[:, at : at + LANES].astype(BF16)
    exchange.start()
    small.start()
    scatter.advance(6, 0)
    exchange.middle(0)
    small.advance(2)
    exchange.middle(1)

    @pl.when(moves == 1)
    def _():
        move.wait()

    @pl.when(moves == 0)
    def _():
        stay.wait()

    out_share.start(0)
    scatter.run(7, shards, 0)
    small.advance(3)
    scatter.start(1)
    scatter.result(own_ref, share, 0)
    for step in range(2, 6):
        scatter.advance(step, 1)
        small.advance(step + 2)
        if step in (3, 4):
            middle(step - 3)
    small.run(8, shards)
    for chunk in range(CHUNKS):
        mlp_share.pass_on(chunk)
    scatter.advance(6, 1)
    out_share.pass_on(0)
    small.result(small_own_ref, small_share)
    for chunk in scatter.chunks(0):
        share.pass_on(chunk)
    scatter.run(7, shards, 1)
    scatter.result(own_ref, share, 1)
    for chunk in range(2):
        small_share.pass_on(chunk)
    for chunk in scatter.chunks(1):
        share.pass_on(chunk)
    scatter.finish()
    small.finish()
    exchange.finish()
    share.finish()
    small_share.finish()
    mlp_share.finish()
    out_share.finish()


def scatter_in_call(shards, depth, inside, given, small, tokens, d_mixed, gain, mlp, out):
    length, width = tokens.shape
    hbm = pl.BlockSpec(memory_space=pl.ANY)
    vmem = pl.BlockSpec(memory_space=pltpu.VMEM)
    wide = given[0].shape[0] if inside else given[0].shape[-2]
    tall, lanes = small.shape[1:]
    extra = []
    if inside:
        extra = [
            pltpu.VMEM(given[2].shape, BF16),
            pltpu.VMEM(given[3].shape, BF16),
            pltpu.VMEM((4, length, width), BF16),
            pltpu.VMEM(small.shape, BF16),
            pltpu.VMEM((8, width), F32),
            pltpu.SemaphoreType.DMA((2,)),
            pltpu.VMEM((2, wide // (2 * GROUPS), depth), F32),
        ]
    return pl.pallas_call(
        functools.partial(scatter_in, shards, inside),
        out_shape=[
            jax.ShapeDtypeStruct((4, wide, depth), BF16),
            jax.ShapeDtypeStruct((4, tall, lanes), BF16),
            jax.ShapeDtypeStruct((4,) + mlp.shape, BF16),
            jax.ShapeDtypeStruct((4,) + out.shape, BF16),
            jax.ShapeDtypeStruct((length, width), BF16),
        ],
        in_specs=([vmem] * 2 + [hbm] * 2 if inside else [vmem] * 2) + [vmem] * 6,
        out_specs=[hbm] * 4 + [vmem],
        scratch_shapes=exchange_scratch(length, width)
        + scatter_scratch(shards, wide, depth, PIECES)
        + scatter_scratch(shards, tall, lanes, 1)
        + share_scratch(wide, depth, 2 * PIECES)
        + share_scratch(tall, lanes, 2)
        + share_sems(CHUNKS)
        + share_sems(1)
        + [pltpu.VMEM(out.shape, BF16), pltpu.SemaphoreType.DMA((3,))]
        + extra,
        compiler_params=pltpu.CompilerParams(
            collective_id=5, has_side_effects=True, vmem_limit_bytes=60 * MIB
        ),
        name="scatter_in",
    )(*given, small, tokens, d_mixed, gain, mlp, out)


def columns(array, start, width):
    return lax.dynamic_slice_in_dim(array, start, width, axis=array.ndim - 1)


def norm_scale(values):
    return lax.rsqrt(jnp.mean(values * values, axis=-1, keepdims=True) + epsilon)


def norm_back(values, scale, gain, grad):
    inner = jnp.mean(gain * grad * values, axis=-1, keepdims=True)
    d_values = scale * gain * grad - values * (scale * scale * scale) * inner
    return d_values, jnp.sum(grad * values * scale, axis=0, keepdims=True)


def ring_at(position, shards):
    place = (position + 2 * shards) % shards
    back = place // (shards // 2)
    return (1 - back) * 2 * place + back * (2 * (shards - 1 - place) + 1)


def ring_place(index, shards):
    odd = index % 2
    return (1 - odd) * (index // 2) + odd * (shards - 1 - index // 2)


def after(value, *others):
    return lax.optimization_barrier((value,) + others)[0]


def rep_order(reps):
    order = [0]
    bit = reps // 2
    while bit:
        order = order + [member ^ bit for member in order]
        bit //= 2
    return order


def on_device(
    sizes,
    tokens,
    lengths,
    mixer_gain,
    in_proj,
    conv_weight,
    conv_bias,
    decay_log,
    step_bias,
    skip_gain,
    query_weight,
    key_weight,
    value_weight,
    mamba_out,
    attn_out,
    mlp_gain,
    gate_weight,
    up_weight,
    down_weight,
    cotangent,
):
    shards, reps = sizes
    cut = Cut(reps)
    rep = lax.axis_index("rep")
    fsdp = lax.axis_index("fsdp")
    place = ring_place(fsdp, shards)
    assert reps == 4
    length, width = tokens.shape
    depth = in_proj.shape[0]
    own = conv_weight.shape[1]
    channels = own * shards
    low = lambda v: v.astype(BF16)

    in_t = in_proj.T
    extra = 16
    aux = jnp.concatenate([mixer_gain, mlp_gain, conv_weight.reshape(-1), conv_bias], axis=0)
    aux_size = aux.shape[0]
    aux = jnp.pad(aux, (0, extra * 2 * LANES - aux_size)).reshape(extra, 2 * LANES)
    group = shards // reps
    pairs = [
        (g * reps + part, (reps * (g % group) + part) * reps + g // group)
        for g in range(shards)
        for part in range(reps)
    ]
    mamba_rows = mamba_out.shape[0] // reps
    attn_rows = attn_out.shape[0] // reps
    out_rows = mamba_rows + attn_rows
    share_out = jnp.concatenate(
        [
            lax.dynamic_slice_in_dim(mamba_out, mamba_rows * rep, mamba_rows, axis=0),
            lax.dynamic_slice_in_dim(attn_out, attn_rows * rep, attn_rows, axis=0),
        ],
        axis=0,
    )
    units = down_weight.shape[0] // reps
    if units % LANES:
        pick = lambda w: lax.dynamic_index_in_dim(
            w.reshape(depth, shards, reps, units), rep, axis=2, keepdims=False
        ).reshape(depth, shards * units)
        sources = (jnp.concatenate([pick(gate_weight), pick(up_weight)], axis=1),)
    else:
        sources = (gate_weight, up_weight)
    share_down = lax.dynamic_slice_in_dim(down_weight, units * rep, units, axis=0)

    live = (jnp.arange(length) < lengths[0]).astype(F32)[:, None]
    stream = tokens.astype(F32)
    live_wide = jnp.broadcast_to(live, (length, LANES))
    w_in, aux_all, branch_two, tokens_all = gather_in_call(
        shards,
        cut,
        in_t,
        query_weight,
        key_weight,
        value_weight,
        aux,
        tokens,
        cotangent,
        live_wide,
    )
    if w_in.ndim == 3:
        w_in = jnp.moveaxis(w_in, 0, 1).reshape(cut.width, width)
    branch_two = branch_two.reshape(reps * length, width)
    share_out = lax.ppermute(share_out, ("fsdp", "rep"), pairs)

    put = lax.dynamic_update_slice
    inner_rows = mamba_rows * shards
    half_ff = shards * units

    aux_all = aux_all.reshape(shards, -1)[:, :aux_size].astype(F32)
    gain_one = aux_all[:, :depth].reshape(1, width)
    gain_two = aux_all[:, depth : 2 * depth].reshape(1, width)
    conv_all = aux_all[:, 2 * depth :].reshape(shards, CONV + 1, own)
    conv_all = conv_all.transpose(1, 0, 2).reshape(CONV + 1, channels)
    conv_own = jnp.concatenate(
        [columns(conv_all, cut.inner * rep, cut.inner), conv_all[:, INNER:]], axis=1
    )
    conv_own = jnp.pad(conv_own, ((0, 7 - CONV), (0, 0)))
    of_heads = lambda v: jnp.pad(
        lax.dynamic_slice_in_dim(v, cut.heads * rep, cut.heads), (0, LANES - cut.heads)
    )
    head_own = jnp.stack([of_heads(decay_log), of_heads(step_bias)])
    head_own = jnp.pad(head_own, ((0, 6), (0, 0)))
    chan_own = lax.dynamic_slice_in_dim(skip_gain, cut.heads * rep, cut.heads)
    chan_own = jnp.pad(jnp.repeat(chan_own, HDIM)[None, :], ((0, 7), (0, 0)))
    cosine, sine = turn_tables(length)

    inside = depth % LANES == 0
    ordered = mamba_rows % 16 == 0 and attn_rows % 16 == 0
    w_out, w_down, mixed_heads, normed, proj, steps = gather_rows_call(
        shards,
        cut,
        length,
        ordered,
        share_out,
        share_down,
        w_in,
        tokens_all,
        jnp.broadcast_to(gain_one, (8, width)),
        conv_own,
        head_own,
        chan_own,
        cosine,
        sine,
    )
    if not ordered:
        w_out = jnp.concatenate(
            [
                w_out[:, :mamba_rows].reshape(-1, width),
                w_out[:, mamba_rows:].reshape(-1, width),
            ],
            axis=0,
        )
    w_down = w_down.reshape(-1, width)
    gain_rows = jnp.broadcast_to(gain_two, (8, width))
    w_mlp, normed_two, mixed, *gate_up = gather_mlp_call(
        shards, inside, sources, 2 * half_ff, mixed_heads, w_out, tokens, live_wide, gain_rows
    )
    w_mlp = w_mlp.reshape(width, -1)
    normed_two = normed_two.reshape(reps * length, width)
    gate_up = gate_up[0] if inside else dot(normed_two, w_mlp)
    activated, d_gate_up, d_two = mlp_back_call(gate_up, branch_two, w_down, w_mlp)
    d_two = d_two.reshape(reps, length, width)
    branch_one, s_down, g_mlp, ffn, d_mixed, gain_two_sum = scatter_down_call(
        shards,
        d_two,
        branch_two,
        normed_two,
        d_gate_up,
        activated,
        w_down,
        mixed,
        cotangent,
        live_wide,
        gain_rows,
    )
    g_mlp = g_mlp.reshape(shards, depth, -1)
    ffn = ffn.reshape(reps, length, width)

    branch_one = branch_one.reshape(reps * length, width)
    d_heads = dot_nt(branch_one, w_out)
    g_out = low(dot_tn(mixed_heads, branch_one))
    if not ordered:
        g_out = jnp.concatenate(
            [
                g_out[:inner_rows].reshape(shards, mamba_rows, width),
                g_out[inner_rows:].reshape(shards, attn_rows, width),
            ],
            axis=1,
        )
    downs, came, s_mlp, s_out, d_proj, d_proj_t, conv_sum, head_sum, chan_sum = scatter_mlp_call(
        shards,
        cut,
        length,
        g_mlp,
        g_out,
        proj,
        steps,
        d_heads,
        conv_own,
        head_own,
        chan_own,
        cosine,
        sine,
        s_down,
        ffn,
    )
    ffn_sum = ffn[0].astype(F32) + came.astype(F32).sum(axis=0)
    output = low(mixed + live * ffn_sum)
    if inside:
        given = (d_proj_t, normed, d_proj, w_in)
        gain_one_sum = jnp.zeros((width,), F32)
    else:
        g_in = low(dot(d_proj_t, normed))
        g_in = jnp.moveaxis(g_in.reshape(2 * cut.way, shards, depth), 1, 0)
        d_one = dot(d_proj, w_in)
        stream_all = tokens_all.reshape(reps * length, width).astype(F32)
        scale_all = norm_scale(stream_all)
        gain_one_sum = jnp.sum(d_one * stream_all * scale_all, axis=0)
        given = (g_in, low(d_one).reshape(reps, length, width))

    conv_sums = jnp.zeros((CONV + 1, channels), F32)
    conv_sums = put(conv_sums, conv_sum[: CONV + 1, : cut.inner], (0, cut.inner * rep))
    conv_sums = put(conv_sums, conv_sum[: CONV + 1, cut.inner :], (0, INNER))
    head_sums = jnp.zeros((3, HEADS), F32)
    own_sums = jnp.stack(
        [
            head_sum[0, : cut.heads],
            head_sum[1, : cut.heads],
            jnp.sum(chan_sum[0].reshape(cut.heads, HDIM), axis=1),
        ]
    )
    head_sums = put(head_sums, own_sums, (0, cut.heads * rep))
    small = jnp.concatenate(
        [
            gain_one_sum.reshape(shards, depth),
            gain_two_sum[0].reshape(shards, depth),
            conv_sums.reshape(CONV + 1, shards, own).transpose(1, 0, 2).reshape(shards, -1),
            jnp.broadcast_to(head_sums.reshape(1, -1), (shards, 3 * HEADS)),
        ],
        axis=1,
    )
    small_size = small.shape[1]
    tall = 32
    small = jnp.pad(low(small), ((0, 0), (0, tall * LANES - small_size)))
    small = small.reshape(shards, tall, LANES)
    ins, smalls, mlps, outs, grad_tokens = scatter_in_call(
        shards,
        depth,
        inside,
        given,
        small,
        tokens,
        d_mixed,
        jnp.broadcast_to(gain_one, (8, width)),
        s_mlp,
        s_out,
    )

    places = jnp.stack([rep ^ member for member in rep_order(reps)]).astype(jnp.int32)
    spread = functools.partial(spread_call, places)
    out_mamba, out_attn = spread(
        outs,
        [(mamba_rows * reps, width), (attn_rows * reps, width)],
        [
            (0, slice(0, mamba_rows), slice(0, width), mamba_rows, 0, 0),
            (1, slice(mamba_rows, out_rows), slice(0, width), attn_rows, 0, 0),
        ],
    )
    (out_down,) = spread(
        downs,
        [(units * reps, width)],
        [(0, slice(0, units), slice(0, width), units, 0, 0)],
    )
    out_gate, out_up = spread(
        mlps,
        [(depth, half_ff * reps)] * 2,
        [
            (
                which,
                slice(0, depth),
                slice(which * half_ff + shard * units, which * half_ff + (shard + 1) * units),
                0,
                units,
                shard * units * reps,
            )
            for which in range(2)
            for shard in range(shards)
        ],
    )
    out_wide, out_query, out_key, out_value = spread_in_call(cut, places, ins)
    out_proj = out_wide.T
    small = smalls.astype(F32).sum(axis=0).reshape(-1)[:small_size]
    out_gain_one = small[:depth]
    out_gain_two = small[depth : 2 * depth]
    conv_sums = small[2 * depth : 2 * depth + (CONV + 1) * own].reshape(CONV + 1, own)
    out_decay, out_step, out_skip = small[2 * depth + (CONV + 1) * own :].reshape(3, HEADS)
    return (
        output,
        grad_tokens,
        out_gain_one,
        out_proj,
        conv_sums[:CONV],
        conv_sums[CONV],
        out_decay,
        out_step,
        out_skip,
        out_query,
        out_key,
        out_value,
        out_mamba,
        out_attn,
        out_gain_two,
        out_gate,
        out_up,
        out_down,
    )


def solution(mesh):
    rows = P(("fsdp", "rep"), None)
    shard = P("fsdp", None)
    in_specs = (
        rows,
        P(("fsdp", "rep")),
        P("fsdp"),
        shard,
        P(None, "fsdp"),
        P("fsdp"),
        P(),
        P(),
        P(),
        shard,
        shard,
        shard,
        shard,
        shard,
        P("fsdp"),
        shard,
        shard,
        shard,
        rows,
    )
    out_specs = (
        rows,
        rows,
        P("fsdp"),
        shard,
        P(None, "fsdp"),
        P("fsdp"),
        P(),
        P(),
        P(),
        shard,
        shard,
        shard,
        shard,
        shard,
        P("fsdp"),
        shard,
        shard,
        shard,
    )
    sizes = (mesh.shape["fsdp"], mesh.shape["rep"])
    return jax.shard_map(
        functools.partial(on_device, sizes),
        mesh=mesh,
        in_specs=in_specs,
        out_specs=out_specs,
        check_vma=False,
    )
```
